512 devices in a mesh: tm: 4 (over x), height: 8 (over z_lo, core), chan: 16 (over z_hi, y).
Axes of the slice: x: 4, y: 4, z: 16 (z_hi: 4, z_lo: 4; z = z_hi * 4 + z_lo), core: 2. Of those that a mesh axis runs over, the one named last changes fastest.
Arguments:
- features: bfloat16 [384, 8, 32, 160], P('chan', 'tm', 'height'), may hold values from -400 to 400, as said below
- cotangent: bfloat16 [384, 8, 32, 160], P('chan', 'tm', 'height'), may hold values from -6 to 6
- conv_weight: bfloat16 [384, 27, 384], P('chan'), may hold values from -0.0625 to 0.0625
- norm_gain: float32 [384], replicated, may hold values from 0.5 to 1.5
- norm_bias: float32 [384], replicated, may hold values from -3 to 3
Outputs:
- input_grad: bfloat16 [384, 8, 32, 160], P('chan', 'tm', 'height')
- weight_grad: float32 [384, 27, 384], P('chan')
The draws below stay inside these ranges and needn't reach their ends.
Inputs may be any that keep to these rules, and one draw needn't show every extreme that they name: `features`: bounded activations.
All inputs are finite; a program needn't handle non-finite values.
Results may differ from the reference program's by a relative error of at most 0.003.
Values may be sent and summed in bfloat16 or wider, within the bound.
A program may use at most 64 MiB of HBM per device.

```python
import math
import jax
import jax.numpy as jnp
from jax import lax

C = 384
WIDTH = 160
FRAMES = 8
ROWS_ALL = 32


def draw_features(key, part):
    k_chan, k_cell, k_base = jax.random.split(key, 3)
    lift = jnp.log(3.0)
    chan_index = jnp.arange(C, dtype=jnp.float32).reshape(C, 1, 1, 1)
    chan_scale = jnp.exp(jax.random.uniform(k_chan, (C, 1, 1, 1), jnp.float32, -1.2, 1.2) + lift * chan_index / C)
    row_index = jnp.arange(ROWS_ALL, dtype=jnp.float32).reshape(1, 1, ROWS_ALL, 1)
    cell_scale = jnp.exp(jax.random.uniform(k_cell, (1, FRAMES, ROWS_ALL, WIDTH), jnp.float32, -1.2, 1.2) + lift * row_index / ROWS_ALL)
    shape = (C, FRAMES, ROWS_ALL, WIDTH)
    base = jax.random.truncated_normal(k_base, -4.0, 4.0, shape, jnp.float32)
    return (base * chan_scale * cell_scale).astype(jnp.bfloat16)


def steps_of(own_key, dims, cuts, low, largest):
    gain, own = 1.0, jax.random.fold_in(own_key, 6)
    for axis_at, shards_of in cuts:
        draws = jnp.exp(jax.random.uniform(jax.random.fold_in(own, axis_at), (shards_of,), jnp.float32, low / len(cuts), largest / len(cuts)))
        gain = gain * jnp.repeat(draws, dims[axis_at] // shards_of).reshape([-1 if axis == axis_at else 1 for axis in range(len(dims))])
    return gain


def bell_draw(own_key, extent, width, most, shards=(), kind=jnp.bfloat16):
    values = width * jax.random.normal(own_key, extent, jnp.float32)
    if shards:
        values = values * steps_of(own_key, extent, shards, -0.22, 0.18)
    return jnp.clip(values, -most, most).astype(kind)


def setup_inputs(seed: int = 0) -> dict:
    seeds = jax.random.split(jax.random.key(seed), 6)
    return {
        "features": draw_features(jax.random.fold_in(seeds[5], 71), 0),
        "cotangent": bell_draw(seeds[1], (C, FRAMES, ROWS_ALL, WIDTH), 1.0, 6.0, ((0, 16), (1, 4), (2, 8))),
        "conv_weight": bell_draw(seeds[2], (C, 27, C), (27 * C) ** -0.5, 0.0625, ((0, 16),)),
        "norm_gain": jnp.clip(1.0 + 0.1 * jax.random.normal(seeds[3], (C,), jnp.float32), 0.5, 1.5),
        "norm_bias": bell_draw(seeds[4], (C,), 0.5, 3.0, (), jnp.float32),
    }


def reference(features, cotangent, conv_weight, norm_gain, norm_bias):
    total = features.shape[0]
    flat_x = features.reshape(total, -1).astype(jnp.float32)
    inv_rms = lax.rsqrt(lax.optimization_barrier(jnp.mean(flat_x * flat_x, axis=0, keepdims=True)) + 1e-06)
    normed = flat_x * inv_rms * norm_gain[:, None] + norm_bias[:, None]
    active = jax.nn.silu(normed).astype(jnp.bfloat16)
    frames, rows, cols = (features.shape[1], features.shape[2], features.shape[3])
    padded = jnp.pad(cotangent, ((0, 0), (0, 2), (1, 1), (1, 1)))
    act_grad = jnp.zeros(flat_x.shape, jnp.float32)
    pieces = []
    for kt in range(3):
        for kh in range(3):
            for kw in range(3):
                tapped = padded[:, 2 - kt:2 - kt + frames, 2 - kh:2 - kh + rows, 2 - kw:2 - kw + cols].reshape(total, -1)
                weight_tap = conv_weight[:, 9 * kt + 3 * kh + kw, :]
                act_grad = act_grad + lax.dot_general(weight_tap, tapped, (((0,), (0,)), ((), ())), preferred_element_type=jnp.float32)
                pieces.append(lax.dot_general(tapped, active, (((1,), (1,)), ((), ())), preferred_element_type=jnp.float32))
    weight_grad = jnp.stack(pieces, axis=1) / math.sqrt(flat_x.shape[1])
    sig = jax.nn.sigmoid(normed)
    upstream = act_grad * (sig * (1.0 + normed * (1.0 - sig))) * norm_gain[:, None]
    dots = lax.optimization_barrier(jnp.sum(upstream * flat_x, axis=0, keepdims=True))
    back = inv_rms * upstream - flat_x * inv_rms ** 3 * dots / total
    result = cotangent.reshape(total, -1).astype(jnp.float32) + back
    return (result.astype(jnp.bfloat16).reshape(features.shape), weight_grad)
```

```python
import functools
import math

import jax
import jax.numpy as jnp
from jax import lax
from jax.experimental import pallas as pl
from jax.experimental.pallas import tpu as pltpu
from jax.sharding import PartitionSpec as P

MESH = pl.DeviceIdType.MESH
SIZES = {"x": 4, "zl": 4, "k": 2, "zh": 4, "y": 4}
CH = 24
TOTAL = 384
LANES = 640
COL = 656
GROWS = 2048
F32 = jnp.float32
BF16 = jnp.bfloat16


def coords():
    t = lax.axis_index("tm")
    h = lax.axis_index("height")
    c = lax.axis_index("chan")
    return {"x": t, "zl": h // 2, "k": h % 2, "zh": c // 4, "y": c % 4}


def shifted(at, **offsets):
    at = dict(at)
    for name, by in offsets.items():
        at[name] = (at[name] + (by % SIZES[name])) % SIZES[name]
    return {"tm": at["x"], "height": at["zl"] * 2 + at["k"], "chan": at["zh"] * 4 + at["y"]}


def neighbour(at, dx, dh):
    t = (at["x"] + (dx % 4)) % 4
    h = (at["zl"] * 2 + at["k"] + (dh % 8)) % 8
    return {"tm": t, "height": h, "chan": at["zh"] * 4 + at["y"]}


HALO = ((-1, 0), (0, 1), (0, -1), (-1, 1), (-1, -1))


def kernel(
    f_ref, d_ref, w_ref, gb_ref, og_ref, od_ref,
    dn, edges, fall, s9, p, pb, ry, q, qb, rz, act, sumsq, inv, dacc, dsend, dmid, dry, drz,
    g, gr, h, hb, hr, zs, zr, ag, ssem, rsem,
):
    at = coords()
    chan = at["zh"] * 4 + at["y"]
    count = [0]

    def send(src, dst, target):
        i = count[0]
        count[0] += 1
        copy = pltpu.make_async_remote_copy(
            src_ref=src, dst_ref=dst, send_sem=ssem.at[i], recv_sem=rsem.at[i],
            device_id=target, device_id_type=MESH,
        )
        copy.start()
        return copy

    barrier = pltpu.get_barrier_semaphore()
    greeted = [neighbour(at, -dx, -dh) for dx, dh in HALO]
    for name in ("x", "zl", "zh", "y"):
        greeted += [shifted(at, **{name: -by}) for by in (1, 2, 3)]
    greeted.append(shifted(at, k=1))
    for one in greeted:
        pl.semaphore_signal(barrier, inc=1, device_id=one, device_id_type=MESH)
    pl.semaphore_wait(barrier, len(greeted))

    started = []
    halo = []
    for n, (dx, dh) in enumerate(HALO):
        if n == 0:
            src, dst = d_ref, dn
        else:
            src = d_ref.at[:, pl.ds(384 if dh == 1 else 0, 256)]
            dst = edges.at[n - 1]
        halo.append(send(src, dst, neighbour(at, dx, dh)))
    fz = {by: send(f_ref, fall.at[chan], shifted(at, zh=by)) for by in (1, 3, 2)}
    fy = []

    def forward(src, block):
        for by in (1, 3, 2):
            fy.append(send(src, fall.at[block], shifted(at, y=by)))

    forward(f_ref, chan)
    fall[chan] = f_ref[...]

    for copy in halo:
        copy.wait_recv()
    lane = lax.broadcasted_iota(jnp.int32, (CH, LANES), 1) % 160
    first, last = lane == 0, lane == 159
    row = at["zl"] * 2 + at["k"]
    top_on = jnp.where(row > 0, 1.0, 0.0).astype(F32)
    bottom_on = jnp.where(row < 7, 1.0, 0.0).astype(F32)
    next_on = jnp.where(at["x"] < 3, 1.0, 0.0).astype(F32)
    for tp in range(4):
        rows = slice(CH * (tp % 2), CH * (tp % 2) + CH)
        late = tp >= 2
        own = (dn if late else d_ref)[...].astype(F32)[rows]
        top = edges[2 if late else 0].astype(F32)[rows] * top_on
        bottom = edges[3 if late else 1].astype(F32)[rows] * bottom_on
        if late:
            own, top, bottom = own * next_on, top * next_on, bottom * next_on
        moved = (
            jnp.concatenate([own[:, 160:], bottom[:, :160]], axis=1),
            own,
            jnp.concatenate([top[:, 96:], own[:, :480]], axis=1),
        )
        pieces = []
        for one in moved:
            pieces.append(jnp.where(last, 0.0, pltpu.roll(one, LANES - 1, 1)))
            pieces.append(one)
            pieces.append(jnp.where(first, 0.0, pltpu.roll(one, 1, 1)))
        s9[tp] = jnp.concatenate(pieces, axis=0).astype(BF16)

    for t in range(2):
        total = None
        for kt in range(3):
            part = jnp.dot(w_ref[kt], s9[t + 2 - kt], preferred_element_type=F32)
            total = part if total is None else total + part
        p[t] = total

    def parts(zh, y):
        start = pl.multiple_of((zh * 4 + y) * CH, 8)
        return jnp.concatenate([p[0, pl.ds(start, CH)], p[1, pl.ds(start, CH)]], axis=0)

    for by in (1, 3):
        fz[by].wait_recv()
        block = (at["zh"] + (4 - by)) % 4 * 4 + at["y"]
        forward(fall.at[block], block)
    ys = []
    for by in (1, 3, 2):
        for zh in range(4):
            pb[by - 1, zh] = parts(zh, (at["y"] + by) % 4).astype(BF16)
        ys.append(send(pb.at[by - 1], ry.at[by - 1], shifted(at, y=by)))
    fz[2].wait_recv()
    block = (at["zh"] + 2) % 4 * 4 + at["y"]
    forward(fall.at[block], block)

    for copy in ys:
        copy.wait_recv()
    zsends = []
    for by in (2, 1, 3, 0):
        zh = (at["zh"] + by) % 4
        value = parts(zh, at["y"])
        for n in range(3):
            value = value + ry[n, zh].astype(F32)
        if by == 0:
            q[...] = value
        else:
            qb[by - 1] = value.astype(BF16)
            zsends.append(send(qb.at[by - 1], rz.at[by - 1], shifted(at, zh=by)))

    for copy in fy:
        copy.wait_recv()
    sumsq[...] = jnp.zeros_like(sumsq)

    @pl.loop(0, 16)
    def _(n):
        value = fall[n].astype(F32)
        sumsq[...] += value * value

    for t in range(2):
        mean = jnp.sum(sumsq[CH * t : CH * t + CH], axis=0, keepdims=True) * (1.0 / TOTAL)
        inv[t : t + 1] = lax.rsqrt(mean + 1e-06)
    dacc[...] = jnp.zeros_like(dacc)

    def activation(x, t, block):
        start = pl.multiple_of(block * CH, 8)
        gain = gb_ref[pl.ds(start, CH), 0:1]
        bias = gb_ref[pl.ds(start, CH), 1:2]
        normed = x * inv[t : t + 1] * gain + bias
        sig = 1.0 / (1.0 + jnp.exp(-normed))
        return normed * sig, sig * (1.0 + normed * (1.0 - sig)) * gain

    @pl.loop(0, 8)
    def _(n):
        even = fall[2 * n].astype(F32)
        odd = fall[2 * n + 1].astype(F32)
        for t in range(2):
            both = []
            for j, block in enumerate((even, odd)):
                x = block[CH * t : CH * t + CH]
                active, slope = activation(x, t, 2 * n + j)
                both.append(active)
                start = pl.multiple_of((2 * n + j) * CH, 8)
                dacc[CH * t : CH * t + CH] += p[t, pl.ds(start, CH)] * slope * x
            act[t, pl.ds(pl.multiple_of(n * 48, 16), 48)] = jnp.concatenate(both, axis=0).astype(BF16)

    for t in range(2):
        dsend[t : t + 1] = jnp.sum(dacc[CH * t : CH * t + CH], axis=0, keepdims=True)
    dys = [send(dsend, dry.at[by - 1], shifted(at, y=by)) for by in (1, 3, 2)]

    for n in range(3):
        g[COL * n + 648 : COL * n + COL] = jnp.zeros((8, 128), F32)
    g[3 * COL : GROWS] = jnp.zeros((GROWS - 3 * COL, 128), F32)
    for kt in range(3):
        total = None
        for t in range(2):
            part = lax.dot_general(
                s9[t + 2 - kt], act[t], (((1,), (1,)), ((), ())), preferred_element_type=F32
            )
            total = part if total is None else total + part
        for n in range(3):
            g[COL * n + 216 * kt : COL * n + 216 * kt + 216] = total[:, 128 * n : 128 * n + 128]
    other = pl.multiple_of((1 - at["k"]) * 1024, 1024)
    mine = pl.multiple_of(at["k"] * 1024, 1024)
    core = send(g.at[pl.ds(other, 1024)], gr, shifted(at, k=1))

    for copy in dys:
        copy.wait_recv()
    dmid[...] = dsend[...] + dry[0] + dry[1] + dry[2]
    dzs = [send(dmid, drz.at[by - 1], shifted(at, zh=by)) for by in (2, 1, 3)]

    core.wait_recv()
    xs = []
    for by in (2, 1, 3, 0):
        start = (at["x"] + by) % 4 * 256
        value = g[pl.ds(pl.multiple_of(mine + start, 256), 256)] + gr[pl.ds(pl.multiple_of(start, 256), 256)]
        if by == 0:
            h[...] = value
        else:
            hb[by - 1] = value.astype(BF16)
            xs.append(send(hb.at[by - 1], hr.at[by - 1], shifted(at, x=by)))
    for copy in xs:
        copy.wait_recv()
    h[...] = h[...] + hr[0].astype(F32) + hr[1].astype(F32) + hr[2].astype(F32)
    zls = []
    for by in (3, 1, 2):
        start = pl.multiple_of((at["zl"] + by) % 4 * 64, 64)
        zs[by - 1] = h[pl.ds(start, 64)]
        zls.append(send(zs.at[by - 1], zr.at[by - 1], shifted(at, zl=by)))
    for copy in zls:
        copy.wait_recv()
    value = h[pl.ds(pl.multiple_of(at["zl"] * 64, 64), 64)] + zr[0] + zr[1] + zr[2]
    base = pl.multiple_of(mine + at["x"] * 256, 256)
    piece = pl.multiple_of(base + at["zl"] * 64, 64)
    ag[pl.ds(piece, 64)] = (value * (1.0 / math.sqrt(40960))).astype(BF16)
    agz = [send(ag.at[pl.ds(piece, 64)], ag.at[pl.ds(piece, 64)], shifted(at, zl=by)) for by in (3, 1, 2)]

    for copy in zsends + dzs:
        copy.wait_recv()
    grad = q[...] + rz[0].astype(F32) + rz[1].astype(F32) + rz[2].astype(F32)
    dots = dmid[...] + drz[0] + drz[1] + drz[2]
    mine_x = f_ref[...].astype(F32)
    ct = d_ref[...].astype(F32)
    outs = []
    for t in range(2):
        rows = slice(CH * t, CH * t + CH)
        x = mine_x[rows]
        _, slope = activation(x, t, chan)
        up = grad[rows] * slope
        r = inv[t : t + 1]
        back = r * up - x * (r * r * r * dots[t : t + 1] * (1.0 / TOTAL))
        outs.append(ct[rows] + back)
    od_ref[...] = jnp.concatenate(outs, axis=0).astype(BF16)

    for copy in agz:
        copy.wait_recv()
    agx = [send(ag.at[pl.ds(base, 256)], ag.at[pl.ds(base, 256)], shifted(at, x=by)) for by in (2, 1, 3)]
    for copy in agx:
        copy.wait_recv()
    last_copy = send(ag.at[pl.ds(mine, 1024)], ag.at[pl.ds(mine, 1024)], shifted(at, k=1))
    last_copy.wait_recv()
    og_ref[...] = ag[...]
    for copy in halo + list(fz.values()) + fy + ys + zsends + dys + [core] + dzs + xs + zls + agz + agx + [last_copy]:
        copy.wait_send()


COPIES = 5 + 3 + 12 + 3 + 3 + 6 + 1 + 3 + 3 + 3 + 3 + 1


def on_device(features, cotangent, conv_weight, norm_gain, norm_bias):
    chans, frames, rows, cols = features.shape
    f = jnp.transpose(features, (1, 0, 2, 3)).reshape(frames * chans, rows * cols)
    d = jnp.transpose(cotangent, (1, 0, 2, 3)).reshape(frames * chans, rows * cols)
    w = jnp.transpose(conv_weight.reshape(chans, 3, 9, TOTAL), (1, 3, 2, 0)).reshape(3, TOTAL, 9 * chans)
    gb = jnp.stack([norm_gain, norm_bias], axis=1)
    vmem = pl.BlockSpec(memory_space=pltpu.VMEM)
    grads, out = pl.pallas_call(
        kernel,
        name="unit_backward",
        out_shape=(
            jax.ShapeDtypeStruct((GROWS, 128), BF16),
            jax.ShapeDtypeStruct((48, LANES), BF16),
        ),
        in_specs=[vmem] * 4,
        out_specs=(vmem, vmem),
        scratch_shapes=[
            pltpu.VMEM((48, LANES), BF16),
            pltpu.VMEM((4, 48, 256), BF16),
            pltpu.VMEM((16, 48, LANES), BF16),
            pltpu.VMEM((4, 216, LANES), BF16),
            pltpu.VMEM((2, TOTAL, LANES), F32),
            pltpu.VMEM((3, 4, 48, LANES), BF16),
            pltpu.VMEM((3, 4, 48, LANES), BF16),
            pltpu.VMEM((48, LANES), F32),
            pltpu.VMEM((3, 48, LANES), BF16),
            pltpu.VMEM((3, 48, LANES), BF16),
            pltpu.VMEM((2, TOTAL, LANES), BF16),
            pltpu.VMEM((48, LANES), F32),
            pltpu.VMEM((2, LANES), F32),
            pltpu.VMEM((48, LANES), F32),
            pltpu.VMEM((2, LANES), F32),
            pltpu.VMEM((2, LANES), F32),
            pltpu.VMEM((3, 2, LANES), F32),
            pltpu.VMEM((3, 2, LANES), F32),
            pltpu.VMEM((GROWS, 128), F32),
            pltpu.VMEM((1024, 128), F32),
            pltpu.VMEM((256, 128), F32),
            pltpu.VMEM((3, 256, 128), BF16),
            pltpu.VMEM((3, 256, 128), BF16),
            pltpu.VMEM((3, 64, 128), F32),
            pltpu.VMEM((3, 64, 128), F32),
            pltpu.VMEM((GROWS, 128), BF16),
            pltpu.SemaphoreType.DMA((COPIES,)),
            pltpu.SemaphoreType.DMA((COPIES,)),
        ],
        compiler_params=pltpu.CompilerParams(
            collective_id=0, has_side_effects=True, vmem_limit_bytes=40 << 20
        ),
    )(f, d, w, gb)
    result = jnp.transpose(out.reshape(frames, chans, rows, cols), (1, 0, 2, 3))
    flat = jnp.concatenate([grads[COL * n : COL * n + 648] for n in range(3)], axis=1)
    weight_grad = jnp.transpose(flat.reshape(27, chans, TOTAL), (1, 0, 2)).astype(F32)
    return result, weight_grad


def solution(mesh):
    return jax.shard_map(
        on_device,
        mesh=mesh,
        in_specs=(
            P("chan", "tm", "height", None),
            P("chan", "tm", "height", None),
            P("chan", None, None),
            P(),
            P(),
        ),
        out_specs=(P("chan", "tm", "height", None), P("chan", None, None)),
        check_vma=False,
    )
```

```python
import functools
import math

import jax
import jax.numpy as jnp
from jax import lax
from jax.experimental import pallas as pl
from jax.experimental.pallas import tpu as pltpu
from jax.sharding import PartitionSpec as P

MESH = pl.DeviceIdType.MESH
SIZES = {"x": 4, "zl": 4, "k": 2, "zh": 4, "y": 4}
CH = 24
TOTAL = 384
LANES = 640
F32 = jnp.float32
BF16 = jnp.bfloat16


def coords():
    t = lax.axis_index("tm")
    h = lax.axis_index("height")
    c = lax.axis_index("chan")
    return {"x": t, "zl": h // 2, "k": h % 2, "zh": c // 4, "y": c % 4}


def shifted(at, **offsets):
    at = dict(at)
    for name, by in offsets.items():
        at[name] = (at[name] + (by % SIZES[name])) % SIZES[name]
    return {"tm": at["x"], "height": at["zl"] * 2 + at["k"], "chan": at["zh"] * 4 + at["y"]}


def neighbour(at, dx, dh):
    t = (at["x"] + (dx % 4)) % 4
    h = (at["zl"] * 2 + at["k"] + (dh % 8)) % 8
    return {"tm": t, "height": h, "chan": at["zh"] * 4 + at["y"]}


HALO = ((-1, 0), (0, 1), (0, -1), (-1, 1), (-1, -1))
FIRST, FAR = 3 * 512, 512
COPIES = 80


def kernel(
    f_ref, d_ref, w_ref, gb_ref, og_ref, od_ref,
    dn, edges, fall, s9, p, pb, ry, q, qb, rz, actx, acty, inv, dacc,
    sown, smid, sry, srz, dsend, dmid, dry, drz, gc, first_bufs, far_bufs, ssem, rsem,
):
    at = coords()
    chan = at["zh"] * 4 + at["y"]
    count = [0]
    started = []

    def send(src, dst, target):
        i = count[0]
        count[0] += 1
        copy = pltpu.make_async_remote_copy(
            src_ref=src, dst_ref=dst, send_sem=ssem.at[i], recv_sem=rsem.at[i],
            device_id=target, device_id_type=MESH,
        )
        copy.start()
        started.append(copy)
        return copy

    def arrived(copies):
        for copy in copies:
            copy.wait_recv()

    barrier = pltpu.get_barrier_semaphore()
    greeted = [shifted(at, zh=1), shifted(at, zh=3)]
    greeted += [neighbour(at, -dx, -dh) for dx, dh in HALO]
    for name in ("y", "x", "zl"):
        greeted += [shifted(at, **{name: by}) for by in (1, 2, 3)]
    greeted.append(shifted(at, k=1))
    for one in greeted:
        pl.semaphore_signal(barrier, inc=1, device_id=one, device_id_type=MESH)

    fall[chan] = f_ref[...]
    squares = f_ref[...].astype(F32)
    squares = squares * squares
    for t in range(2):
        sown[t : t + 1] = jnp.sum(squares[CH * t : CH * t + CH], axis=0, keepdims=True)
    pl.semaphore_wait(barrier, len(greeted))

    fz = [send(f_ref, fall.at[chan], shifted(at, zh=by)) for by in (1, 3)]
    halo = []
    for n, (dx, dh) in enumerate(HALO):
        if n == 0:
            src, dst = d_ref, dn
        else:
            src = d_ref.at[:, pl.ds(384 if dh == 1 else 0, 256)]
            dst = edges.at[n - 1]
        halo.append(send(src, dst, neighbour(at, dx, dh)))
    sys = [send(sown, sry.at[by - 1], shifted(at, y=by)) for by in (2, 1, 3)]

    def forward(src, block):
        return [send(src, fall.at[block], shifted(at, y=by)) for by in (2, 1, 3)]

    fy_own = forward(f_ref, chan)

    arrived(halo)
    lane = lax.broadcasted_iota(jnp.int32, (CH, LANES), 1) % 160
    left_end, right_end = lane == 0, lane == 159
    row = at["zl"] * 2 + at["k"]
    top_on = jnp.where(row > 0, 1.0, 0.0).astype(F32)
    bottom_on = jnp.where(row < 7, 1.0, 0.0).astype(F32)
    next_on = jnp.where(at["x"] < 3, 1.0, 0.0).astype(F32)
    for tp in range(4):
        rows = slice(CH * (tp % 2), CH * (tp % 2) + CH)
        late = tp >= 2
        own = (dn if late else d_ref)[...].astype(F32)[rows]
        top = edges[2 if late else 0].astype(F32)[rows] * top_on
        bottom = edges[3 if late else 1].astype(F32)[rows] * bottom_on
        if late:
            own, top, bottom = own * next_on, top * next_on, bottom * next_on
        moved = (
            jnp.concatenate([own[:, 160:], bottom[:, :160]], axis=1),
            own,
            jnp.concatenate([top[:, 96:], own[:, :480]], axis=1),
        )
        pieces = []
        for one in moved:
            pieces.append(jnp.where(right_end, 0.0, pltpu.roll(one, LANES - 1, 1)))
            pieces.append(one)
            pieces.append(jnp.where(left_end, 0.0, pltpu.roll(one, 1, 1)))
        s9[tp] = jnp.concatenate(pieces, axis=0).astype(BF16)

    arrived(sys)
    smid[0] = sown[...] + sry[0] + sry[1] + sry[2]
    szs = [send(smid.at[0], smid.at[by], shifted(at, zh=by)) for by in (1, 3)]

    for t in range(2):
        total = None
        for kt in range(3):
            part = jnp.dot(w_ref[kt], s9[t + 2 - kt], preferred_element_type=F32)
            total = part if total is None else total + part
        p[t] = total

    def parts(zh, y):
        start = pl.multiple_of((zh * 4 + y) * CH, 8)
        return jnp.concatenate([p[0, pl.ds(start, CH)], p[1, pl.ds(start, CH)]], axis=0)

    ys = []
    for by in (2, 1, 3):
        for zh in range(4):
            pb[by - 1, zh] = parts(zh, (at["y"] + by) % 4).astype(BF16)
        ys.append(send(pb.at[by - 1], ry.at[by - 1], shifted(at, y=by)))

    def block_at(by):
        return (at["zh"] + by) % 4 * 4 + at["y"]

    side = 1 + 2 * at["k"]
    arrived(fz)
    source = (at["zh"] + side) % 4 * 4 + at["y"]
    away = {"tm": at["x"], "height": row, "chan": (at["zh"] + 4 - side) % 4 * 4 + at["y"]}
    fz_far = send(fall.at[source], fall.at[source], away)
    fy_near = forward(fall.at[block_at(3)], block_at(3)) + forward(fall.at[block_at(1)], block_at(1))

    arrived(szs)
    szf = send(smid.at[1], srz, shifted(at, zh=1))
    arrived([szf])
    total = smid[0] + smid[1] + smid[3] + srz[...]
    inv[...] = lax.rsqrt(total * (1.0 / TOTAL) + 1e-06)
    dacc[...] = jnp.zeros_like(dacc)

    def activation(x, t, block):
        start = pl.multiple_of(block * CH, 8)
        gain = gb_ref[pl.ds(start, CH), 0:1]
        bias = gb_ref[pl.ds(start, CH), 1:2]
        normed = x * inv[t : t + 1] * gain + bias
        sig = 1.0 / (1.0 + jnp.exp(-normed))
        return normed * sig, sig * (1.0 + normed * (1.0 - sig)) * gain

    def activate(by, dst, base):
        zh = (at["zh"] + by) % 4

        @pl.loop(0, 2)
        def _(n):
            blocks = [fall[zh * 4 + 2 * n + j].astype(F32) for j in range(2)]
            for t in range(2):
                both = []
                for j in range(2):
                    x = blocks[j][CH * t : CH * t + CH]
                    active, slope = activation(x, t, zh * 4 + 2 * n + j)
                    both.append(active)
                    start = pl.multiple_of((zh * 4 + 2 * n + j) * CH, 8)
                    dacc[CH * t : CH * t + CH] += p[t, pl.ds(start, CH)] * slope * x
                dst[t, pl.ds(pl.multiple_of(base + n * 48, 16), 48)] = jnp.concatenate(both, axis=0).astype(BF16)

    def weigh(act, base, g, at_row):
        for kt in range(3):
            total = None
            for t in range(2):
                part = lax.dot_general(
                    s9[t + 2 - kt], act[t, base : base + 96], (((1,), (1,)), ((), ())), preferred_element_type=F32
                )
                total = part if total is None else total + part
            gc[216 * kt : 216 * kt + 216] = total
        g[at_row : at_row + 328] = jnp.concatenate([gc[0:328, 0:64], gc[320:648, 0:64]], axis=1)
        g[at_row + 328 : at_row + 496] = jnp.concatenate(
            [gc[160 * n : 160 * n + 168, 64:96] for n in range(4)], axis=1
        )

    first_g, far_g = first_bufs[0], far_bufs[0]
    first_g[1488:FIRST] = jnp.zeros((FIRST - 1488, 128), F32)
    far_g[496:FAR] = jnp.zeros((FAR - 496, 128), F32)

    arrived(fy_own)
    activate(0, actx, 0)
    weigh(actx, 0, first_g, 0)
    arrived([fz_far])
    fy_far = forward(fall.at[block_at(2)], block_at(2))

    arrived(ys)
    zsends = []
    for by in (2, 1, 3, 0):
        zh = (at["zh"] + by) % 4
        value = parts(zh, at["y"])
        for n in range(3):
            value = value + ry[n, zh].astype(F32)
        if by == 0:
            q[...] = value
        else:
            qb[by - 1] = value.astype(BF16)
            zsends.append(send(qb.at[by - 1], rz.at[by - 1], shifted(at, zh=by)))

    def core_reduce(bufs, size):
        g, gr = bufs[0], bufs[1]
        other = pl.multiple_of((1 - at["k"]) * (size // 2), size // 2)
        return send(g.at[pl.ds(other, size // 2)], gr, shifted(at, k=1))

    def x_reduce(bufs, size):
        g, gr, h, hb, hr = bufs[:5]
        quarter = size // 8
        sends = []
        for by in (2, 1, 3, 0):
            start = (at["x"] + by) % 4 * quarter
            value = (
                g[pl.ds(pl.multiple_of(at["k"] * (size // 2) + start, quarter), quarter)]
                + gr[pl.ds(pl.multiple_of(start, quarter), quarter)]
            )
            if by == 0:
                h[...] = value
            else:
                hb[by - 1] = value.astype(BF16)
                sends.append(send(hb.at[by - 1], hr.at[by - 1], shifted(at, x=by)))
        return sends

    def z_reduce(bufs, size):
        h, hr, zs, zr = bufs[2], bufs[4], bufs[5], bufs[6]
        part = size // 32
        h[...] = h[...] + hr[0].astype(F32) + hr[1].astype(F32) + hr[2].astype(F32)
        sends = []
        for by in (3, 1, 2):
            start = pl.multiple_of((at["zl"] + by) % 4 * part, part)
            zs[by - 1] = h[pl.ds(start, part)]
            sends.append(send(zs.at[by - 1], zr.at[by - 1], shifted(at, zl=by)))
        return sends

    def z_gather(bufs, size):
        h, zr, ag = bufs[2], bufs[6], bufs[7]
        part = size // 32
        value = h[pl.ds(pl.multiple_of(at["zl"] * part, part), part)] + zr[0] + zr[1] + zr[2]
        piece = pl.multiple_of(at["k"] * (size // 2) + at["x"] * (size // 8) + at["zl"] * part, part)
        ag[pl.ds(piece, part)] = (value * (1.0 / math.sqrt(40960))).astype(BF16)
        ref = ag.at[pl.ds(piece, part)]
        return [send(ref, ref, shifted(at, zl=by)) for by in (3, 1, 2)]

    def x_gather(bufs, size):
        start = pl.multiple_of(at["k"] * (size // 2) + at["x"] * (size // 8), size // 8)
        ref = bufs[7].at[pl.ds(start, size // 8)]
        return [send(ref, ref, shifted(at, x=by)) for by in (2, 1, 3)]

    def core_gather(bufs, size):
        ref = bufs[7].at[pl.ds(pl.multiple_of(at["k"] * (size // 2), size // 2), size // 2)]
        return send(ref, ref, shifted(at, k=1))

    def deliver(bufs, n, by):
        value = bufs[7][496 * n : 496 * n + 496].astype(F32)
        low, high = value[:328], value[328:]
        left = jnp.concatenate([low[:, :64], low[8:, 64:]], axis=0)
        right = jnp.concatenate(
            [high[:, :32], high[8:, 32:64], high[8:, 64:96], high[8:, 96:]], axis=0
        )
        og_ref[(at["zh"] + by) % 4] = jnp.concatenate([left, right], axis=1).astype(BF16)

    arrived(fy_near)
    activate(1, actx, 96)
    activate(3, actx, 192)
    weigh(actx, 96, first_g, 496)
    weigh(actx, 192, first_g, 992)
    a = core_reduce(first_bufs, FIRST)
    arrived(fy_far)
    activate(2, acty, 0)
    for t in range(2):
        dsend[t : t + 1] = jnp.sum(dacc[CH * t : CH * t + CH], axis=0, keepdims=True)
    dys = [send(dsend, dry.at[by - 1], shifted(at, y=by)) for by in (2, 1, 3)]
    arrived([a])
    a = x_reduce(first_bufs, FIRST)
    weigh(acty, 0, far_g, 0)
    b = core_reduce(far_bufs, FAR)
    arrived(dys)
    dmid[...] = dsend[...] + dry[0] + dry[1] + dry[2]
    dzs = [send(dmid, drz.at[by - 1], shifted(at, zh=by)) for by in (2, 1, 3)]
    arrived([b])
    b = x_reduce(far_bufs, FAR)
    arrived(a)
    a = z_reduce(first_bufs, FIRST)
    arrived(b)
    b = z_reduce(far_bufs, FAR)
    arrived(a)
    a = z_gather(first_bufs, FIRST)
    arrived(b)
    b = z_gather(far_bufs, FAR)
    arrived(a)
    a = x_gather(first_bufs, FIRST)
    arrived(b)
    b = x_gather(far_bufs, FAR)

    arrived(zsends + dzs)
    grad = q[...] + rz[0].astype(F32) + rz[1].astype(F32) + rz[2].astype(F32)
    dots = dmid[...] + drz[0] + drz[1] + drz[2]
    mine_x = f_ref[...].astype(F32)
    ct = d_ref[...].astype(F32)
    outs = []
    for t in range(2):
        rows = slice(CH * t, CH * t + CH)
        x = mine_x[rows]
        _, slope = activation(x, t, chan)
        up = grad[rows] * slope
        r = inv[t : t + 1]
        back = r * up - x * (r * r * r * dots[t : t + 1] * (1.0 / TOTAL))
        outs.append(ct[rows] + back)
    od_ref[...] = jnp.concatenate(outs, axis=0).astype(BF16)

    arrived(a)
    a = core_gather(first_bufs, FIRST)
    arrived(b)
    b = core_gather(far_bufs, FAR)
    arrived([a])
    deliver(first_bufs, 0, 0)
    deliver(first_bufs, 1, 1)
    deliver(first_bufs, 2, 3)
    arrived([b])
    deliver(far_bufs, 0, 2)
    for copy in started:
        copy.wait_send()


def chain_buffers(size):
    return [
        pltpu.VMEM((size, 128), F32),
        pltpu.VMEM((size // 2, 128), F32),
        pltpu.VMEM((size // 8, 128), F32),
        pltpu.VMEM((3, size // 8, 128), BF16),
        pltpu.VMEM((3, size // 8, 128), BF16),
        pltpu.VMEM((3, size // 32, 128), F32),
        pltpu.VMEM((3, size // 32, 128), F32),
        pltpu.VMEM((size, 128), BF16),
    ]


def on_device(features, cotangent, conv_weight, norm_gain, norm_bias):
    chans, frames, rows, cols = features.shape
    f = jnp.transpose(features, (1, 0, 2, 3)).reshape(frames * chans, rows * cols)
    d = jnp.transpose(cotangent, (1, 0, 2, 3)).reshape(frames * chans, rows * cols)
    w = jnp.transpose(conv_weight.reshape(chans, 3, 9, TOTAL), (1, 3, 2, 0)).reshape(3, TOTAL, 9 * chans)
    gb = jnp.stack([norm_gain, norm_bias], axis=1)
    vmem = pl.BlockSpec(memory_space=pltpu.VMEM)
    sums = pltpu.VMEM((2, LANES), F32)
    grads, out = pl.pallas_call(
        kernel,
        name="unit_backward",
        out_shape=(
            jax.ShapeDtypeStruct((4, 648, 96), BF16),
            jax.ShapeDtypeStruct((48, LANES), BF16),
        ),
        in_specs=[vmem] * 4,
        out_specs=(vmem, vmem),
        scratch_shapes=[
            pltpu.VMEM((48, LANES), BF16),
            pltpu.VMEM((4, 48, 256), BF16),
            pltpu.VMEM((16, 48, LANES), BF16),
            pltpu.VMEM((4, 216, LANES), BF16),
            pltpu.VMEM((2, TOTAL, LANES), F32),
            pltpu.VMEM((3, 4, 48, LANES), BF16),
            pltpu.VMEM((3, 4, 48, LANES), BF16),
            pltpu.VMEM((48, LANES), F32),
            pltpu.VMEM((3, 48, LANES), BF16),
            pltpu.VMEM((3, 48, LANES), BF16),
            pltpu.VMEM((2, 288, LANES), BF16),
            pltpu.VMEM((2, 96, LANES), BF16),
            sums,
            pltpu.VMEM((48, LANES), F32),
            sums,
            pltpu.VMEM((4, 2, LANES), F32),
            pltpu.VMEM((3, 2, LANES), F32),
            sums,
            sums,
            sums,
            pltpu.VMEM((3, 2, LANES), F32),
            pltpu.VMEM((3, 2, LANES), F32),
            pltpu.VMEM((648, 96), F32),
            chain_buffers(FIRST),
            chain_buffers(FAR),
            pltpu.SemaphoreType.DMA((COPIES,)),
            pltpu.SemaphoreType.DMA((COPIES,)),
        ],
        compiler_params=pltpu.CompilerParams(
            collective_id=0, has_side_effects=True, vmem_limit_bytes=40 << 20
        ),
    )(f, d, w, gb)
    result = jnp.transpose(out.reshape(frames, chans, rows, cols), (1, 0, 2, 3))
    flat = jnp.transpose(grads, (1, 0, 2)).reshape(27, chans, TOTAL)
    weight_grad = jnp.transpose(flat, (1, 0, 2)).astype(F32)
    return result, weight_grad


def solution(mesh):
    return jax.shard_map(
        on_device,
        mesh=mesh,
        in_specs=(
            P("chan", "tm", "height", None),
            P("chan", "tm", "height", None),
            P("chan", None, None),
            P(),
            P(),
        ),
        out_specs=(P("chan", "tm", "height", None), P("chan", None, None)),
        check_vma=False,
    )
```

```python
import functools
import math

import jax
import jax.numpy as jnp
from jax import lax
from jax.experimental import pallas as pl
from jax.experimental.pallas import tpu as pltpu
from jax.sharding import PartitionSpec as P

MESH = pl.DeviceIdType.MESH
SIZES = {"x": 4, "zl": 4, "k": 2, "zh": 4, "y": 4}
CH = 24
TOTAL = 384
LANES = 640
F32 = jnp.float32
BF16 = jnp.bfloat16


def coords():
    t = lax.axis_index("tm")
    h = lax.axis_index("height")
    c = lax.axis_index("chan")
    return {"x": t, "zl": h // 2, "k": h % 2, "zh": c // 4, "y": c % 4}


def shifted(at, **offsets):
    at = dict(at)
    for name, by in offsets.items():
        at[name] = (at[name] + (by % SIZES[name])) % SIZES[name]
    return {"tm": at["x"], "height": at["zl"] * 2 + at["k"], "chan": at["zh"] * 4 + at["y"]}


def neighbour(at, dx, dh):
    t = (at["x"] + (dx % 4)) % 4
    h = (at["zl"] * 2 + at["k"] + (dh % 8)) % 8
    return {"tm": t, "height": h, "chan": at["zh"] * 4 + at["y"]}


HALO = ((-1, 0), (0, 1), (0, -1), (-1, 1), (-1, -1))
FIRST, FAR = 3 * 512, 512
COPIES = 96


def kernel(
    f_ref, d_ref, w_ref, gb_ref, og_ref, od_ref,
    dn, edges, fall, s9, p, pb, ry, q, qb, rz, actx, acty, inv, dacc,
    sown, smid, sry, srz, dsend, dmid, dry, drz, gc, first_bufs, far_bufs, ssem, rsem,
):
    at = coords()
    chan = at["zh"] * 4 + at["y"]
    count = [0]
    started = []

    def send(src, dst, target):
        i = count[0]
        count[0] += 1
        copy = pltpu.make_async_remote_copy(
            src_ref=src, dst_ref=dst, send_sem=ssem.at[i], recv_sem=rsem.at[i],
            device_id=target, device_id_type=MESH,
        )
        copy.start()
        started.append(copy)
        return copy

    def arrived(copies):
        for copy in copies:
            copy.wait_recv()

    barrier = pltpu.get_barrier_semaphore()
    greeted = [shifted(at, zh=1), shifted(at, zh=3)]
    greeted += [neighbour(at, -dx, -dh) for dx, dh in HALO]
    for name in ("y", "x", "zl"):
        greeted += [shifted(at, **{name: by}) for by in (1, 2, 3)]
    greeted.append(shifted(at, k=1))
    for one in greeted:
        pl.semaphore_signal(barrier, inc=1, device_id=one, device_id_type=MESH)

    fall[chan] = f_ref[...]
    squares = f_ref[...].astype(F32)
    squares = squares * squares
    for t in range(2):
        sown[t : t + 1] = jnp.sum(squares[CH * t : CH * t + CH], axis=0, keepdims=True)
    pl.semaphore_wait(barrier, len(greeted))

    halo = []
    for n, (dx, dh) in enumerate(HALO):
        if n == 0:
            src, dst = d_ref, dn
        else:
            src = d_ref.at[:, pl.ds(384 if dh == 1 else 0, 256)]
            dst = edges.at[n - 1]
        halo.append(send(src, dst, neighbour(at, dx, dh)))
    fz = [send(f_ref, fall.at[chan], shifted(at, zh=by)) for by in (1, 3)]
    sys = [send(sown, sry.at[by - 1], shifted(at, y=by)) for by in (2, 1, 3)]

    def forward(src, block):
        return [send(src, fall.at[block], shifted(at, y=by)) for by in (2, 1, 3)]

    fy_own = forward(f_ref, chan)

    arrived(halo)
    lane = lax.broadcasted_iota(jnp.int32, (CH, LANES), 1) % 160
    left_end, right_end = lane == 0, lane == 159
    row = at["zl"] * 2 + at["k"]
    top_on = jnp.where(row > 0, 1.0, 0.0).astype(F32)
    bottom_on = jnp.where(row < 7, 1.0, 0.0).astype(F32)
    next_on = jnp.where(at["x"] < 3, 1.0, 0.0).astype(F32)
    for tp in range(4):
        rows = slice(CH * (tp % 2), CH * (tp % 2) + CH)
        late = tp >= 2
        own = (dn if late else d_ref)[...].astype(F32)[rows]
        top = edges[2 if late else 0].astype(F32)[rows] * top_on
        bottom = edges[3 if late else 1].astype(F32)[rows] * bottom_on
        if late:
            own, top, bottom = own * next_on, top * next_on, bottom * next_on
        moved = (
            jnp.concatenate([own[:, 160:], bottom[:, :160]], axis=1),
            own,
            jnp.concatenate([top[:, 96:], own[:, :480]], axis=1),
        )
        pieces = []
        for one in moved:
            pieces.append(jnp.where(right_end, 0.0, pltpu.roll(one, LANES - 1, 1)))
            pieces.append(one)
            pieces.append(jnp.where(left_end, 0.0, pltpu.roll(one, 1, 1)))
        s9[tp] = jnp.concatenate(pieces, axis=0).astype(BF16)

    arrived(sys)
    smid[0] = sown[...] + sry[0] + sry[1] + sry[2]
    szs = [send(smid.at[0], smid.at[by], shifted(at, zh=by)) for by in (1, 3)]

    for t in range(2):
        total = None
        for kt in range(3):
            part = jnp.dot(w_ref[kt], s9[t + 2 - kt], preferred_element_type=F32)
            total = part if total is None else total + part
        p[t] = total

    def parts(zh, y):
        start = pl.multiple_of((zh * 4 + y) * CH, 8)
        return jnp.concatenate([p[0, pl.ds(start, CH)], p[1, pl.ds(start, CH)]], axis=0)

    ys = {}

    def reduce_y(z_by):
        for by in (2, 1, 3):
            pb[by - 1, z_by] = parts((at["zh"] + z_by) % 4, (at["y"] + by) % 4).astype(BF16)
        ys[z_by] = [send(pb.at[by - 1, z_by], ry.at[by - 1, z_by], shifted(at, y=by)) for by in (2, 1, 3)]

    reduce_y(2)

    def block_at(by):
        return (at["zh"] + by) % 4 * 4 + at["y"]

    side = 1 + 2 * at["k"]
    arrived(fz)
    source = (at["zh"] + side) % 4 * 4 + at["y"]
    away = {"tm": at["x"], "height": row, "chan": (at["zh"] + 4 - side) % 4 * 4 + at["y"]}
    fz_far = send(fall.at[source], fall.at[source], away)
    fy_near = forward(fall.at[block_at(3)], block_at(3)) + forward(fall.at[block_at(1)], block_at(1))
    reduce_y(1)
    reduce_y(3)
    reduce_y(0)

    arrived(szs)
    szf = send(smid.at[1], srz, shifted(at, zh=1))
    arrived([szf])
    total = smid[0] + smid[1] + smid[3] + srz[...]
    inv[...] = lax.rsqrt(total * (1.0 / TOTAL) + 1e-06)
    dacc[...] = jnp.zeros_like(dacc)

    def activation(x, t, block):
        start = pl.multiple_of(block * CH, 8)
        gain = gb_ref[pl.ds(start, CH), 0:1]
        bias = gb_ref[pl.ds(start, CH), 1:2]
        normed = x * inv[t : t + 1] * gain + bias
        sig = 1.0 / (1.0 + jnp.exp(-normed))
        return normed * sig, sig * (1.0 + normed * (1.0 - sig)) * gain

    def activate(by, dst, base):
        zh = (at["zh"] + by) % 4

        @pl.loop(0, 2)
        def _(n):
            blocks = [fall[zh * 4 + 2 * n + j].astype(F32) for j in range(2)]
            for t in range(2):
                both = []
                for j in range(2):
                    x = blocks[j][CH * t : CH * t + CH]
                    active, slope = activation(x, t, zh * 4 + 2 * n + j)
                    both.append(active)
                    start = pl.multiple_of((zh * 4 + 2 * n + j) * CH, 8)
                    dacc[CH * t : CH * t + CH] += p[t, pl.ds(start, CH)] * slope * x
                dst[t, pl.ds(pl.multiple_of(base + n * 48, 16), 48)] = jnp.concatenate(both, axis=0).astype(BF16)

    def weigh(act, base, g, at_row):
        for kt in range(3):
            total = None
            for t in range(2):
                part = lax.dot_general(
                    s9[t + 2 - kt], act[t, base : base + 96], (((1,), (1,)), ((), ())), preferred_element_type=F32
                )
                total = part if total is None else total + part
            gc[216 * kt : 216 * kt + 216] = total
        g[at_row : at_row + 328] = jnp.concatenate([gc[0:328, 0:64], gc[320:648, 0:64]], axis=1)
        g[at_row + 328 : at_row + 496] = jnp.concatenate(
            [gc[160 * n : 160 * n + 168, 64:96] for n in range(4)], axis=1
        )

    first_g, far_g = first_bufs[0], far_bufs[0]
    first_g[1488:FIRST] = jnp.zeros((FIRST - 1488, 128), F32)
    far_g[496:FAR] = jnp.zeros((FAR - 496, 128), F32)

    zsends = []

    def reduce_z(by):
        arrived(ys[by])
        value = parts((at["zh"] + by) % 4, at["y"])
        for n in range(3):
            value = value + ry[n, by].astype(F32)
        if by == 0:
            q[...] = value
        else:
            qb[by - 1] = value.astype(BF16)
            zsends.append(send(qb.at[by - 1], rz.at[by - 1], shifted(at, zh=by)))

    arrived(fy_own)
    activate(0, actx, 0)
    weigh(actx, 0, first_g, 0)
    reduce_z(2)
    arrived([fz_far])
    fy_far = forward(fall.at[block_at(2)], block_at(2))

    def core_reduce(bufs, size):
        g, gr = bufs[0], bufs[1]
        other = pl.multiple_of((1 - at["k"]) * (size // 2), size // 2)
        return send(g.at[pl.ds(other, size // 2)], gr, shifted(at, k=1))

    def x_reduce(bufs, size):
        g, gr, h, hb, hr = bufs[:5]
        quarter = size // 8
        sends = []
        for by in (2, 1, 3, 0):
            start = (at["x"] + by) % 4 * quarter
            value = (
                g[pl.ds(pl.multiple_of(at["k"] * (size // 2) + start, quarter), quarter)]
                + gr[pl.ds(pl.multiple_of(start, quarter), quarter)]
            )
            if by == 0:
                h[...] = value
            else:
                hb[by - 1] = value.astype(BF16)
                sends.append(send(hb.at[by - 1], hr.at[by - 1], shifted(at, x=by)))
        return sends

    def z_reduce(bufs, size):
        h, hr, zs, zr = bufs[2], bufs[4], bufs[5], bufs[6]
        part = size // 32
        h[...] = h[...] + hr[0].astype(F32) + hr[1].astype(F32) + hr[2].astype(F32)
        sends = []
        for by in (3, 1, 2):
            start = pl.multiple_of((at["zl"] + by) % 4 * part, part)
            zs[by - 1] = h[pl.ds(start, part)]
            sends.append(send(zs.at[by - 1], zr.at[by - 1], shifted(at, zl=by)))
        return sends

    def z_gather(bufs, size):
        h, zr, ag = bufs[2], bufs[6], bufs[7]
        part = size // 32
        value = h[pl.ds(pl.multiple_of(at["zl"] * part, part), part)] + zr[0] + zr[1] + zr[2]
        piece = pl.multiple_of(at["k"] * (size // 2) + at["x"] * (size // 8) + at["zl"] * part, part)
        ag[pl.ds(piece, part)] = (value * (1.0 / math.sqrt(40960))).astype(BF16)
        ref = ag.at[pl.ds(piece, part)]
        return [send(ref, ref, shifted(at, zl=by)) for by in (3, 1, 2)]

    def x_gather(bufs, size):
        start = pl.multiple_of(at["k"] * (size // 2) + at["x"] * (size // 8), size // 8)
        ref = bufs[7].at[pl.ds(start, size // 8)]
        return [send(ref, ref, shifted(at, x=by)) for by in (2, 1, 3)]

    def core_gather(bufs, size):
        ref = bufs[7].at[pl.ds(pl.multiple_of(at["k"] * (size // 2), size // 2), size // 2)]
        return send(ref, ref, shifted(at, k=1))

    def deliver(bufs, n, by):
        value = bufs[7][496 * n : 496 * n + 496].astype(F32)
        low, high = value[:328], value[328:]
        left = jnp.concatenate([low[:, :64], low[8:, 64:]], axis=0)
        right = jnp.concatenate(
            [high[:, :32], high[8:, 32:64], high[8:, 64:96], high[8:, 96:]], axis=0
        )
        og_ref[(at["zh"] + by) % 4] = jnp.concatenate([left, right], axis=1).astype(BF16)

    arrived(fy_near)
    activate(1, actx, 96)
    weigh(actx, 96, first_g, 496)
    reduce_z(1)
    activate(3, actx, 192)
    weigh(actx, 192, first_g, 992)
    reduce_z(3)
    a = core_reduce(first_bufs, FIRST)
    arrived(fy_far)
    activate(2, acty, 0)
    for t in range(2):
        dsend[t : t + 1] = jnp.sum(dacc[CH * t : CH * t + CH], axis=0, keepdims=True)
    dys = [send(dsend, dry.at[by - 1], shifted(at, y=by)) for by in (2, 1, 3)]
    arrived([a])
    a = x_reduce(first_bufs, FIRST)
    weigh(acty, 0, far_g, 0)
    b = core_reduce(far_bufs, FAR)
    arrived(dys)
    dmid[...] = dsend[...] + dry[0] + dry[1] + dry[2]
    reduce_z(0)
    dzs = [send(dmid, drz.at[by - 1], shifted(at, zh=by)) for by in (2, 1, 3)]
    arrived([b])
    b = x_reduce(far_bufs, FAR)
    arrived(a)
    a = z_reduce(first_bufs, FIRST)
    arrived(b)
    b = z_reduce(far_bufs, FAR)
    arrived(a)
    a = z_gather(first_bufs, FIRST)
    arrived(b)
    b = z_gather(far_bufs, FAR)
    arrived(a)
    a = x_gather(first_bufs, FIRST)
    arrived(b)
    b = x_gather(far_bufs, FAR)

    arrived(zsends + dzs)
    grad = q[...] + rz[0].astype(F32) + rz[1].astype(F32) + rz[2].astype(F32)
    dots = dmid[...] + drz[0] + drz[1] + drz[2]
    mine_x = f_ref[...].astype(F32)
    ct = d_ref[...].astype(F32)
    outs = []
    for t in range(2):
        rows = slice(CH * t, CH * t + CH)
        x = mine_x[rows]
        _, slope = activation(x, t, chan)
        up = grad[rows] * slope
        r = inv[t : t + 1]
        back = r * up - x * (r * r * r * dots[t : t + 1] * (1.0 / TOTAL))
        outs.append(ct[rows] + back)
    od_ref[...] = jnp.concatenate(outs, axis=0).astype(BF16)

    arrived(a)
    a = core_gather(first_bufs, FIRST)
    arrived(b)
    b = core_gather(far_bufs, FAR)
    arrived([a])
    deliver(first_bufs, 0, 0)
    deliver(first_bufs, 1, 1)
    deliver(first_bufs, 2, 3)
    arrived([b])
    deliver(far_bufs, 0, 2)
    for copy in started:
        copy.wait_send()


def chain_buffers(size):
    return [
        pltpu.VMEM((size, 128), F32),
        pltpu.VMEM((size // 2, 128), F32),
        pltpu.VMEM((size // 8, 128), F32),
        pltpu.VMEM((3, size // 8, 128), BF16),
        pltpu.VMEM((3, size // 8, 128), BF16),
        pltpu.VMEM((3, size // 32, 128), F32),
        pltpu.VMEM((3, size // 32, 128), F32),
        pltpu.VMEM((size, 128), BF16),
    ]


def on_device(features, cotangent, conv_weight, norm_gain, norm_bias):
    chans, frames, rows, cols = features.shape
    f = jnp.transpose(features, (1, 0, 2, 3)).reshape(frames * chans, rows * cols)
    d = jnp.transpose(cotangent, (1, 0, 2, 3)).reshape(frames * chans, rows * cols)
    w = jnp.transpose(conv_weight.reshape(chans, 3, 9, TOTAL), (1, 3, 2, 0)).reshape(3, TOTAL, 9 * chans)
    gb = jnp.stack([norm_gain, norm_bias], axis=1)
    vmem = pl.BlockSpec(memory_space=pltpu.VMEM)
    sums = pltpu.VMEM((2, LANES), F32)
    grads, out = pl.pallas_call(
        kernel,
        name="unit_backward",
        out_shape=(
            jax.ShapeDtypeStruct((4, 648, 96), BF16),
            jax.ShapeDtypeStruct((48, LANES), BF16),
        ),
        in_specs=[vmem] * 4,
        out_specs=(vmem, vmem),
        scratch_shapes=[
            pltpu.VMEM((48, LANES), BF16),
            pltpu.VMEM((4, 48, 256), BF16),
            pltpu.VMEM((16, 48, LANES), BF16),
            pltpu.VMEM((4, 216, LANES), BF16),
            pltpu.VMEM((2, TOTAL, LANES), F32),
            pltpu.VMEM((3, 4, 48, LANES), BF16),
            pltpu.VMEM((3, 4, 48, LANES), BF16),
            pltpu.VMEM((48, LANES), F32),
            pltpu.VMEM((3, 48, LANES), BF16),
            pltpu.VMEM((3, 48, LANES), BF16),
            pltpu.VMEM((2, 288, LANES), BF16),
            pltpu.VMEM((2, 96, LANES), BF16),
            sums,
            pltpu.VMEM((48, LANES), F32),
            sums,
            pltpu.VMEM((4, 2, LANES), F32),
            pltpu.VMEM((3, 2, LANES), F32),
            sums,
            sums,
            sums,
            pltpu.VMEM((3, 2, LANES), F32),
            pltpu.VMEM((3, 2, LANES), F32),
            pltpu.VMEM((648, 96), F32),
            chain_buffers(FIRST),
            chain_buffers(FAR),
            pltpu.SemaphoreType.DMA((COPIES,)),
            pltpu.SemaphoreType.DMA((COPIES,)),
        ],
        compiler_params=pltpu.CompilerParams(
            collective_id=0, has_side_effects=True, vmem_limit_bytes=40 << 20
        ),
    )(f, d, w, gb)
    result = jnp.transpose(out.reshape(frames, chans, rows, cols), (1, 0, 2, 3))
    flat = jnp.transpose(grads, (1, 0, 2)).reshape(27, chans, TOTAL)
    weight_grad = jnp.transpose(flat, (1, 0, 2)).astype(F32)
    return result, weight_grad


def solution(mesh):
    return jax.shard_map(
        on_device,
        mesh=mesh,
        in_specs=(
            P("chan", "tm", "height", None),
            P("chan", "tm", "height", None),
            P("chan", None, None),
            P(),
            P(),
        ),
        out_specs=(P("chan", "tm", "height", None), P("chan", None, None)),
        check_vma=False,
    )
```

```python
import functools
import math

import jax
import jax.numpy as jnp
from jax import lax
from jax.experimental import pallas as pl
from jax.experimental.pallas import tpu as pltpu
from jax.sharding import PartitionSpec as P

MESH = pl.DeviceIdType.MESH
SIZES = {"x": 4, "zl": 4, "k": 2, "zh": 4, "y": 4}
CH = 24
TOTAL = 384
LANES = 640
F32 = jnp.float32
BF16 = jnp.bfloat16


def coords():
    t = lax.axis_index("tm")
    h = lax.axis_index("height")
    c = lax.axis_index("chan")
    return {"x": t, "zl": h // 2, "k": h % 2, "zh": c // 4, "y": c % 4}


def shifted(at, **offsets):
    at = dict(at)
    for name, by in offsets.items():
        at[name] = (at[name] + (by % SIZES[name])) % SIZES[name]
    return {"tm": at["x"], "height": at["zl"] * 2 + at["k"], "chan": at["zh"] * 4 + at["y"]}


def neighbour(at, dx, dh):
    t = (at["x"] + (dx % 4)) % 4
    h = (at["zl"] * 2 + at["k"] + (dh % 8)) % 8
    return {"tm": t, "height": h, "chan": at["zh"] * 4 + at["y"]}


HALO = ((-1, 0), (0, 1), (0, -1), (-1, 1), (-1, -1))
FIRST, FAR = 3 * 512, 512
COPIES = 112
STEPS = tuple(slice(16 * n, 16 * n + 16) for n in range(3))


def kernel(
    f_ref, d_ref, raw_ref, gain_ref, bias_ref, og_ref, od_ref, wide, w_ref, gb_ref,
    dn, edges, fall, s9, p, pb, ry, q, qb, rz, actx, acty, inv, dacc,
    sown, smid, sry, srz, dsend, dmid, dry, drz, gc, first_bufs, far_bufs, ssem, rsem,
):
    at = coords()
    chan = at["zh"] * 4 + at["y"]
    count = [0]
    started = []

    def send(src, dst, target):
        i = count[0]
        count[0] += 1
        copy = pltpu.make_async_remote_copy(
            src_ref=src, dst_ref=dst, send_sem=ssem.at[i], recv_sem=rsem.at[i],
            device_id=target, device_id_type=MESH,
        )
        copy.start()
        started.append(copy)
        return copy

    def arrived(copies):
        for copy in copies:
            copy.wait_recv()

    edges[...] = jnp.zeros_like(edges)
    barrier = pltpu.get_barrier_semaphore()
    greeted = [shifted(at, zh=1), shifted(at, zh=3)]
    greeted += [neighbour(at, -dx, -dh) for dx, dh in HALO]
    for name in ("y", "x", "zl"):
        greeted += [shifted(at, **{name: by}) for by in (1, 2, 3)]
    greeted.append(shifted(at, k=1))
    for one in greeted:
        pl.semaphore_signal(barrier, inc=1, device_id=one, device_id_type=MESH)

    fall[chan] = f_ref[...]
    squares = f_ref[...].astype(F32)
    squares = squares * squares
    for t in range(2):
        sown[t : t + 1] = jnp.sum(squares[CH * t : CH * t + CH], axis=0, keepdims=True)
    both = jnp.concatenate([gain_ref[...], bias_ref[...], jnp.zeros((6, TOTAL), F32)], axis=0)
    gb_ref[...] = both.T

    @pl.loop(0, CH)
    def _(n):
        whole = raw_ref[n].astype(F32)
        for c in range(3):
            wide[c, pl.ds(pl.multiple_of(n * 32, 32), 27)] = whole[:, 128 * c : 128 * c + 128]

    for kt in range(3):
        for c in range(3):
            taps = [wide[c, pl.ds(9 * kt + j, CH, stride=32), :] for j in range(9)]
            w_ref[kt, 128 * c : 128 * c + 128] = jnp.concatenate(taps, axis=0).T.astype(BF16)

    pl.semaphore_wait(barrier, len(greeted))

    row = at["zl"] * 2 + at["k"]
    below, above = row < 7, row > 0
    frame = send(d_ref, dn, neighbour(at, -1, 0))
    halo = []
    for n, (dx, dh) in enumerate(HALO[1:]):
        i = count[0]
        count[0] += 1
        copy = pltpu.make_async_remote_copy(
            src_ref=d_ref.at[:, pl.ds(384 if dh == 1 else 0, 256)], dst_ref=edges.at[n],
            send_sem=ssem.at[i], recv_sem=rsem.at[i],
            device_id=neighbour(at, dx, dh), device_id_type=MESH,
        )
        goes, comes = (below, above) if dh == 1 else (above, below)
        pl.when(goes)(copy.start)
        halo.append((copy, goes, comes))
    fz = [
        [send(f_ref.at[rows], fall.at[chan, rows], shifted(at, zh=by)) for by in (1, 3)] for rows in STEPS
    ]
    sys = [send(sown, sry.at[by - 1], shifted(at, y=by)) for by in (2, 1, 3)]

    def forward(src, block):
        return [send(src, fall.at[block], shifted(at, y=by)) for by in (2, 1, 3)]

    fy_own = forward(f_ref, chan)

    arrived([frame])
    for copy, _, comes in halo:
        pl.when(comes)(copy.wait_recv)
    lane = lax.broadcasted_iota(jnp.int32, (CH, LANES), 1) % 160
    left_end, right_end = lane == 0, lane == 159
    next_on = jnp.where(at["x"] < 3, 1.0, 0.0).astype(F32)
    for tp in range(4):
        rows = slice(CH * (tp % 2), CH * (tp % 2) + CH)
        late = tp >= 2
        own = (dn if late else d_ref)[...].astype(F32)[rows]
        top = edges[2 if late else 0].astype(F32)[rows]
        bottom = edges[3 if late else 1].astype(F32)[rows]
        if late:
            own, top, bottom = own * next_on, top * next_on, bottom * next_on
        moved = (
            jnp.concatenate([own[:, 160:], bottom[:, :160]], axis=1),
            own,
            jnp.concatenate([top[:, 96:], own[:, :480]], axis=1),
        )
        pieces = []
        for one in moved:
            pieces.append(jnp.where(right_end, 0.0, pltpu.roll(one, LANES - 1, 1)))
            pieces.append(one)
            pieces.append(jnp.where(left_end, 0.0, pltpu.roll(one, 1, 1)))
        s9[tp] = jnp.concatenate(pieces, axis=0).astype(BF16)

    side = 1 + 2 * at["k"]
    source = (at["zh"] + side) % 4 * 4 + at["y"]
    away = {"tm": at["x"], "height": row, "chan": (at["zh"] + 4 - side) % 4 * 4 + at["y"]}
    fz_far = []

    def far_step(n):
        arrived(fz[n])
        ref = fall.at[source, STEPS[n]]
        fz_far.append(send(ref, ref, away))

    arrived(sys)
    smid[0] = sown[...] + sry[0] + sry[1] + sry[2]
    szs = [send(smid.at[0], smid.at[by], shifted(at, zh=by)) for by in (1, 3)]
    far_step(0)

    for t in range(2):
        total = None
        for kt in range(3):
            part = jnp.dot(w_ref[kt], s9[t + 2 - kt], preferred_element_type=F32)
            total = part if total is None else total + part
        p[t] = total

    far_step(1)

    def parts(zh, y):
        start = pl.multiple_of((zh * 4 + y) * CH, 8)
        return jnp.concatenate([p[0, pl.ds(start, CH)], p[1, pl.ds(start, CH)]], axis=0)

    ys = {}

    def reduce_y(z_by):
        for by in (2, 1, 3):
            pb[by - 1, z_by] = parts((at["zh"] + z_by) % 4, (at["y"] + by) % 4).astype(BF16)
        ys[z_by] = [send(pb.at[by - 1, z_by], ry.at[by - 1, z_by], shifted(at, y=by)) for by in (2, 1, 3)]

    reduce_y(2)

    def block_at(by):
        return (at["zh"] + by) % 4 * 4 + at["y"]

    far_step(2)
    fy_near = forward(fall.at[block_at(3)], block_at(3)) + forward(fall.at[block_at(1)], block_at(1))

    arrived(szs)
    szf = send(smid.at[1], srz, shifted(at, zh=1))
    arrived([szf])
    total = smid[0] + smid[1] + smid[3] + srz[...]
    inv[...] = lax.rsqrt(total * (1.0 / TOTAL) + 1e-06)
    dacc[...] = jnp.zeros_like(dacc)

    def activation(x, t, block):
        start = pl.multiple_of(block * CH, 8)
        gain = gb_ref[pl.ds(start, CH), 0:1]
        bias = gb_ref[pl.ds(start, CH), 1:2]
        normed = x * inv[t : t + 1] * gain + bias
        sig = 0.5 * jnp.tanh(0.5 * normed) + 0.5
        return normed * sig, sig * (1.0 + normed * (1.0 - sig)) * gain

    def activate(by, dst, base):
        zh = (at["zh"] + by) % 4

        @pl.loop(0, 2)
        def _(n):
            blocks = [fall[zh * 4 + 2 * n + j].astype(F32) for j in range(2)]
            for t in range(2):
                both = []
                for j in range(2):
                    x = blocks[j][CH * t : CH * t + CH]
                    active, slope = activation(x, t, zh * 4 + 2 * n + j)
                    both.append(active)
                    start = pl.multiple_of((zh * 4 + 2 * n + j) * CH, 8)
                    dacc[CH * t : CH * t + CH] += p[t, pl.ds(start, CH)] * slope * x
                dst[t, pl.ds(pl.multiple_of(base + n * 48, 16), 48)] = jnp.concatenate(both, axis=0).astype(BF16)

    def weigh(act, base, g, at_row):
        for kt in range(3):
            total = None
            for t in range(2):
                part = lax.dot_general(
                    s9[t + 2 - kt], act[t, base : base + 96], (((1,), (1,)), ((), ())), preferred_element_type=F32
                )
                total = part if total is None else total + part
            gc[216 * kt : 216 * kt + 216] = total
        g[at_row : at_row + 328] = jnp.concatenate([gc[0:328, 0:64], gc[320:648, 0:64]], axis=1)
        g[at_row + 328 : at_row + 496] = jnp.concatenate(
            [gc[160 * n : 160 * n + 168, 64:96] for n in range(4)], axis=1
        )

    first_g, far_g = first_bufs[0], far_bufs[0]
    first_g[1488:FIRST] = jnp.zeros((FIRST - 1488, 128), F32)
    far_g[496:FAR] = jnp.zeros((FAR - 496, 128), F32)

    zsends = []

    def reduce_z(by):
        arrived(ys[by])
        value = parts((at["zh"] + by) % 4, at["y"])
        for n in range(3):
            value = value + ry[n, by].astype(F32)
        if by == 0:
            q[...] = value
        else:
            qb[by - 1] = value.astype(BF16)
            zsends.append(send(qb.at[by - 1], rz.at[by - 1], shifted(at, zh=by)))

    arrived(fy_own)
    activate(0, actx, 0)
    weigh(actx, 0, first_g, 0)
    fy_far = []
    for n in range(3):
        arrived([fz_far[n]])
        ref = fall.at[block_at(2), STEPS[n]]
        fy_far += [send(ref, ref, shifted(at, y=by)) for by in (2, 1, 3)]
    reduce_y(1)
    reduce_y(3)
    reduce_y(0)
    reduce_z(2)

    def core_reduce(bufs, size):
        g, gr = bufs[0], bufs[1]
        other = pl.multiple_of((1 - at["k"]) * (size // 2), size // 2)
        return send(g.at[pl.ds(other, size // 2)], gr, shifted(at, k=1))

    def x_reduce(bufs, size):
        g, gr, h, hb, hr = bufs[:5]
        quarter = size // 8
        sends = []
        for by in (2, 1, 3, 0):
            start = (at["x"] + by) % 4 * quarter
            value = (
                g[pl.ds(pl.multiple_of(at["k"] * (size // 2) + start, quarter), quarter)]
                + gr[pl.ds(pl.multiple_of(start, quarter), quarter)]
            )
            if by == 0:
                h[...] = value
            else:
                hb[by - 1] = value.astype(BF16)
                sends.append(send(hb.at[by - 1], hr.at[by - 1], shifted(at, x=by)))
        return sends

    def z_reduce(bufs, size):
        h, hr, zs, zr = bufs[2], bufs[4], bufs[5], bufs[6]
        part = size // 32
        h[...] = h[...] + hr[0].astype(F32) + hr[1].astype(F32) + hr[2].astype(F32)
        sends = []
        for by in (3, 1, 2):
            start = pl.multiple_of((at["zl"] + by) % 4 * part, part)
            zs[by - 1] = h[pl.ds(start, part)]
            sends.append(send(zs.at[by - 1], zr.at[by - 1], shifted(at, zl=by)))
        return sends

    def z_gather(bufs, size):
        h, zr, ag = bufs[2], bufs[6], bufs[7]
        part = size // 32
        value = h[pl.ds(pl.multiple_of(at["zl"] * part, part), part)] + zr[0] + zr[1] + zr[2]
        piece = pl.multiple_of(at["k"] * (size // 2) + at["x"] * (size // 8) + at["zl"] * part, part)
        ag[pl.ds(piece, part)] = (value * (1.0 / math.sqrt(40960))).astype(BF16)
        ref = ag.at[pl.ds(piece, part)]
        return [send(ref, ref, shifted(at, zl=by)) for by in (3, 1, 2)]

    def x_gather(bufs, size):
        start = pl.multiple_of(at["k"] * (size // 2) + at["x"] * (size // 8), size // 8)
        ref = bufs[7].at[pl.ds(start, size // 8)]
        return [send(ref, ref, shifted(at, x=by)) for by in (2, 1, 3)]

    def core_gather(bufs, size):
        ref = bufs[7].at[pl.ds(pl.multiple_of(at["k"] * (size // 2), size // 2), size // 2)]
        return send(ref, ref, shifted(at, k=1))

    def deliver(bufs, n, by):
        value = bufs[7][496 * n : 496 * n + 496].astype(F32)
        low, high = value[:328], value[328:]
        left = jnp.concatenate([low[:, :64], low[8:, 64:]], axis=0)
        right = jnp.concatenate(
            [high[:, :32], high[8:, 32:64], high[8:, 64:96], high[8:, 96:]], axis=0
        )
        og_ref[(at["zh"] + by) % 4] = jnp.concatenate([left, right], axis=1).astype(BF16)

    arrived(fy_near)
    activate(1, actx, 96)
    weigh(actx, 96, first_g, 496)
    reduce_z(1)
    activate(3, actx, 192)
    weigh(actx, 192, first_g, 992)
    reduce_z(3)
    a = core_reduce(first_bufs, FIRST)
    arrived(fy_far)
    activate(2, acty, 0)
    for t in range(2):
        dsend[t : t + 1] = jnp.sum(dacc[CH * t : CH * t + CH], axis=0, keepdims=True)
    dys = [send(dsend, dry.at[by - 1], shifted(at, y=by)) for by in (2, 1, 3)]
    arrived([a])
    a = x_reduce(first_bufs, FIRST)
    weigh(acty, 0, far_g, 0)
    b = core_reduce(far_bufs, FAR)
    arrived(dys)
    dmid[...] = dsend[...] + dry[0] + dry[1] + dry[2]
    reduce_z(0)
    dzs = [send(dmid, drz.at[by - 1], shifted(at, zh=by)) for by in (2, 1, 3)]
    arrived([b])
    b = x_reduce(far_bufs, FAR)
    arrived(a)
    a = z_reduce(first_bufs, FIRST)
    arrived(b)
    b = z_reduce(far_bufs, FAR)
    arrived(a)
    a = z_gather(first_bufs, FIRST)
    arrived(b)
    b = z_gather(far_bufs, FAR)
    arrived(a)
    a = x_gather(first_bufs, FIRST)
    arrived(b)
    b = x_gather(far_bufs, FAR)

    arrived(zsends + dzs)
    grad = q[...] + rz[0].astype(F32) + rz[1].astype(F32) + rz[2].astype(F32)
    dots = dmid[...] + drz[0] + drz[1] + drz[2]
    mine_x = f_ref[...].astype(F32)
    ct = d_ref[...].astype(F32)
    outs = []
    for t in range(2):
        rows = slice(CH * t, CH * t + CH)
        x = mine_x[rows]
        _, slope = activation(x, t, chan)
        up = grad[rows] * slope
        r = inv[t : t + 1]
        back = r * up - x * (r * r * r * dots[t : t + 1] * (1.0 / TOTAL))
        outs.append(ct[rows] + back)
    od_ref[...] = jnp.concatenate(outs, axis=0).astype(BF16)

    arrived(a)
    a = core_gather(first_bufs, FIRST)
    arrived(b)
    b = core_gather(far_bufs, FAR)
    arrived([a])
    deliver(first_bufs, 0, 0)
    deliver(first_bufs, 1, 1)
    deliver(first_bufs, 2, 3)
    arrived([b])
    deliver(far_bufs, 0, 2)
    for copy in started:
        copy.wait_send()
    for copy, goes, _ in halo:
        pl.when(goes)(copy.wait_send)


def chain_buffers(size):
    return [
        pltpu.VMEM((size, 128), F32),
        pltpu.VMEM((size // 2, 128), F32),
        pltpu.VMEM((size // 8, 128), F32),
        pltpu.VMEM((3, size // 8, 128), BF16),
        pltpu.VMEM((3, size // 8, 128), BF16),
        pltpu.VMEM((3, size // 32, 128), F32),
        pltpu.VMEM((3, size // 32, 128), F32),
        pltpu.VMEM((size, 128), BF16),
    ]


def on_device(features, cotangent, conv_weight, norm_gain, norm_bias):
    chans, frames, rows, cols = features.shape
    f = jnp.transpose(features, (1, 0, 2, 3)).reshape(frames * chans, rows * cols)
    d = jnp.transpose(cotangent, (1, 0, 2, 3)).reshape(frames * chans, rows * cols)
    vmem = pl.BlockSpec(memory_space=pltpu.VMEM)
    sums = pltpu.VMEM((2, LANES), F32)
    grads, out = pl.pallas_call(
        kernel,
        name="unit_backward",
        out_shape=(
            jax.ShapeDtypeStruct((4, 648, 96), BF16),
            jax.ShapeDtypeStruct((48, LANES), BF16),
        ),
        in_specs=[vmem] * 5,
        out_specs=(vmem, vmem),
        scratch_shapes=[
            pltpu.VMEM((3, CH * 32, 128), F32),
            pltpu.VMEM((3, TOTAL, 9 * CH), BF16),
            pltpu.VMEM((TOTAL, 8), F32),
            pltpu.VMEM((48, LANES), BF16),
            pltpu.VMEM((4, 48, 256), BF16),
            pltpu.VMEM((16, 48, LANES), BF16),
            pltpu.VMEM((4, 216, LANES), BF16),
            pltpu.VMEM((2, TOTAL, LANES), F32),
            pltpu.VMEM((3, 4, 48, LANES), BF16),
            pltpu.VMEM((3, 4, 48, LANES), BF16),
            pltpu.VMEM((48, LANES), F32),
            pltpu.VMEM((3, 48, LANES), BF16),
            pltpu.VMEM((3, 48, LANES), BF16),
            pltpu.VMEM((2, 288, LANES), BF16),
            pltpu.VMEM((2, 96, LANES), BF16),
            sums,
            pltpu.VMEM((48, LANES), F32),
            sums,
            pltpu.VMEM((4, 2, LANES), F32),
            pltpu.VMEM((3, 2, LANES), F32),
            sums,
            sums,
            sums,
            pltpu.VMEM((3, 2, LANES), F32),
            pltpu.VMEM((3, 2, LANES), F32),
            pltpu.VMEM((648, 96), F32),
            chain_buffers(FIRST),
            chain_buffers(FAR),
            pltpu.SemaphoreType.DMA((COPIES,)),
            pltpu.SemaphoreType.DMA((COPIES,)),
        ],
        compiler_params=pltpu.CompilerParams(
            collective_id=0, has_side_effects=True, vmem_limit_bytes=40 << 20
        ),
    )(f, d, conv_weight, norm_gain.reshape(1, TOTAL), norm_bias.reshape(1, TOTAL))
    result = jnp.transpose(out.reshape(frames, chans, rows, cols), (1, 0, 2, 3))
    flat = jnp.transpose(grads, (1, 0, 2)).reshape(27, chans, TOTAL)
    weight_grad = jnp.transpose(flat, (1, 0, 2)).astype(F32)
    return result, weight_grad


def solution(mesh):
    return jax.shard_map(
        on_device,
        mesh=mesh,
        in_specs=(
            P("chan", "tm", "height", None),
            P("chan", "tm", "height", None),
            P("chan", None, None),
            P(),
            P(),
        ),
        out_specs=(P("chan", "tm", "height", None), P("chan", None, None)),
        check_vma=False,
    )
```

```python
import functools
import math

import jax
import jax.numpy as jnp
from jax import lax
from jax.experimental import pallas as pl
from jax.experimental.pallas import tpu as pltpu
from jax.sharding import PartitionSpec as P

MESH = pl.DeviceIdType.MESH
SIZES = {"x": 4, "zl": 4, "k": 2, "zh": 4, "y": 4}
CH = 24
TOTAL = 384
LANES = 640
F32 = jnp.float32
BF16 = jnp.bfloat16


def coords():
    t = lax.axis_index("tm")
    h = lax.axis_index("height")
    c = lax.axis_index("chan")
    return {"x": t, "zl": h // 2, "k": h % 2, "zh": c // 4, "y": c % 4}


def shifted(at, **offsets):
    at = dict(at)
    for name, by in offsets.items():
        at[name] = (at[name] + (by % SIZES[name])) % SIZES[name]
    return {"tm": at["x"], "height": at["zl"] * 2 + at["k"], "chan": at["zh"] * 4 + at["y"]}


def neighbour(at, dx, dh):
    t = (at["x"] + (dx % 4)) % 4
    h = (at["zl"] * 2 + at["k"] + (dh % 8)) % 8
    return {"tm": t, "height": h, "chan": at["zh"] * 4 + at["y"]}


HALO = ((-1, 0), (0, 1), (0, -1), (-1, 1), (-1, -1))
COPIES = 96
STEPS = tuple(slice(16 * n, 16 * n + 16) for n in range(3))
SLOTS = (0, 1, 3, 2)
ROWS = 512
USED = 496


def kernel(
    f_ref, d_ref, raw_hbm, gain_ref, bias_ref, og_ref, od_ref,
    raw, wide, tall, slabs, wall, gb_ref, dall, dnall, edall, fall, s9, p, q, qb, rz, act, sx, inv,
    sown, smid, sry, srz, dsend, dmid, dry, drz, gc, perm, ag, chain_a, chain_b, lsem, ssem, rsem,
):
    at = coords()
    count = [0]
    started = []

    def send(src, dst, target):
        i = count[0]
        count[0] += 1
        copy = pltpu.make_async_remote_copy(
            src_ref=src, dst_ref=dst, send_sem=ssem.at[i], recv_sem=rsem.at[i],
            device_id=target, device_id_type=MESH,
        )
        copy.start()
        started.append(copy)
        return copy

    def arrived(copies):
        for copy in copies:
            copy.wait_recv()

    own_weight = pltpu.make_async_copy(raw_hbm, raw, lsem)
    own_weight.start()
    edall[0] = jnp.zeros((4, 48, 256), BF16)
    barrier = pltpu.get_barrier_semaphore()
    greeted = [shifted(at, zh=1), shifted(at, zh=3)]
    greeted += [neighbour(at, -dx, -dh) for dx, dh in HALO]
    greeted += [shifted(at, x=by) for by in (1, 2, 3)]
    greeted += [shifted(at, y=dy, zl=dz) for dy in range(4) for dz in range(4) if dy or dz]
    greeted.append(shifted(at, k=1))
    for one in greeted:
        pl.semaphore_signal(barrier, inc=1, device_id=one, device_id_type=MESH)

    fall[at["zh"]] = f_ref[...]
    squares = f_ref[...].astype(F32)
    squares = squares * squares
    for t in range(2):
        sown[t : t + 1] = jnp.sum(squares[CH * t : CH * t + CH], axis=0, keepdims=True)
    both = jnp.concatenate([gain_ref[...], bias_ref[...], jnp.zeros((6, TOTAL), F32)], axis=0)
    gb_ref[...] = both.T

    own_weight.wait()

    @pl.loop(0, CH)
    def _(n):
        whole = raw[n].astype(F32)
        for c in range(3):
            wide[c, pl.ds(pl.multiple_of(n * 32, 32), 27)] = whole[:, 128 * c : 128 * c + 128]

    for kt in range(3):
        for c in range(3):
            taps = [wide[c, pl.ds(9 * kt + j, CH, stride=32), :] for j in range(9)]
            tall[kt, 128 * c : 128 * c + 128] = jnp.concatenate(taps, axis=0).T

    def slab(by):
        y = (at["y"] + by) % 4
        groups = [
            tall[kt, pl.ds(pl.multiple_of(96 * zh + y * CH, 8), CH)] for kt in range(3) for zh in range(4)
        ]
        return jnp.concatenate(groups, axis=0).astype(BF16)

    wall[0] = slab(0)
    for by in (1, 2, 3):
        slabs[by - 1] = slab(by)
    r = lax.broadcasted_iota(jnp.int32, (96, TOTAL), 0)
    lane = lax.broadcasted_iota(jnp.int32, (96, TOTAL), 1)
    group = (r >= 24).astype(jnp.int32) + (r >= 48).astype(jnp.int32) + (r >= 72).astype(jnp.int32)
    for s in range(4):
        target = r + 72 * group + CH * ((at["y"] + s) % 4)
        perm[s] = jnp.where(lane == target, 1.0, 0.0).astype(BF16)

    pl.semaphore_wait(barrier, len(greeted))

    row = at["zl"] * 2 + at["k"]
    below, above = row < 7, row > 0
    frame = send(d_ref, dnall.at[0], neighbour(at, -1, 0))
    halo = []
    for n, (dx, dh) in enumerate(HALO[1:]):
        i = count[0]
        count[0] += 1
        copy = pltpu.make_async_remote_copy(
            src_ref=d_ref.at[:, pl.ds(384 if dh == 1 else 0, 256)], dst_ref=edall.at[0, n],
            send_sem=ssem.at[i], recv_sem=rsem.at[i],
            device_id=neighbour(at, dx, dh), device_id_type=MESH,
        )
        goes, comes = (below, above) if dh == 1 else (above, below)
        pl.when(goes)(copy.start)
        halo.append((copy, goes, comes))
    fz = [
        [send(f_ref.at[rows], fall.at[at["zh"], rows], shifted(at, zh=by)) for by in (1, 3)] for rows in STEPS
    ]
    sys = [send(sown, sry.at[by - 1], shifted(at, y=by)) for by in (2, 1, 3)]
    dy = {by: [send(d_ref, dall.at[by - 1], shifted(at, y=by))] for by in (2, 1, 3)}

    arrived([frame])
    for by in (2, 1, 3):
        dy[by].append(send(dnall.at[0], dnall.at[by], shifted(at, y=by)))
    for copy, _, comes in halo:
        pl.when(comes)(copy.wait_recv)
    for by in (2, 1, 3):
        dy[by].append(send(edall.at[0], edall.at[by], shifted(at, y=by)))
    half = pl.multiple_of(at["k"] * 144, 16)
    ws = [
        send(slabs.at[by - 1, pl.ds(half, 144)], wall.at[by, pl.ds(half, 144)], shifted(at, y=by))
        for by in (2, 1, 3)
    ]

    column = lax.broadcasted_iota(jnp.int32, (CH, LANES), 1) % 160
    left_end, right_end = column == 0, column == 159
    next_on = jnp.where(at["x"] < 3, 1.0, 0.0).astype(F32)

    def build(slot):
        for tp in range(4):
            rows = slice(CH * (tp % 2), CH * (tp % 2) + CH)
            late = tp >= 2
            if late:
                own = dnall[slot].astype(F32)[rows]
            else:
                own = (d_ref[...] if slot == 0 else dall[slot - 1]).astype(F32)[rows]
            top = edall[slot, 2 if late else 0].astype(F32)[rows]
            bottom = edall[slot, 3 if late else 1].astype(F32)[rows]
            if late:
                own, top, bottom = own * next_on, top * next_on, bottom * next_on
            moved = (
                jnp.concatenate([own[:, 160:], bottom[:, :160]], axis=1),
                own,
                jnp.concatenate([top[:, 96:], own[:, :480]], axis=1),
            )
            pieces = []
            for one in moved:
                pieces.append(jnp.where(right_end, 0.0, pltpu.roll(one, LANES - 1, 1)))
                pieces.append(one)
                pieces.append(jnp.where(left_end, 0.0, pltpu.roll(one, 1, 1)))
            s9[slot, tp] = jnp.concatenate(pieces, axis=0).astype(BF16)

    side = 1 + 2 * at["k"]
    source = (at["zh"] + side) % 4
    away = {"tm": at["x"], "height": row, "chan": (at["zh"] + 4 - side) % 4 * 4 + at["y"]}
    fz_far = []

    def far_step(n):
        arrived(fz[n])
        ref = fall.at[source, STEPS[n]]
        fz_far.append(send(ref, ref, away))

    arrived(sys)
    smid[0] = sown[...] + sry[0] + sry[1] + sry[2]
    szs = [send(smid.at[0], smid.at[by], shifted(at, zh=by)) for by in (1, 3)]
    far_step(0)
    build(0)
    far_step(1)
    far_step(2)
    arrived(szs)
    szf = send(smid.at[1], srz, shifted(at, zh=1))
    for by in (1, 3, 2):
        arrived(dy[by])
        build(by)

    arrived([szf])
    total = smid[0] + smid[1] + smid[3] + srz[...]
    inv[...] = lax.rsqrt(total * (1.0 / TOTAL) + 1e-06)

    def activation(x, t, block):
        start = pl.multiple_of(block * CH, 8)
        gain = gb_ref[pl.ds(start, CH), 0:1]
        bias = gb_ref[pl.ds(start, CH), 1:2]
        normed = x * inv[t : t + 1] * gain + bias
        sig = 0.5 * jnp.tanh(0.5 * normed) + 0.5
        return normed * sig, sig * (1.0 + normed * (1.0 - sig)) * gain

    arrived(fz_far)

    @pl.loop(0, 2)
    def _(n):
        blocks = [fall[2 * n + j].astype(F32) for j in range(2)]
        for t in range(2):
            pair, slopes = [], []
            for j in range(2):
                x = blocks[j][CH * t : CH * t + CH]
                active, slope = activation(x, t, (2 * n + j) * 4 + at["y"])
                pair.append(active)
                slopes.append(slope * x)
            start = pl.multiple_of(n * 48, 16)
            act[t, pl.ds(start, 48)] = jnp.concatenate(pair, axis=0).astype(BF16)
            sx[t, pl.ds(start, 48)] = jnp.concatenate(slopes, axis=0)

    def weigh(slot, g, n):
        for kt in range(3):
            total = None
            for t in range(2):
                part = lax.dot_general(
                    s9[slot, t + 2 - kt], act[t], (((1,), (1,)), ((), ())), preferred_element_type=F32
                )
                total = part if total is None else total + part
            gc[216 * kt : 216 * kt + 216] = total
        g[n, 0:328] = jnp.concatenate([gc[0:328, 0:64], gc[320:648, 0:64]], axis=1)
        g[n, 328:USED] = jnp.concatenate([gc[160 * m : 160 * m + 168, 64:96] for m in range(4)], axis=1)
        g[n, USED:ROWS] = jnp.zeros((ROWS - USED, 128), F32)

    def core_reduce(bufs):
        other = pl.multiple_of((1 - at["k"]) * 256, 256)
        return send(bufs[0].at[:, pl.ds(other, 256)], bufs[1], shifted(at, k=1))

    def x_reduce(bufs):
        g, gr, h, hb, hr = bufs[:5]
        sends = []
        for by in (2, 1, 3, 0):
            start = (at["x"] + by) % 4 * 64
            value = (
                g[:, pl.ds(pl.multiple_of(at["k"] * 256 + start, 64), 64)]
                + gr[:, pl.ds(pl.multiple_of(start, 64), 64)]
            )
            if by == 0:
                h[...] = value
            else:
                hb[by - 1] = value.astype(BF16)
                sends.append(send(hb.at[by - 1], hr.at[by - 1], shifted(at, x=by)))
        return sends

    def z_reduce(bufs):
        h, hr, zs, zr = bufs[2], bufs[4], bufs[5], bufs[6]
        h[...] = h[...] + hr[0].astype(F32) + hr[1].astype(F32) + hr[2].astype(F32)
        sends = []
        for by in (3, 1, 2):
            zs[by - 1] = h[:, pl.ds(pl.multiple_of((at["zl"] + by) % 4 * 16, 16), 16)]
            sends.append(send(zs.at[by - 1], zr.at[by - 1], shifted(at, zl=by)))
        return sends

    def yz_gather(bufs, base):
        h, zr, sb = bufs[2], bufs[6], bufs[7]
        value = h[:, pl.ds(pl.multiple_of(at["zl"] * 16, 16), 16)] + zr[0] + zr[1] + zr[2]
        sb[...] = (value * (1.0 / math.sqrt(40960))).astype(BF16)
        piece = pl.multiple_of(at["k"] * 256 + at["x"] * 64 + at["zl"] * 16, 16)
        sends = []
        for n in range(2):
            slot = SLOTS[base + n]
            for dz in (3, 2, 1, 0):
                if slot == 0 and dz == 0:
                    ag[0, pl.ds(piece, 16)] = sb[0]
                else:
                    dst = ag.at[base + n, pl.ds(piece, 16)]
                    sends.append(send(sb.at[n], dst, shifted(at, y=-slot, zl=dz)))
        return sends

    def x_gather(base):
        start = pl.multiple_of(at["k"] * 256 + at["x"] * 64, 64)
        ref = ag.at[pl.ds(base, 2), pl.ds(start, 64)]
        return [send(ref, ref, shifted(at, x=by)) for by in (2, 1, 3)]

    def core_gather(base):
        ref = ag.at[pl.ds(base, 2), pl.ds(pl.multiple_of(at["k"] * 256, 256), 256)]
        return send(ref, ref, shifted(at, k=1))

    def unpack(place):
        value = ag[place].astype(F32)
        low, high = value[:328], value[328:USED]
        left = jnp.concatenate([low[:, :64], low[8:, 64:]], axis=0)
        right = jnp.concatenate(
            [high[:, :32], high[8:, 32:64], high[8:, 64:96], high[8:, 96:]], axis=0
        )
        piece = jnp.concatenate([left, right], axis=1).astype(BF16)
        return jnp.dot(piece, perm[SLOTS[place]], preferred_element_type=F32)

    weigh(SLOTS[0], chain_a[0], 0)
    weigh(SLOTS[1], chain_a[0], 1)
    a = core_reduce(chain_a)
    arrived(ws)
    ref = wall.at[pl.ds(1, 3), pl.ds(half, 144)]
    wx = send(ref, ref, shifted(at, k=1))
    weigh(SLOTS[2], chain_b[0], 0)
    weigh(SLOTS[3], chain_b[0], 1)
    b = core_reduce(chain_b)
    arrived([a])
    a = x_reduce(chain_a)
    arrived([wx])
    for tp, (low, high) in enumerate(((192, 288), (96, 288), (0, 192), (0, 96))):
        total = None
        for slot in range(4):
            part = jnp.dot(wall[slot, low:high], s9[slot, tp], preferred_element_type=F32)
            total = part if total is None else total + part
        if tp == 0:
            p[0] = total
        elif tp == 1:
            p[0] += total[:96]
            p[1] = total[96:]
        elif tp == 2:
            p[0] += total[:96]
            p[1] += total[96:]
        else:
            p[1] += total

    arrived([b])
    b = x_reduce(chain_b)
    zsends = []
    for by in (2, 1, 3, 0):
        start = pl.multiple_of((at["zh"] + by) % 4 * CH, 8)
        value = jnp.concatenate([p[0, pl.ds(start, CH)], p[1, pl.ds(start, CH)]], axis=0)
        if by == 0:
            q[...] = value
        else:
            qb[by - 1] = value.astype(BF16)
            zsends.append(send(qb.at[by - 1], rz.at[by - 1], shifted(at, zh=by)))
    for t in range(2):
        dsend[t : t + 1] = jnp.sum(p[t] * sx[t], axis=0, keepdims=True)
    dys = [send(dsend, dry.at[by - 1], shifted(at, y=by)) for by in (2, 1, 3)]
    arrived(a)
    a = z_reduce(chain_a)
    arrived(b)
    b = z_reduce(chain_b)
    arrived(dys)
    dmid[...] = dsend[...] + dry[0] + dry[1] + dry[2]
    dzs = [send(dmid, drz.at[by - 1], shifted(at, zh=by)) for by in (2, 1, 3)]
    arrived(a)
    a = yz_gather(chain_a, 0)
    arrived(b)
    b = yz_gather(chain_b, 2)
    arrived(a)
    a = x_gather(0)
    arrived(b)
    b = x_gather(2)
    arrived(a)
    a = core_gather(0)
    arrived(b)
    b = core_gather(2)

    arrived(zsends + dzs)
    grad = q[...] + rz[0].astype(F32) + rz[1].astype(F32) + rz[2].astype(F32)
    dots = dmid[...] + drz[0] + drz[1] + drz[2]
    mine_x = f_ref[...].astype(F32)
    ct = d_ref[...].astype(F32)
    outs = []
    for t in range(2):
        rows = slice(CH * t, CH * t + CH)
        x = mine_x[rows]
        _, slope = activation(x, t, at["zh"] * 4 + at["y"])
        up = grad[rows] * slope
        r = inv[t : t + 1]
        back = r * up - x * (r * r * r * dots[t : t + 1] * (1.0 / TOTAL))
        outs.append(ct[rows] + back)
    od_ref[...] = jnp.concatenate(outs, axis=0).astype(BF16)

    arrived([a, b])
    og_ref[...] = (unpack(0) + unpack(1) + unpack(2) + unpack(3)).astype(BF16)
    for copy in started:
        copy.wait_send()
    for copy, goes, _ in halo:
        pl.when(goes)(copy.wait_send)


def chain_buffers():
    return [
        pltpu.VMEM((2, ROWS, 128), F32),
        pltpu.VMEM((2, 256, 128), F32),
        pltpu.VMEM((2, 64, 128), F32),
        pltpu.VMEM((3, 2, 64, 128), BF16),
        pltpu.VMEM((3, 2, 64, 128), BF16),
        pltpu.VMEM((3, 2, 16, 128), F32),
        pltpu.VMEM((3, 2, 16, 128), F32),
        pltpu.VMEM((2, 16, 128), BF16),
    ]


def on_device(features, cotangent, conv_weight, norm_gain, norm_bias):
    chans, frames, rows, cols = features.shape
    f = jnp.transpose(features, (1, 0, 2, 3)).reshape(frames * chans, rows * cols)
    d = jnp.transpose(cotangent, (1, 0, 2, 3)).reshape(frames * chans, rows * cols)
    vmem = pl.BlockSpec(memory_space=pltpu.VMEM)
    sums = pltpu.VMEM((2, LANES), F32)
    sums3 = pltpu.VMEM((3, 2, LANES), F32)
    cells = pltpu.VMEM((3, 48, LANES), BF16)
    grads, out = pl.pallas_call(
        kernel,
        name="unit_backward",
        out_shape=(
            jax.ShapeDtypeStruct((648, TOTAL), BF16),
            jax.ShapeDtypeStruct((48, LANES), BF16),
        ),
        in_specs=[vmem, vmem, pl.BlockSpec(memory_space=pl.ANY), vmem, vmem],
        out_specs=(vmem, vmem),
        scratch_shapes=[
            pltpu.VMEM((CH, 27, TOTAL), BF16),
            pltpu.VMEM((3, CH * 32, 128), F32),
            pltpu.VMEM((3, TOTAL, 9 * CH), F32),
            pltpu.VMEM((3, 288, 9 * CH), BF16),
            pltpu.VMEM((4, 288, 9 * CH), BF16),
            pltpu.VMEM((TOTAL, 8), F32),
            cells,
            pltpu.VMEM((4, 48, LANES), BF16),
            pltpu.VMEM((4, 4, 48, 256), BF16),
            pltpu.VMEM((4, 48, LANES), BF16),
            pltpu.VMEM((4, 4, 216, LANES), BF16),
            pltpu.VMEM((2, 96, LANES), F32),
            pltpu.VMEM((48, LANES), F32),
            cells,
            cells,
            pltpu.VMEM((2, 96, LANES), BF16),
            pltpu.VMEM((2, 96, LANES), F32),
            sums,
            sums,
            pltpu.VMEM((4, 2, LANES), F32),
            sums3,
            sums,
            sums,
            sums,
            sums3,
            sums3,
            pltpu.VMEM((648, 96), F32),
            pltpu.VMEM((4, 96, TOTAL), BF16),
            pltpu.VMEM((4, ROWS, 128), BF16),
            chain_buffers(),
            chain_buffers(),
            pltpu.SemaphoreType.DMA,
            pltpu.SemaphoreType.DMA((COPIES,)),
            pltpu.SemaphoreType.DMA((COPIES,)),
        ],
        compiler_params=pltpu.CompilerParams(
            collective_id=0, has_side_effects=True, vmem_limit_bytes=40 << 20
        ),
    )(f, d, conv_weight, norm_gain.reshape(1, TOTAL), norm_bias.reshape(1, TOTAL))
    result = jnp.transpose(out.reshape(frames, chans, rows, cols), (1, 0, 2, 3))
    weight_grad = jnp.transpose(grads.reshape(27, chans, TOTAL), (1, 0, 2)).astype(F32)
    return result, weight_grad


def solution(mesh):
    return jax.shard_map(
        on_device,
        mesh=mesh,
        in_specs=(
            P("chan", "tm", "height", None),
            P("chan", "tm", "height", None),
            P("chan", None, None),
            P(),
            P(),
        ),
        out_specs=(P("chan", "tm", "height", None), P("chan", None, None)),
        check_vma=False,
    )
```

```python
import functools
import math

import jax
import jax.numpy as jnp
from jax import lax
from jax.experimental import pallas as pl
from jax.experimental.pallas import tpu as pltpu
from jax.sharding import PartitionSpec as P

MESH = pl.DeviceIdType.MESH
SIZES = {"x": 4, "zl": 4, "k": 2, "zh": 4, "y": 4}
CH = 24
TOTAL = 384
LANES = 640
F32 = jnp.float32
BF16 = jnp.bfloat16


def coords():
    t = lax.axis_index("tm")
    h = lax.axis_index("height")
    c = lax.axis_index("chan")
    return {"x": t, "zl": h // 2, "k": h % 2, "zh": c // 4, "y": c % 4}


def shifted(at, **offsets):
    at = dict(at)
    for name, by in offsets.items():
        at[name] = (at[name] + (by % SIZES[name])) % SIZES[name]
    return {"tm": at["x"], "height": at["zl"] * 2 + at["k"], "chan": at["zh"] * 4 + at["y"]}


def neighbour(at, dx, dh):
    t = (at["x"] + (dx % 4)) % 4
    h = (at["zl"] * 2 + at["k"] + (dh % 8)) % 8
    return {"tm": t, "height": h, "chan": at["zh"] * 4 + at["y"]}


HALO = ((-1, 0), (0, 1), (0, -1), (-1, 1), (-1, -1))
COPIES = 96
STEPS = tuple(slice(16 * n, 16 * n + 16) for n in range(3))
SLOTS = (0, 1, 3, 2)
ROWS = 512
USED = 496


def kernel(
    f_ref, d_ref, raw_hbm, gain_hbm, bias_hbm, og_ref, od_ref,
    raw, gain_ref, bias_ref, tall, slabs, wall, gb_ref, dall, dnall, edall, fall, s9, p, q, qb, rz, act, sx, inv,
    sown, smid, sry, srz, dsend, dmid, dry, drz, gc, perm, ag, chain_a, chain_b, lsem, ssem, rsem,
):
    at = coords()
    count = [0]
    started = []

    def send(src, dst, target):
        i = count[0]
        count[0] += 1
        copy = pltpu.make_async_remote_copy(
            src_ref=src, dst_ref=dst, send_sem=ssem.at[i], recv_sem=rsem.at[i],
            device_id=target, device_id_type=MESH,
        )
        copy.start()
        started.append(copy)
        return copy

    def arrived(copies):
        for copy in copies:
            copy.wait_recv()

    loads = [
        pltpu.make_async_copy(src, dst, lsem.at[n])
        for n, (src, dst) in enumerate(((gain_hbm, gain_ref), (bias_hbm, bias_ref), (raw_hbm, raw)))
    ]
    for copy in loads:
        copy.start()
    edall[0] = jnp.zeros((4, 48, 256), BF16)
    barrier = pltpu.get_barrier_semaphore()
    greeted = [shifted(at, zh=1), shifted(at, zh=3)]
    greeted += [neighbour(at, -dx, -dh) for dx, dh in HALO]
    greeted += [shifted(at, x=by) for by in (1, 2, 3)]
    greeted += [shifted(at, y=dy, zl=dz) for dy in range(4) for dz in range(4) if dy or dz]
    greeted.append(shifted(at, k=1))
    for one in greeted:
        pl.semaphore_signal(barrier, inc=1, device_id=one, device_id_type=MESH)

    fall[at["zh"]] = f_ref[...]
    squares = f_ref[...].astype(F32)
    squares = squares * squares
    for t in range(2):
        sown[t : t + 1] = jnp.sum(squares[CH * t : CH * t + CH], axis=0, keepdims=True)
    loads[0].wait()
    loads[1].wait()
    pair = [ref[...].reshape(1, TOTAL) for ref in (gain_ref, bias_ref)]
    both = jnp.concatenate(pair + [jnp.zeros((6, TOTAL), F32)], axis=0)
    gb_ref[...] = both.T

    loads[2].wait()
    for kt in range(3):
        tall[kt] = raw[216 * kt : 216 * kt + 216].astype(F32).T

    def slab(by):
        y = (at["y"] + by) % 4
        groups = [
            tall[kt, pl.ds(pl.multiple_of(96 * zh + y * CH, 8), CH)] for kt in range(3) for zh in range(4)
        ]
        return jnp.concatenate(groups, axis=0).astype(BF16)

    wall[0] = slab(0)
    for by in (1, 2, 3):
        slabs[by - 1] = slab(by)
    r = lax.broadcasted_iota(jnp.int32, (96, TOTAL), 0)
    lane = lax.broadcasted_iota(jnp.int32, (96, TOTAL), 1)
    group = (r >= 24).astype(jnp.int32) + (r >= 48).astype(jnp.int32) + (r >= 72).astype(jnp.int32)
    for s in range(4):
        target = r + 72 * group + CH * ((at["y"] + s) % 4)
        perm[s] = jnp.where(lane == target, 1.0, 0.0).astype(BF16)

    pl.semaphore_wait(barrier, len(greeted))

    row = at["zl"] * 2 + at["k"]
    below, above = row < 7, row > 0
    frame = send(d_ref, dnall.at[0], neighbour(at, -1, 0))
    halo = []
    for n, (dx, dh) in enumerate(HALO[1:]):
        i = count[0]
        count[0] += 1
        copy = pltpu.make_async_remote_copy(
            src_ref=d_ref.at[:, pl.ds(384 if dh == 1 else 0, 256)], dst_ref=edall.at[0, n],
            send_sem=ssem.at[i], recv_sem=rsem.at[i],
            device_id=neighbour(at, dx, dh), device_id_type=MESH,
        )
        goes, comes = (below, above) if dh == 1 else (above, below)
        pl.when(goes)(copy.start)
        halo.append((copy, goes, comes))
    fz = [
        [send(f_ref.at[rows], fall.at[at["zh"], rows], shifted(at, zh=by)) for by in (1, 3)] for rows in STEPS
    ]
    sys = [send(sown, sry.at[by - 1], shifted(at, y=by)) for by in (2, 1, 3)]
    dy = {by: [send(d_ref, dall.at[by - 1], shifted(at, y=by))] for by in (2, 1, 3)}

    half = pl.multiple_of(at["k"] * 144, 16)
    ws = [
        send(slabs.at[by - 1, pl.ds(half, 144)], wall.at[by, pl.ds(half, 144)], shifted(at, y=by))
        for by in (2, 1, 3)
    ]

    arrived([frame])
    for by in (2, 1, 3):
        dy[by].append(send(dnall.at[0], dnall.at[by], shifted(at, y=by)))
    for copy, _, comes in halo:
        pl.when(comes)(copy.wait_recv)
    for by in (2, 1, 3):
        dy[by].append(send(edall.at[0], edall.at[by], shifted(at, y=by)))
    column = lax.broadcasted_iota(jnp.int32, (CH, LANES), 1) % 160
    left_end, right_end = column == 0, column == 159
    next_on = jnp.where(at["x"] < 3, 1.0, 0.0).astype(F32)

    def build(slot):
        for tp in range(4):
            rows = slice(CH * (tp % 2), CH * (tp % 2) + CH)
            late = tp >= 2
            if late:
                own = dnall[slot].astype(F32)[rows]
            else:
                own = (d_ref[...] if slot == 0 else dall[slot - 1]).astype(F32)[rows]
            top = edall[slot, 2 if late else 0].astype(F32)[rows]
            bottom = edall[slot, 3 if late else 1].astype(F32)[rows]
            if late:
                own, top, bottom = own * next_on, top * next_on, bottom * next_on
            moved = (
                jnp.concatenate([own[:, 160:], bottom[:, :160]], axis=1),
                own,
                jnp.concatenate([top[:, 96:], own[:, :480]], axis=1),
            )
            pieces = []
            for one in moved:
                pieces.append(jnp.where(right_end, 0.0, pltpu.roll(one, LANES - 1, 1)))
                pieces.append(one)
                pieces.append(jnp.where(left_end, 0.0, pltpu.roll(one, 1, 1)))
            s9[slot, tp] = jnp.concatenate(pieces, axis=0).astype(BF16)

    side = 1 + 2 * at["k"]
    source = (at["zh"] + side) % 4
    away = {"tm": at["x"], "height": row, "chan": (at["zh"] + 4 - side) % 4 * 4 + at["y"]}
    fz_far = []

    def far_step(n):
        arrived(fz[n])
        ref = fall.at[source, STEPS[n]]
        fz_far.append(send(ref, ref, away))

    arrived(sys)
    smid[0] = sown[...] + sry[0] + sry[1] + sry[2]
    szs = [send(smid.at[0], smid.at[by], shifted(at, zh=by)) for by in (1, 3)]
    far_step(0)
    build(0)
    far_step(1)
    far_step(2)
    arrived(ws)
    ref = wall.at[pl.ds(1, 3), pl.ds(half, 144)]
    wx = send(ref, ref, shifted(at, k=1))
    arrived(szs)
    szf = send(smid.at[1], srz, shifted(at, zh=1))
    for by in (1, 3, 2):
        arrived(dy[by])
        build(by)

    arrived([wx])
    for tp, (low, high) in enumerate(((192, 288), (96, 288), (0, 192), (0, 96))):
        total = None
        for slot in range(4):
            part = jnp.dot(wall[slot, low:high], s9[slot, tp], preferred_element_type=F32)
            total = part if total is None else total + part
        if tp == 0:
            p[0] = total
        elif tp == 1:
            p[0] += total[:96]
            p[1] = total[96:]
        elif tp == 2:
            p[0] += total[:96]
            p[1] += total[96:]
        else:
            p[1] += total

    zsends = []
    for by in (2, 1, 3, 0):
        start = pl.multiple_of((at["zh"] + by) % 4 * CH, 8)
        value = jnp.concatenate([p[0, pl.ds(start, CH)], p[1, pl.ds(start, CH)]], axis=0)
        if by == 0:
            q[...] = value
        else:
            qb[by - 1] = value.astype(BF16)
            zsends.append(send(qb.at[by - 1], rz.at[by - 1], shifted(at, zh=by)))
    arrived([szf])
    total = smid[0] + smid[1] + smid[3] + srz[...]
    inv[...] = lax.rsqrt(total * (1.0 / TOTAL) + 1e-06)

    def activation(x, t, block):
        start = pl.multiple_of(block * CH, 8)
        gain = gb_ref[pl.ds(start, CH), 0:1]
        bias = gb_ref[pl.ds(start, CH), 1:2]
        normed = x * inv[t : t + 1] * gain + bias
        sig = 0.5 * jnp.tanh(0.5 * normed) + 0.5
        return normed * sig, sig * (1.0 + normed * (1.0 - sig)) * gain

    arrived(fz_far)

    @pl.loop(0, 2)
    def _(n):
        blocks = [fall[2 * n + j].astype(F32) for j in range(2)]
        for t in range(2):
            pair, slopes = [], []
            for j in range(2):
                x = blocks[j][CH * t : CH * t + CH]
                active, slope = activation(x, t, (2 * n + j) * 4 + at["y"])
                pair.append(active)
                slopes.append(slope * x)
            start = pl.multiple_of(n * 48, 16)
            act[t, pl.ds(start, 48)] = jnp.concatenate(pair, axis=0).astype(BF16)
            sx[t, pl.ds(start, 48)] = jnp.concatenate(slopes, axis=0)

    def weigh(slot, g, n):
        for kt in range(3):
            total = None
            for t in range(2):
                part = lax.dot_general(
                    s9[slot, t + 2 - kt], act[t], (((1,), (1,)), ((), ())), preferred_element_type=F32
                )
                total = part if total is None else total + part
            gc[216 * kt : 216 * kt + 216] = total
        g[n, 0:328] = jnp.concatenate([gc[0:328, 0:64], gc[320:648, 0:64]], axis=1)
        g[n, 328:USED] = jnp.concatenate([gc[160 * m : 160 * m + 168, 64:96] for m in range(4)], axis=1)
        g[n, USED:ROWS] = jnp.zeros((ROWS - USED, 128), F32)

    def core_reduce(bufs):
        other = pl.multiple_of((1 - at["k"]) * 256, 256)
        return send(bufs[0].at[:, pl.ds(other, 256)], bufs[1], shifted(at, k=1))

    def x_reduce(bufs):
        g, gr, h, hb, hr = bufs[:5]
        sends = []
        for by in (2, 1, 3, 0):
            start = (at["x"] + by) % 4 * 64
            value = (
                g[:, pl.ds(pl.multiple_of(at["k"] * 256 + start, 64), 64)]
                + gr[:, pl.ds(pl.multiple_of(start, 64), 64)]
            )
            if by == 0:
                h[...] = value
            else:
                hb[by - 1] = value.astype(BF16)
                sends.append(send(hb.at[by - 1], hr.at[by - 1], shifted(at, x=by)))
        return sends

    def z_reduce(bufs):
        h, hr, zs, zr = bufs[2], bufs[4], bufs[5], bufs[6]
        h[...] = h[...] + hr[0].astype(F32) + hr[1].astype(F32) + hr[2].astype(F32)
        sends = []
        for by in (3, 1, 2):
            zs[by - 1] = h[:, pl.ds(pl.multiple_of((at["zl"] + by) % 4 * 16, 16), 16)]
            sends.append(send(zs.at[by - 1], zr.at[by - 1], shifted(at, zl=by)))
        return sends

    def yz_gather(bufs, base):
        h, zr, sb = bufs[2], bufs[6], bufs[7]
        value = h[:, pl.ds(pl.multiple_of(at["zl"] * 16, 16), 16)] + zr[0] + zr[1] + zr[2]
        sb[...] = (value * (1.0 / math.sqrt(40960))).astype(BF16)
        piece = pl.multiple_of(at["k"] * 256 + at["x"] * 64 + at["zl"] * 16, 16)
        sends = []
        for n in range(2):
            slot = SLOTS[base + n]
            for dz in (3, 2, 1, 0):
                if slot == 0 and dz == 0:
                    ag[0, pl.ds(piece, 16)] = sb[0]
                else:
                    dst = ag.at[base + n, pl.ds(piece, 16)]
                    sends.append(send(sb.at[n], dst, shifted(at, y=-slot, zl=dz)))
        return sends

    def x_gather(base):
        start = pl.multiple_of(at["k"] * 256 + at["x"] * 64, 64)
        ref = ag.at[pl.ds(base, 2), pl.ds(start, 64)]
        return [send(ref, ref, shifted(at, x=by)) for by in (2, 1, 3)]

    def core_gather(base):
        ref = ag.at[pl.ds(base, 2), pl.ds(pl.multiple_of(at["k"] * 256, 256), 256)]
        return send(ref, ref, shifted(at, k=1))

    def unpack(place):
        value = ag[place].astype(F32)
        low, high = value[:328], value[328:USED]
        left = jnp.concatenate([low[:, :64], low[8:, 64:]], axis=0)
        right = jnp.concatenate(
            [high[:, :32], high[8:, 32:64], high[8:, 64:96], high[8:, 96:]], axis=0
        )
        piece = jnp.concatenate([left, right], axis=1).astype(BF16)
        return jnp.dot(piece, perm[SLOTS[place]], preferred_element_type=F32)

    for t in range(2):
        dsend[t : t + 1] = jnp.sum(p[t] * sx[t], axis=0, keepdims=True)
    dys = [send(dsend, dry.at[by - 1], shifted(at, y=by)) for by in (2, 1, 3)]
    weigh(SLOTS[0], chain_a[0], 0)
    weigh(SLOTS[1], chain_a[0], 1)
    a = core_reduce(chain_a)
    weigh(SLOTS[2], chain_b[0], 0)
    weigh(SLOTS[3], chain_b[0], 1)
    b = core_reduce(chain_b)
    arrived([a])
    a = x_reduce(chain_a)
    arrived(dys)
    dmid[...] = dsend[...] + dry[0] + dry[1] + dry[2]
    dzs = [send(dmid, drz.at[by - 1], shifted(at, zh=by)) for by in (2, 1, 3)]
    arrived([b])
    b = x_reduce(chain_b)
    arrived(a)
    a = z_reduce(chain_a)
    arrived(b)
    b = z_reduce(chain_b)
    arrived(a)
    a = yz_gather(chain_a, 0)
    arrived(b)
    b = yz_gather(chain_b, 2)
    arrived(a)
    a = x_gather(0)
    arrived(b)
    b = x_gather(2)
    arrived(a)
    a = core_gather(0)
    arrived(b)
    b = core_gather(2)

    arrived(zsends + dzs)
    grad = q[...] + rz[0].astype(F32) + rz[1].astype(F32) + rz[2].astype(F32)
    dots = dmid[...] + drz[0] + drz[1] + drz[2]
    mine_x = f_ref[...].astype(F32)
    ct = d_ref[...].astype(F32)
    outs = []
    for t in range(2):
        rows = slice(CH * t, CH * t + CH)
        x = mine_x[rows]
        _, slope = activation(x, t, at["zh"] * 4 + at["y"])
        up = grad[rows] * slope
        r = inv[t : t + 1]
        back = r * up - x * (r * r * r * dots[t : t + 1] * (1.0 / TOTAL))
        outs.append(ct[rows] + back)
    od_ref[...] = jnp.concatenate(outs, axis=0).astype(BF16)

    arrived([a, b])
    og_ref[...] = (unpack(0) + unpack(1) + unpack(2) + unpack(3)).astype(BF16)
    for copy in started:
        copy.wait_send()
    for copy, goes, _ in halo:
        pl.when(goes)(copy.wait_send)


def chain_buffers():
    return [
        pltpu.VMEM((2, ROWS, 128), F32),
        pltpu.VMEM((2, 256, 128), F32),
        pltpu.VMEM((2, 64, 128), F32),
        pltpu.VMEM((3, 2, 64, 128), BF16),
        pltpu.VMEM((3, 2, 64, 128), BF16),
        pltpu.VMEM((3, 2, 16, 128), F32),
        pltpu.VMEM((3, 2, 16, 128), F32),
        pltpu.VMEM((2, 16, 128), BF16),
    ]


def on_device(features, cotangent, conv_weight, norm_gain, norm_bias):
    chans, frames, rows, cols = features.shape
    f = jnp.transpose(features, (1, 0, 2, 3)).reshape(frames * chans, rows * cols)
    d = jnp.transpose(cotangent, (1, 0, 2, 3)).reshape(frames * chans, rows * cols)
    vmem = pl.BlockSpec(memory_space=pltpu.VMEM)
    hbm = pl.BlockSpec(memory_space=pl.ANY)
    w = jnp.transpose(conv_weight, (1, 0, 2)).reshape(27 * chans, TOTAL)
    sums = pltpu.VMEM((2, LANES), F32)
    sums3 = pltpu.VMEM((3, 2, LANES), F32)
    cells = pltpu.VMEM((3, 48, LANES), BF16)
    grads, out = pl.pallas_call(
        kernel,
        name="unit_backward",
        out_shape=(
            jax.ShapeDtypeStruct((648, TOTAL), BF16),
            jax.ShapeDtypeStruct((48, LANES), BF16),
        ),
        in_specs=[vmem, vmem, hbm, hbm, hbm],
        out_specs=(vmem, vmem),
        scratch_shapes=[
            pltpu.VMEM((27 * CH, TOTAL), BF16),
            pltpu.VMEM((TOTAL,), F32),
            pltpu.VMEM((TOTAL,), F32),
            pltpu.VMEM((3, TOTAL, 9 * CH), F32),
            pltpu.VMEM((3, 288, 9 * CH), BF16),
            pltpu.VMEM((4, 288, 9 * CH), BF16),
            pltpu.VMEM((TOTAL, 8), F32),
            cells,
            pltpu.VMEM((4, 48, LANES), BF16),
            pltpu.VMEM((4, 4, 48, 256), BF16),
            pltpu.VMEM((4, 48, LANES), BF16),
            pltpu.VMEM((4, 4, 216, LANES), BF16),
            pltpu.VMEM((2, 96, LANES), F32),
            pltpu.VMEM((48, LANES), F32),
            cells,
            cells,
            pltpu.VMEM((2, 96, LANES), BF16),
            pltpu.VMEM((2, 96, LANES), F32),
            sums,
            sums,
            pltpu.VMEM((4, 2, LANES), F32),
            sums3,
            sums,
            sums,
            sums,
            sums3,
            sums3,
            pltpu.VMEM((648, 96), F32),
            pltpu.VMEM((4, 96, TOTAL), BF16),
            pltpu.VMEM((4, ROWS, 128), BF16),
            chain_buffers(),
            chain_buffers(),
            pltpu.SemaphoreType.DMA((3,)),
            pltpu.SemaphoreType.DMA((COPIES,)),
            pltpu.SemaphoreType.DMA((COPIES,)),
        ],
        compiler_params=pltpu.CompilerParams(
            collective_id=0, has_side_effects=True, vmem_limit_bytes=40 << 20
        ),
    )(f, d, w, norm_gain, norm_bias)
    result = jnp.transpose(out.reshape(frames, chans, rows, cols), (1, 0, 2, 3))
    weight_grad = jnp.transpose(grads.reshape(27, chans, TOTAL), (1, 0, 2)).astype(F32)
    return result, weight_grad


def solution(mesh):
    return jax.shard_map(
        on_device,
        mesh=mesh,
        in_specs=(
            P("chan", "tm", "height", None),
            P("chan", "tm", "height", None),
            P("chan", None, None),
            P(),
            P(),
        ),
        out_specs=(P("chan", "tm", "height", None), P("chan", None, None)),
        check_vma=False,
    )
```

```python
import functools
import math

import jax
import jax.numpy as jnp
from jax import lax
from jax.experimental import pallas as pl
from jax.experimental.pallas import tpu as pltpu
from jax.sharding import PartitionSpec as P

MESH = pl.DeviceIdType.MESH
SIZES = {"x": 4, "zl": 4, "k": 2, "zh": 4, "y": 4}
CH = 24
TOTAL = 384
LANES = 640
F32 = jnp.float32
BF16 = jnp.bfloat16


def coords():
    t = lax.axis_index("tm")
    h = lax.axis_index("height")
    c = lax.axis_index("chan")
    return {"x": t, "zl": h // 2, "k": h % 2, "zh": c // 4, "y": c % 4}


def shifted(at, **offsets):
    at = dict(at)
    for name, by in offsets.items():
        at[name] = (at[name] + (by % SIZES[name])) % SIZES[name]
    return {"tm": at["x"], "height": at["zl"] * 2 + at["k"], "chan": at["zh"] * 4 + at["y"]}


def neighbour(at, dx, dh):
    t = (at["x"] + (dx % 4)) % 4
    h = (at["zl"] * 2 + at["k"] + (dh % 8)) % 8
    return {"tm": t, "height": h, "chan": at["zh"] * 4 + at["y"]}


HALO = ((-1, 0), (0, 1), (0, -1), (-1, 1), (-1, -1))
COPIES = 96
STEPS = tuple(slice(16 * n, 16 * n + 16) for n in range(3))
SLOTS = (0, 1, 3, 2)
ROWS = 512
USED = 496


def kernel(
    fd_ref, raw_hbm, gain_hbm, bias_hbm, og_ref, od_ref,
    raw, gain_ref, bias_ref, tall, slabs, wall, gb_ref, dall, dnall, edall, fall, s9, p, q, qb, rz, act, sx, inv,
    sown, smid, sry, srz, dsend, dmid, dry, drz, gc, perm, wgrad, ag, chain_a, chain_b, lsem, ssem, rsem,
):
    f_ref, d_ref = fd_ref.at[0:48], fd_ref.at[48:96]
    at = coords()
    count = [0]
    started = []

    def send(src, dst, target):
        i = count[0]
        count[0] += 1
        copy = pltpu.make_async_remote_copy(
            src_ref=src, dst_ref=dst, send_sem=ssem.at[i], recv_sem=rsem.at[i],
            device_id=target, device_id_type=MESH,
        )
        copy.start()
        started.append(copy)
        return copy

    def arrived(copies):
        for copy in copies:
            copy.wait_recv()

    loads = [
        pltpu.make_async_copy(src, dst, lsem.at[n])
        for n, (src, dst) in enumerate(((gain_hbm, gain_ref), (bias_hbm, bias_ref), (raw_hbm, raw)))
    ]
    for copy in loads:
        copy.start()
    edall[0] = jnp.zeros((4, 48, 256), BF16)
    barrier = pltpu.get_barrier_semaphore()
    greeted = [shifted(at, zh=1), shifted(at, zh=3)]
    greeted += [neighbour(at, -dx, -dh) for dx, dh in HALO]
    greeted += [shifted(at, x=by) for by in (1, 2, 3)]
    greeted += [shifted(at, y=dy, zl=dz) for dy in range(4) for dz in range(4) if dy or dz]
    greeted.append(shifted(at, k=1))
    for one in greeted:
        pl.semaphore_signal(barrier, inc=1, device_id=one, device_id_type=MESH)

    fall[at["zh"]] = f_ref[...]
    squares = f_ref[...].astype(F32)
    squares = squares * squares
    for t in range(2):
        sown[t : t + 1] = jnp.sum(squares[CH * t : CH * t + CH], axis=0, keepdims=True)
    pl.semaphore_wait(barrier, len(greeted))

    row = at["zl"] * 2 + at["k"]
    below, above = row < 7, row > 0
    frame = send(d_ref, dnall.at[0], neighbour(at, -1, 0))
    halo = []
    for n, (dx, dh) in enumerate(HALO[1:]):
        i = count[0]
        count[0] += 1
        copy = pltpu.make_async_remote_copy(
            src_ref=d_ref.at[:, pl.ds(384 if dh == 1 else 0, 256)], dst_ref=edall.at[0, n],
            send_sem=ssem.at[i], recv_sem=rsem.at[i],
            device_id=neighbour(at, dx, dh), device_id_type=MESH,
        )
        goes, comes = (below, above) if dh == 1 else (above, below)
        pl.when(goes)(copy.start)
        halo.append((copy, goes, comes))
    fz = [
        [send(f_ref.at[rows], fall.at[at["zh"], rows], shifted(at, zh=by)) for by in (1, 3)] for rows in STEPS
    ]
    sys = [send(sown, sry.at[by - 1], shifted(at, y=by)) for by in (2, 1, 3)]
    dy = {by: [send(d_ref, dall.at[by - 1], shifted(at, y=by))] for by in (1, 3, 2)}

    loads[2].wait()
    for kt in range(3):
        tall[kt] = raw[216 * kt : 216 * kt + 216].astype(F32).T

    def slab(by):
        y = (at["y"] + by) % 4
        groups = [
            tall[kt, pl.ds(pl.multiple_of(96 * zh + y * CH, 8), CH)] for kt in range(3) for zh in range(4)
        ]
        return jnp.concatenate(groups, axis=0).astype(BF16)

    wall[0] = slab(0)
    for by in (1, 2, 3):
        slabs[by - 1] = slab(by)
    half = pl.multiple_of(at["k"] * 144, 16)
    ws = [
        send(slabs.at[by - 1, pl.ds(half, 144)], wall.at[by, pl.ds(half, 144)], shifted(at, y=by))
        for by in (2, 1, 3)
    ]

    arrived([frame])
    for by in (1, 3, 2):
        dy[by].append(send(dnall.at[0], dnall.at[by], shifted(at, y=by)))
    for copy, _, comes in halo:
        pl.when(comes)(copy.wait_recv)
    for by in (1, 3, 2):
        dy[by].append(send(edall.at[0], edall.at[by], shifted(at, y=by)))
    column = lax.broadcasted_iota(jnp.int32, (CH, LANES), 1) % 160
    left_end, right_end = column == 0, column == 159
    next_on = jnp.where(at["x"] < 3, 1.0, 0.0).astype(F32)

    def build(slot):
        for tp in range(4):
            rows = slice(CH * (tp % 2), CH * (tp % 2) + CH)
            late = tp >= 2
            if late:
                own = dnall[slot].astype(F32)[rows]
            else:
                own = (d_ref[...] if slot == 0 else dall[slot - 1]).astype(F32)[rows]
            top = edall[slot, 2 if late else 0].astype(F32)[rows]
            bottom = edall[slot, 3 if late else 1].astype(F32)[rows]
            if late:
                own, top, bottom = own * next_on, top * next_on, bottom * next_on
            moved = (
                jnp.concatenate([own[:, 160:], bottom[:, :160]], axis=1),
                own,
                jnp.concatenate([top[:, 96:], own[:, :480]], axis=1),
            )
            pieces = []
            for one in moved:
                pieces.append(jnp.where(right_end, 0.0, pltpu.roll(one, LANES - 1, 1)))
                pieces.append(one)
                pieces.append(jnp.where(left_end, 0.0, pltpu.roll(one, 1, 1)))
            s9[slot, tp] = jnp.concatenate(pieces, axis=0).astype(BF16)

    def dgrad(slot):
        for tp, (low, high) in enumerate(((192, 288), (96, 288), (0, 192), (0, 96))):
            part = jnp.dot(wall[slot, low:high], s9[slot, tp], preferred_element_type=F32)
            for n in range((high - low) // 96):
                t = n if high - low > 96 else tp // 3
                piece = part[96 * n : 96 * n + 96]
                if slot == 0 and (tp == 0 or (tp == 1 and t == 1)):
                    p[t] = piece
                else:
                    p[t] += piece

    side = 1 + 2 * at["k"]
    source = (at["zh"] + side) % 4
    away = {"tm": at["x"], "height": row, "chan": (at["zh"] + 4 - side) % 4 * 4 + at["y"]}
    fz_far = []

    def far_step(n):
        arrived(fz[n])
        ref = fall.at[source, STEPS[n]]
        fz_far.append(send(ref, ref, away))

    arrived(sys)
    smid[0] = sown[...] + sry[0] + sry[1] + sry[2]
    szs = [send(smid.at[0], smid.at[by], shifted(at, zh=by)) for by in (1, 3)]
    far_step(0)
    build(0)
    far_step(1)
    dgrad(0)
    far_step(2)
    arrived(ws)
    ref = wall.at[pl.ds(1, 3), pl.ds(half, 144)]
    wx = send(ref, ref, shifted(at, k=1))
    arrived(szs)
    szf = send(smid.at[1], srz, shifted(at, zh=1))
    loads[0].wait()
    loads[1].wait()
    pair = [ref[...].reshape(1, TOTAL) for ref in (gain_ref, bias_ref)]
    both = jnp.concatenate(pair + [jnp.zeros((6, TOTAL), F32)], axis=0)
    gb_ref[...] = both.T

    r = lax.broadcasted_iota(jnp.int32, (96, TOTAL), 0)
    lane = lax.broadcasted_iota(jnp.int32, (96, TOTAL), 1)
    group = (r >= 24).astype(jnp.int32) + (r >= 48).astype(jnp.int32) + (r >= 72).astype(jnp.int32)
    for s in range(4):
        target = r + 72 * group + CH * ((at["y"] + s) % 4)
        perm[s] = jnp.where(lane == target, 1.0, 0.0).astype(BF16)

    arrived(dy[1])
    build(1)
    arrived([wx])
    dgrad(1)
    arrived(dy[3])
    build(3)
    dgrad(3)
    arrived([szf])
    total = smid[0] + smid[1] + smid[3] + srz[...]
    inv[...] = lax.rsqrt(total * (1.0 / TOTAL) + 1e-06)

    def activation(x, t, block):
        start = pl.multiple_of(block * CH, 8)
        gain = gb_ref[pl.ds(start, CH), 0:1]
        bias = gb_ref[pl.ds(start, CH), 1:2]
        normed = x * inv[t : t + 1] * gain + bias
        sig = 0.5 * jnp.tanh(0.5 * normed) + 0.5
        return normed * sig, sig * (1.0 + normed * (1.0 - sig)) * gain

    arrived(fz_far)

    @pl.loop(0, 2)
    def _(n):
        blocks = [fall[2 * n + j].astype(F32) for j in range(2)]
        for t in range(2):
            pair, slopes = [], []
            for j in range(2):
                x = blocks[j][CH * t : CH * t + CH]
                active, slope = activation(x, t, (2 * n + j) * 4 + at["y"])
                pair.append(active)
                slopes.append(slope * x)
            start = pl.multiple_of(n * 48, 16)
            act[t, pl.ds(start, 48)] = jnp.concatenate(pair, axis=0).astype(BF16)
            sx[t, pl.ds(start, 48)] = jnp.concatenate(slopes, axis=0)

    def weigh(slot, g, n):
        for kt in range(3):
            total = None
            for t in range(2):
                part = lax.dot_general(
                    s9[slot, t + 2 - kt], act[t], (((1,), (1,)), ((), ())), preferred_element_type=F32
                )
                total = part if total is None else total + part
            gc[216 * kt : 216 * kt + 216] = total
        g[n, 0:328] = jnp.concatenate([gc[0:328, 0:64], gc[320:648, 0:64]], axis=1)
        g[n, 328:USED] = jnp.concatenate([gc[160 * m : 160 * m + 168, 64:96] for m in range(4)], axis=1)
        g[n, USED:ROWS] = jnp.zeros((ROWS - USED, 128), F32)

    def core_reduce(bufs):
        other = pl.multiple_of((1 - at["k"]) * 256, 256)
        return send(bufs[0].at[:, pl.ds(other, 256)], bufs[1], shifted(at, k=1))

    def x_reduce(bufs):
        g, gr, h, hb, hr = bufs[:5]
        sends = []
        for by in (2, 1, 3, 0):
            start = (at["x"] + by) % 4 * 64
            value = (
                g[:, pl.ds(pl.multiple_of(at["k"] * 256 + start, 64), 64)]
                + gr[:, pl.ds(pl.multiple_of(start, 64), 64)]
            )
            if by == 0:
                h[...] = value
            else:
                hb[by - 1] = value.astype(BF16)
                sends.append(send(hb.at[by - 1], hr.at[by - 1], shifted(at, x=by)))
        return sends

    def z_reduce(bufs):
        h, hr, zs, zr = bufs[2], bufs[4], bufs[5], bufs[6]
        h[...] = h[...] + hr[0].astype(F32) + hr[1].astype(F32) + hr[2].astype(F32)
        sends = []
        for by in (3, 1, 2):
            zs[by - 1] = h[:, pl.ds(pl.multiple_of((at["zl"] + by) % 4 * 16, 16), 16)]
            sends.append(send(zs.at[by - 1], zr.at[by - 1], shifted(at, zl=by)))
        return sends

    def yz_gather(bufs, base):
        h, zr, sb = bufs[2], bufs[6], bufs[7]
        value = h[:, pl.ds(pl.multiple_of(at["zl"] * 16, 16), 16)] + zr[0] + zr[1] + zr[2]
        sb[...] = (value * (1.0 / math.sqrt(40960))).astype(BF16)
        piece = pl.multiple_of(at["k"] * 256 + at["x"] * 64 + at["zl"] * 16, 16)
        sends = []
        for n in range(2):
            slot = SLOTS[base + n]
            for dz in (3, 2, 1, 0):
                if slot == 0 and dz == 0:
                    ag[0, pl.ds(piece, 16)] = sb[0]
                else:
                    dst = ag.at[base + n, pl.ds(piece, 16)]
                    sends.append(send(sb.at[n], dst, shifted(at, y=-slot, zl=dz)))
        return sends

    def x_gather(base):
        start = pl.multiple_of(at["k"] * 256 + at["x"] * 64, 64)
        ref = ag.at[pl.ds(base, 2), pl.ds(start, 64)]
        return [send(ref, ref, shifted(at, x=by)) for by in (2, 1, 3)]

    def core_gather(base):
        ref = ag.at[pl.ds(base, 2), pl.ds(pl.multiple_of(at["k"] * 256, 256), 256)]
        return send(ref, ref, shifted(at, k=1))

    def unpack(place):
        value = ag[place].astype(F32)
        low, high = value[:328], value[328:USED]
        left = jnp.concatenate([low[:, :64], low[8:, 64:]], axis=0)
        right = jnp.concatenate(
            [high[:, :32], high[8:, 32:64], high[8:, 64:96], high[8:, 96:]], axis=0
        )
        piece = jnp.concatenate([left, right], axis=1).astype(BF16)
        return jnp.dot(piece, perm[SLOTS[place]], preferred_element_type=F32)

    weigh(SLOTS[0], chain_a[0], 0)
    weigh(SLOTS[1], chain_a[0], 1)
    a = core_reduce(chain_a)
    arrived(dy[2])
    build(2)
    dgrad(2)
    zsends = []
    for by in (2, 1, 3, 0):
        start = pl.multiple_of((at["zh"] + by) % 4 * CH, 8)
        value = jnp.concatenate([p[0, pl.ds(start, CH)], p[1, pl.ds(start, CH)]], axis=0)
        if by == 0:
            q[...] = value
        else:
            qb[by - 1] = value.astype(BF16)
            zsends.append(send(qb.at[by - 1], rz.at[by - 1], shifted(at, zh=by)))
    for t in range(2):
        dsend[t : t + 1] = jnp.sum(p[t] * sx[t], axis=0, keepdims=True)
    dys = [send(dsend, dry.at[by - 1], shifted(at, y=by)) for by in (2, 1, 3)]
    weigh(SLOTS[2], chain_b[0], 0)
    weigh(SLOTS[3], chain_b[0], 1)
    b = core_reduce(chain_b)
    arrived([a])
    a = x_reduce(chain_a)
    arrived(dys)
    dmid[...] = dsend[...] + dry[0] + dry[1] + dry[2]
    dzs = [send(dmid, drz.at[by - 1], shifted(at, zh=by)) for by in (2, 1, 3)]
    arrived([b])
    b = x_reduce(chain_b)
    arrived(a)
    a = z_reduce(chain_a)
    arrived(b)
    b = z_reduce(chain_b)
    arrived(a)
    a = yz_gather(chain_a, 0)
    arrived(b)
    b = yz_gather(chain_b, 2)
    arrived(a)
    a = x_gather(0)
    arrived(b)
    b = x_gather(2)
    arrived(a)
    a = core_gather(0)
    arrived(b)
    b = core_gather(2)

    arrived(zsends + dzs)
    grad = q[...] + rz[0].astype(F32) + rz[1].astype(F32) + rz[2].astype(F32)
    dots = dmid[...] + drz[0] + drz[1] + drz[2]
    mine_x = f_ref[...].astype(F32)
    ct = d_ref[...].astype(F32)
    outs = []
    for t in range(2):
        rows = slice(CH * t, CH * t + CH)
        x = mine_x[rows]
        _, slope = activation(x, t, at["zh"] * 4 + at["y"])
        up = grad[rows] * slope
        r = inv[t : t + 1]
        back = r * up - x * (r * r * r * dots[t : t + 1] * (1.0 / TOTAL))
        outs.append(ct[rows] + back)
    od_ref[...] = jnp.concatenate(outs, axis=0).astype(BF16)

    arrived([a])
    wgrad[...] = unpack(0) + unpack(1)
    arrived([b])
    og_ref[...] = (wgrad[...] + unpack(2) + unpack(3)).astype(BF16)
    for copy in started:
        copy.wait_send()
    for copy, goes, _ in halo:
        pl.when(goes)(copy.wait_send)


def chain_buffers():
    return [
        pltpu.VMEM((2, ROWS, 128), F32),
        pltpu.VMEM((2, 256, 128), F32),
        pltpu.VMEM((2, 64, 128), F32),
        pltpu.VMEM((3, 2, 64, 128), BF16),
        pltpu.VMEM((3, 2, 64, 128), BF16),
        pltpu.VMEM((3, 2, 16, 128), F32),
        pltpu.VMEM((3, 2, 16, 128), F32),
        pltpu.VMEM((2, 16, 128), BF16),
    ]


def on_device(features, cotangent, conv_weight, norm_gain, norm_bias):
    chans, frames, rows, cols = features.shape
    fd = jnp.transpose(jnp.stack([features, cotangent]), (0, 2, 1, 3, 4))
    fd = fd.reshape(2 * frames * chans, rows * cols)
    vmem = pl.BlockSpec(memory_space=pltpu.VMEM)
    hbm = pl.BlockSpec(memory_space=pl.ANY)
    w = jnp.transpose(conv_weight, (1, 0, 2)).reshape(27 * chans, TOTAL)
    sums = pltpu.VMEM((2, LANES), F32)
    sums3 = pltpu.VMEM((3, 2, LANES), F32)
    cells = pltpu.VMEM((3, 48, LANES), BF16)
    grads, out = pl.pallas_call(
        kernel,
        name="unit_backward",
        out_shape=(
            jax.ShapeDtypeStruct((648, TOTAL), BF16),
            jax.ShapeDtypeStruct((48, LANES), BF16),
        ),
        in_specs=[vmem, hbm, hbm, hbm],
        out_specs=(vmem, vmem),
        scratch_shapes=[
            pltpu.VMEM((27 * CH, TOTAL), BF16),
            pltpu.VMEM((TOTAL,), F32),
            pltpu.VMEM((TOTAL,), F32),
            pltpu.VMEM((3, TOTAL, 9 * CH), F32),
            pltpu.VMEM((3, 288, 9 * CH), BF16),
            pltpu.VMEM((4, 288, 9 * CH), BF16),
            pltpu.VMEM((TOTAL, 8), F32),
            cells,
            pltpu.VMEM((4, 48, LANES), BF16),
            pltpu.VMEM((4, 4, 48, 256), BF16),
            pltpu.VMEM((4, 48, LANES), BF16),
            pltpu.VMEM((4, 4, 216, LANES), BF16),
            pltpu.VMEM((2, 96, LANES), F32),
            pltpu.VMEM((48, LANES), F32),
            cells,
            cells,
            pltpu.VMEM((2, 96, LANES), BF16),
            pltpu.VMEM((2, 96, LANES), F32),
            sums,
            sums,
            pltpu.VMEM((4, 2, LANES), F32),
            sums3,
            sums,
            sums,
            sums,
            sums3,
            sums3,
            pltpu.VMEM((648, 96), F32),
            pltpu.VMEM((4, 96, TOTAL), BF16),
            pltpu.VMEM((648, TOTAL), F32),
            pltpu.VMEM((4, ROWS, 128), BF16),
            chain_buffers(),
            chain_buffers(),
            pltpu.SemaphoreType.DMA((3,)),
            pltpu.SemaphoreType.DMA((COPIES,)),
            pltpu.SemaphoreType.DMA((COPIES,)),
        ],
        compiler_params=pltpu.CompilerParams(
            collective_id=0, has_side_effects=True, vmem_limit_bytes=40 << 20
        ),
    )(fd, w, norm_gain, norm_bias)
    result = jnp.transpose(out.reshape(frames, chans, rows, cols), (1, 0, 2, 3))
    weight_grad = jnp.transpose(grads.reshape(27, chans, TOTAL), (1, 0, 2)).astype(F32)
    return result, weight_grad


def solution(mesh):
    return jax.shard_map(
        on_device,
        mesh=mesh,
        in_specs=(
            P("chan", "tm", "height", None),
            P("chan", "tm", "height", None),
            P("chan", None, None),
            P(),
            P(),
        ),
        out_specs=(P("chan", "tm", "height", None), P("chan", None, None)),
        check_vma=False,
    )
```

```python
import functools
import math

import jax
import jax.numpy as jnp
from jax import lax
from jax.experimental import pallas as pl
from jax.experimental.pallas import tpu as pltpu
from jax.sharding import PartitionSpec as P

MESH = pl.DeviceIdType.MESH
SIZES = {"x": 4, "zl": 4, "k": 2, "zh": 4, "y": 4}
CH = 24
TOTAL = 384
LANES = 640
F32 = jnp.float32
BF16 = jnp.bfloat16


def coords():
    t = lax.axis_index("tm")
    h = lax.axis_index("height")
    c = lax.axis_index("chan")
    return {"x": t, "zl": h // 2, "k": h % 2, "zh": c // 4, "y": c % 4}


def shifted(at, **offsets):
    at = dict(at)
    for name, by in offsets.items():
        at[name] = (at[name] + (by % SIZES[name])) % SIZES[name]
    return {"tm": at["x"], "height": at["zl"] * 2 + at["k"], "chan": at["zh"] * 4 + at["y"]}


def neighbour(at, dx, dh):
    t = (at["x"] + (dx % 4)) % 4
    h = (at["zl"] * 2 + at["k"] + (dh % 8)) % 8
    return {"tm": t, "height": h, "chan": at["zh"] * 4 + at["y"]}


HALO = ((-1, 0), (0, 1), (0, -1), (-1, 1), (-1, -1))
COPIES = 96
STEPS = tuple(slice(16 * n, 16 * n + 16) for n in range(3))
SLOTS = (0, 1, 3, 2)
ROWS = 512
USED = 496


def kernel(
    fd_ref, raw_hbm, gain_hbm, bias_hbm, og_ref, od_ref,
    raw, gain_ref, bias_ref, tall, slabs, wall, gb_ref, dall, dnall, edall, fall, s9, p, q, qb, rz, act, sx, inv,
    sown, smid, sry, srz, dsend, dmid, dry, drz, gc, perm, wgrad, ag, chain_a, chain_b, lsem, ssem, rsem,
):
    f_ref, d_ref = fd_ref.at[0:48], fd_ref.at[48:96]
    at = coords()
    count = [0]
    started = []

    def send(src, dst, target):
        i = count[0]
        count[0] += 1
        copy = pltpu.make_async_remote_copy(
            src_ref=src, dst_ref=dst, send_sem=ssem.at[i], recv_sem=rsem.at[i],
            device_id=target, device_id_type=MESH,
        )
        copy.start()
        started.append(copy)
        return copy

    def arrived(copies):
        for copy in copies:
            copy.wait_recv()

    loads = [
        pltpu.make_async_copy(src, dst, lsem.at[n])
        for n, (src, dst) in enumerate(((gain_hbm, gain_ref), (bias_hbm, bias_ref), (raw_hbm, raw)))
    ]
    for copy in loads:
        copy.start()
    edall[0] = jnp.zeros((4, 48, 256), BF16)
    barrier = pltpu.get_barrier_semaphore()
    greeted = [shifted(at, zh=1), shifted(at, zh=3)]
    greeted += [neighbour(at, -dx, -dh) for dx, dh in HALO]
    greeted += [shifted(at, x=by) for by in (1, 2, 3)]
    greeted += [shifted(at, y=dy, zl=dz) for dy in range(4) for dz in range(4) if dy or dz]
    greeted.append(shifted(at, k=1))
    for one in greeted:
        pl.semaphore_signal(barrier, inc=1, device_id=one, device_id_type=MESH)

    fall[at["zh"]] = f_ref[...]
    squares = f_ref[...].astype(F32)
    squares = squares * squares
    for t in range(2):
        sown[t : t + 1] = jnp.sum(squares[CH * t : CH * t + CH], axis=0, keepdims=True)
    pl.semaphore_wait(barrier, len(greeted))

    row = at["zl"] * 2 + at["k"]
    below, above = row < 7, row > 0
    frame = send(d_ref, dnall.at[0], neighbour(at, -1, 0))
    halo = []
    for n, (dx, dh) in enumerate(HALO[1:]):
        i = count[0]
        count[0] += 1
        copy = pltpu.make_async_remote_copy(
            src_ref=d_ref.at[:, pl.ds(384 if dh == 1 else 0, 256)], dst_ref=edall.at[0, n],
            send_sem=ssem.at[i], recv_sem=rsem.at[i],
            device_id=neighbour(at, dx, dh), device_id_type=MESH,
        )
        goes, comes = (below, above) if dh == 1 else (above, below)
        pl.when(goes)(copy.start)
        halo.append((copy, goes, comes))
    fz = [
        [send(f_ref.at[rows], fall.at[at["zh"], rows], shifted(at, zh=by)) for by in (1, 3)] for rows in STEPS
    ]
    sys = [send(sown, sry.at[by - 1], shifted(at, y=by)) for by in (2, 1, 3)]
    dy = {by: [send(d_ref, dall.at[by - 1], shifted(at, y=by))] for by in (1, 3, 2)}

    loads[2].wait()
    for kt in range(3):
        tall[kt] = raw[216 * kt : 216 * kt + 216].astype(F32).T

    def slab(by):
        y = (at["y"] + by) % 4
        groups = [
            tall[kt, pl.ds(pl.multiple_of(96 * zh + y * CH, 8), CH)] for kt in range(3) for zh in range(4)
        ]
        return jnp.concatenate(groups, axis=0).astype(BF16)

    wall[0] = slab(0)
    for by in (1, 2, 3):
        slabs[by - 1] = slab(by)
    arrived([frame])
    for by in (1, 3, 2):
        dy[by].append(send(dnall.at[0], dnall.at[by], shifted(at, y=by)))
    for copy, _, comes in halo:
        pl.when(comes)(copy.wait_recv)
    for by in (1, 3, 2):
        dy[by].append(send(edall.at[0], edall.at[by], shifted(at, y=by)))
    half = pl.multiple_of(at["k"] * 144, 16)
    ws = [
        send(slabs.at[by - 1, pl.ds(half, 144)], wall.at[by, pl.ds(half, 144)], shifted(at, y=by))
        for by in (2, 1, 3)
    ]


    column = lax.broadcasted_iota(jnp.int32, (CH, LANES), 1) % 160
    left_end, right_end = column == 0, column == 159
    next_on = jnp.where(at["x"] < 3, 1.0, 0.0).astype(F32)

    def build(slot):
        for tp in range(4):
            rows = slice(CH * (tp % 2), CH * (tp % 2) + CH)
            late = tp >= 2
            if late:
                own = dnall[slot].astype(F32)[rows]
            else:
                own = (d_ref[...] if slot == 0 else dall[slot - 1]).astype(F32)[rows]
            top = edall[slot, 2 if late else 0].astype(F32)[rows]
            bottom = edall[slot, 3 if late else 1].astype(F32)[rows]
            if late:
                own, top, bottom = own * next_on, top * next_on, bottom * next_on
            moved = (
                jnp.concatenate([own[:, 160:], bottom[:, :160]], axis=1),
                own,
                jnp.concatenate([top[:, 96:], own[:, :480]], axis=1),
            )
            pieces = []
            for one in moved:
                pieces.append(jnp.where(right_end, 0.0, pltpu.roll(one, LANES - 1, 1)))
                pieces.append(one)
                pieces.append(jnp.where(left_end, 0.0, pltpu.roll(one, 1, 1)))
            s9[slot, tp] = jnp.concatenate(pieces, axis=0).astype(BF16)

    def dgrad(slot):
        for tp, (low, high) in enumerate(((192, 288), (96, 288), (0, 192), (0, 96))):
            part = jnp.dot(wall[slot, low:high], s9[slot, tp], preferred_element_type=F32)
            for n in range((high - low) // 96):
                t = n if high - low > 96 else tp // 3
                piece = part[96 * n : 96 * n + 96]
                if slot == 0 and (tp == 0 or (tp == 1 and t == 1)):
                    p[t] = piece
                else:
                    p[t] += piece

    side = 1 + 2 * at["k"]
    source = (at["zh"] + side) % 4
    away = {"tm": at["x"], "height": row, "chan": (at["zh"] + 4 - side) % 4 * 4 + at["y"]}
    fz_far = []

    def far_step(n):
        arrived(fz[n])
        ref = fall.at[source, STEPS[n]]
        fz_far.append(send(ref, ref, away))

    arrived(sys)
    smid[0] = sown[...] + sry[0] + sry[1] + sry[2]
    szs = [send(smid.at[0], smid.at[by], shifted(at, zh=by)) for by in (1, 3)]
    far_step(0)
    build(0)
    far_step(1)
    dgrad(0)
    far_step(2)
    arrived(szs)
    szf = send(smid.at[1], srz, shifted(at, zh=1))
    loads[0].wait()
    loads[1].wait()
    pair = [ref[...].reshape(1, TOTAL) for ref in (gain_ref, bias_ref)]
    both = jnp.concatenate(pair + [jnp.zeros((6, TOTAL), F32)], axis=0)
    gb_ref[...] = both.T

    r = lax.broadcasted_iota(jnp.int32, (96, TOTAL), 0)
    lane = lax.broadcasted_iota(jnp.int32, (96, TOTAL), 1)
    group = (r >= 24).astype(jnp.int32) + (r >= 48).astype(jnp.int32) + (r >= 72).astype(jnp.int32)
    for s in range(4):
        target = r + 72 * group + CH * ((at["y"] + s) % 4)
        perm[s] = jnp.where(lane == target, 1.0, 0.0).astype(BF16)

    arrived(dy[1])
    build(1)
    arrived(dy[3])
    build(3)
    arrived([szf])
    total = smid[0] + smid[1] + smid[3] + srz[...]
    inv[...] = lax.rsqrt(total * (1.0 / TOTAL) + 1e-06)

    def activation(x, t, block):
        start = pl.multiple_of(block * CH, 8)
        gain = gb_ref[pl.ds(start, CH), 0:1]
        bias = gb_ref[pl.ds(start, CH), 1:2]
        normed = x * inv[t : t + 1] * gain + bias
        sig = 0.5 * jnp.tanh(0.5 * normed) + 0.5
        return normed * sig, sig * (1.0 + normed * (1.0 - sig)) * gain

    arrived(fz_far)

    @pl.loop(0, 2)
    def _(n):
        blocks = [fall[2 * n + j].astype(F32) for j in range(2)]
        for t in range(2):
            pair, slopes = [], []
            for j in range(2):
                x = blocks[j][CH * t : CH * t + CH]
                active, slope = activation(x, t, (2 * n + j) * 4 + at["y"])
                pair.append(active)
                slopes.append(slope * x)
            start = pl.multiple_of(n * 48, 16)
            act[t, pl.ds(start, 48)] = jnp.concatenate(pair, axis=0).astype(BF16)
            sx[t, pl.ds(start, 48)] = jnp.concatenate(slopes, axis=0)

    def weigh(slot, g, n):
        for kt in range(3):
            total = None
            for t in range(2):
                part = lax.dot_general(
                    s9[slot, t + 2 - kt], act[t], (((1,), (1,)), ((), ())), preferred_element_type=F32
                )
                total = part if total is None else total + part
            gc[216 * kt : 216 * kt + 216] = total
        g[n, 0:328] = jnp.concatenate([gc[0:328, 0:64], gc[320:648, 0:64]], axis=1)
        g[n, 328:USED] = jnp.concatenate([gc[160 * m : 160 * m + 168, 64:96] for m in range(4)], axis=1)
        g[n, USED:ROWS] = jnp.zeros((ROWS - USED, 128), F32)

    def core_reduce(bufs):
        other = pl.multiple_of((1 - at["k"]) * 256, 256)
        return send(bufs[0].at[:, pl.ds(other, 256)], bufs[1], shifted(at, k=1))

    def x_reduce(bufs):
        g, gr, h, hb, hr = bufs[:5]
        sends = []
        for by in (2, 1, 3, 0):
            start = (at["x"] + by) % 4 * 64
            value = (
                g[:, pl.ds(pl.multiple_of(at["k"] * 256 + start, 64), 64)]
                + gr[:, pl.ds(pl.multiple_of(start, 64), 64)]
            )
            if by == 0:
                h[...] = value
            else:
                hb[by - 1] = value.astype(BF16)
                sends.append(send(hb.at[by - 1], hr.at[by - 1], shifted(at, x=by)))
        return sends

    def z_reduce(bufs):
        h, hr, zs, zr = bufs[2], bufs[4], bufs[5], bufs[6]
        h[...] = h[...] + hr[0].astype(F32) + hr[1].astype(F32) + hr[2].astype(F32)
        sends = []
        for by in (3, 1, 2):
            zs[by - 1] = h[:, pl.ds(pl.multiple_of((at["zl"] + by) % 4 * 16, 16), 16)]
            sends.append(send(zs.at[by - 1], zr.at[by - 1], shifted(at, zl=by)))
        return sends

    def yz_gather(bufs, base):
        h, zr, sb = bufs[2], bufs[6], bufs[7]
        value = h[:, pl.ds(pl.multiple_of(at["zl"] * 16, 16), 16)] + zr[0] + zr[1] + zr[2]
        sb[...] = (value * (1.0 / math.sqrt(40960))).astype(BF16)
        piece = pl.multiple_of(at["k"] * 256 + at["x"] * 64 + at["zl"] * 16, 16)
        sends = []
        for n in range(2):
            slot = SLOTS[base + n]
            for dz in (3, 2, 1, 0):
                if slot == 0 and dz == 0:
                    ag[0, pl.ds(piece, 16)] = sb[0]
                else:
                    dst = ag.at[base + n, pl.ds(piece, 16)]
                    sends.append(send(sb.at[n], dst, shifted(at, y=-slot, zl=dz)))
        return sends

    def x_gather(base):
        start = pl.multiple_of(at["k"] * 256 + at["x"] * 64, 64)
        ref = ag.at[pl.ds(base, 2), pl.ds(start, 64)]
        return [send(ref, ref, shifted(at, x=by)) for by in (2, 1, 3)]

    def core_gather(base):
        ref = ag.at[pl.ds(base, 2), pl.ds(pl.multiple_of(at["k"] * 256, 256), 256)]
        return send(ref, ref, shifted(at, k=1))

    def unpack(place):
        value = ag[place].astype(F32)
        low, high = value[:328], value[328:USED]
        left = jnp.concatenate([low[:, :64], low[8:, 64:]], axis=0)
        right = jnp.concatenate(
            [high[:, :32], high[8:, 32:64], high[8:, 64:96], high[8:, 96:]], axis=0
        )
        piece = jnp.concatenate([left, right], axis=1).astype(BF16)
        return jnp.dot(piece, perm[SLOTS[place]], preferred_element_type=F32)

    weigh(SLOTS[0], chain_a[0], 0)
    weigh(SLOTS[1], chain_a[0], 1)
    a = core_reduce(chain_a)
    arrived(dy[2])
    build(2)
    arrived(ws)
    ref = wall.at[pl.ds(1, 3), pl.ds(half, 144)]
    wx = send(ref, ref, shifted(at, k=1))
    weigh(SLOTS[2], chain_b[0], 0)
    weigh(SLOTS[3], chain_b[0], 1)
    b = core_reduce(chain_b)
    arrived([a])
    a = x_reduce(chain_a)
    arrived([wx])
    dgrad(1)
    arrived([b])
    b = x_reduce(chain_b)
    dgrad(3)
    dgrad(2)
    for t in range(2):
        dsend[t : t + 1] = jnp.sum(p[t] * sx[t], axis=0, keepdims=True)
    dys = [send(dsend, dry.at[by - 1], shifted(at, y=by)) for by in (2, 1, 3)]
    arrived(a)
    a = z_reduce(chain_a)
    arrived(b)
    b = z_reduce(chain_b)
    zsends = []
    for by in (2, 1, 3, 0):
        start = pl.multiple_of((at["zh"] + by) % 4 * CH, 8)
        value = jnp.concatenate([p[0, pl.ds(start, CH)], p[1, pl.ds(start, CH)]], axis=0)
        if by == 0:
            q[...] = value
        else:
            qb[by - 1] = value.astype(BF16)
            zsends.append(send(qb.at[by - 1], rz.at[by - 1], shifted(at, zh=by)))
    arrived(dys)
    dmid[...] = dsend[...] + dry[0] + dry[1] + dry[2]
    dzs = [send(dmid, drz.at[by - 1], shifted(at, zh=by)) for by in (2, 1, 3)]
    arrived(a)
    a = yz_gather(chain_a, 0)
    arrived(b)
    b = yz_gather(chain_b, 2)
    arrived(a)
    a = x_gather(0)
    arrived(b)
    b = x_gather(2)
    arrived(a)
    a = core_gather(0)
    arrived(b)
    b = core_gather(2)

    arrived(zsends + dzs)
    grad = q[...] + rz[0].astype(F32) + rz[1].astype(F32) + rz[2].astype(F32)
    dots = dmid[...] + drz[0] + drz[1] + drz[2]
    mine_x = f_ref[...].astype(F32)
    ct = d_ref[...].astype(F32)
    outs = []
    for t in range(2):
        rows = slice(CH * t, CH * t + CH)
        x = mine_x[rows]
        _, slope = activation(x, t, at["zh"] * 4 + at["y"])
        up = grad[rows] * slope
        r = inv[t : t + 1]
        back = r * up - x * (r * r * r * dots[t : t + 1] * (1.0 / TOTAL))
        outs.append(ct[rows] + back)
    od_ref[...] = jnp.concatenate(outs, axis=0).astype(BF16)

    arrived([a])
    wgrad[...] = unpack(0) + unpack(1)
    arrived([b])
    og_ref[...] = (wgrad[...] + unpack(2) + unpack(3)).astype(BF16)
    for copy in started:
        copy.wait_send()
    for copy, goes, _ in halo:
        pl.when(goes)(copy.wait_send)


def chain_buffers():
    return [
        pltpu.VMEM((2, ROWS, 128), F32),
        pltpu.VMEM((2, 256, 128), F32),
        pltpu.VMEM((2, 64, 128), F32),
        pltpu.VMEM((3, 2, 64, 128), BF16),
        pltpu.VMEM((3, 2, 64, 128), BF16),
        pltpu.VMEM((3, 2, 16, 128), F32),
        pltpu.VMEM((3, 2, 16, 128), F32),
        pltpu.VMEM((2, 16, 128), BF16),
    ]


def on_device(features, cotangent, conv_weight, norm_gain, norm_bias):
    chans, frames, rows, cols = features.shape
    fd = jnp.transpose(jnp.stack([features, cotangent]), (0, 2, 1, 3, 4))
    fd = fd.reshape(2 * frames * chans, rows * cols)
    vmem = pl.BlockSpec(memory_space=pltpu.VMEM)
    hbm = pl.BlockSpec(memory_space=pl.ANY)
    w = jnp.transpose(conv_weight, (1, 0, 2)).reshape(27 * chans, TOTAL)
    sums = pltpu.VMEM((2, LANES), F32)
    sums3 = pltpu.VMEM((3, 2, LANES), F32)
    cells = pltpu.VMEM((3, 48, LANES), BF16)
    grads, out = pl.pallas_call(
        kernel,
        name="unit_backward",
        out_shape=(
            jax.ShapeDtypeStruct((648, TOTAL), BF16),
            jax.ShapeDtypeStruct((48, LANES), BF16),
        ),
        in_specs=[vmem, hbm, hbm, hbm],
        out_specs=(vmem, vmem),
        scratch_shapes=[
            pltpu.VMEM((27 * CH, TOTAL), BF16),
            pltpu.VMEM((TOTAL,), F32),
            pltpu.VMEM((TOTAL,), F32),
            pltpu.VMEM((3, TOTAL, 9 * CH), F32),
            pltpu.VMEM((3, 288, 9 * CH), BF16),
            pltpu.VMEM((4, 288, 9 * CH), BF16),
            pltpu.VMEM((TOTAL, 8), F32),
            cells,
            pltpu.VMEM((4, 48, LANES), BF16),
            pltpu.VMEM((4, 4, 48, 256), BF16),
            pltpu.VMEM((4, 48, LANES), BF16),
            pltpu.VMEM((4, 4, 216, LANES), BF16),
            pltpu.VMEM((2, 96, LANES), F32),
            pltpu.VMEM((48, LANES), F32),
            cells,
            cells,
            pltpu.VMEM((2, 96, LANES), BF16),
            pltpu.VMEM((2, 96, LANES), F32),
            sums,
            sums,
            pltpu.VMEM((4, 2, LANES), F32),
            sums3,
            sums,
            sums,
            sums,
            sums3,
            sums3,
            pltpu.VMEM((648, 96), F32),
            pltpu.VMEM((4, 96, TOTAL), BF16),
            pltpu.VMEM((648, TOTAL), F32),
            pltpu.VMEM((4, ROWS, 128), BF16),
            chain_buffers(),
            chain_buffers(),
            pltpu.SemaphoreType.DMA((3,)),
            pltpu.SemaphoreType.DMA((COPIES,)),
            pltpu.SemaphoreType.DMA((COPIES,)),
        ],
        compiler_params=pltpu.CompilerParams(
            collective_id=0, has_side_effects=True, vmem_limit_bytes=40 << 20
        ),
    )(fd, w, norm_gain, norm_bias)
    result = jnp.transpose(out.reshape(frames, chans, rows, cols), (1, 0, 2, 3))
    weight_grad = jnp.transpose(grads.reshape(27, chans, TOTAL), (1, 0, 2)).astype(F32)
    return result, weight_grad


def solution(mesh):
    return jax.shard_map(
        on_device,
        mesh=mesh,
        in_specs=(
            P("chan", "tm", "height", None),
            P("chan", "tm", "height", None),
            P("chan", None, None),
            P(),
            P(),
        ),
        out_specs=(P("chan", "tm", "height", None), P("chan", None, None)),
        check_vma=False,
    )
```

```python
import functools
import math

import jax
import jax.numpy as jnp
from jax import lax
from jax.experimental import pallas as pl
from jax.experimental.pallas import tpu as pltpu
from jax.sharding import PartitionSpec as P

MESH = pl.DeviceIdType.MESH
SIZES = {"x": 4, "zl": 4, "k": 2, "zh": 4, "y": 4}
CH = 24
TOTAL = 384
LANES = 640
F32 = jnp.float32
BF16 = jnp.bfloat16


def coords():
    t = lax.axis_index("tm")
    h = lax.axis_index("height")
    c = lax.axis_index("chan")
    return {"x": t, "zl": h // 2, "k": h % 2, "zh": c // 4, "y": c % 4}


def shifted(at, **offsets):
    at = dict(at)
    for name, by in offsets.items():
        at[name] = (at[name] + (by % SIZES[name])) % SIZES[name]
    return {"tm": at["x"], "height": at["zl"] * 2 + at["k"], "chan": at["zh"] * 4 + at["y"]}


def neighbour(at, dx, dh):
    t = (at["x"] + (dx % 4)) % 4
    h = (at["zl"] * 2 + at["k"] + (dh % 8)) % 8
    return {"tm": t, "height": h, "chan": at["zh"] * 4 + at["y"]}


HALO = ((-1, 0), (0, 1), (0, -1), (-1, 1), (-1, -1))
COPIES = 96
STEPS = tuple(slice(16 * n, 16 * n + 16) for n in range(3))
SLOTS = (0, 1, 3, 2)
ROWS = 512
USED = 496


def kernel(
    fd_ref, raw_hbm, gain_hbm, bias_hbm, og_ref, od_ref,
    raw, gain_ref, bias_ref, tall, slabs, wall, gb_ref, dall, dnall, edall, fall, s9, p, q, qb, rz, act, sx, inv,
    sown, smid, sry, srz, dsend, dmid, dry, drz, gc, perm, wgrad, ag, chain_a, chain_b, lsem, ssem, rsem,
):
    f_ref, d_ref = fd_ref.at[0:48], fd_ref.at[48:96]
    at = coords()
    count = [0]
    started = []

    def send(src, dst, target):
        i = count[0]
        count[0] += 1
        copy = pltpu.make_async_remote_copy(
            src_ref=src, dst_ref=dst, send_sem=ssem.at[i], recv_sem=rsem.at[i],
            device_id=target, device_id_type=MESH,
        )
        copy.start()
        started.append(copy)
        return copy

    def arrived(copies):
        for copy in copies:
            copy.wait_recv()

    loads = [
        pltpu.make_async_copy(src, dst, lsem.at[n])
        for n, (src, dst) in enumerate(((gain_hbm, gain_ref), (bias_hbm, bias_ref), (raw_hbm, raw)))
    ]
    for copy in loads:
        copy.start()
    edall[0] = jnp.zeros((4, 48, 256), BF16)
    barrier = pltpu.get_barrier_semaphore()
    greeted = [shifted(at, zh=1), shifted(at, zh=3)]
    greeted += [neighbour(at, -dx, -dh) for dx, dh in HALO]
    greeted += [shifted(at, x=by) for by in (1, 2, 3)]
    greeted += [shifted(at, y=dy, zl=dz) for dy in range(4) for dz in range(4) if dy or dz]
    greeted.append(shifted(at, k=1))
    for one in greeted:
        pl.semaphore_signal(barrier, inc=1, device_id=one, device_id_type=MESH)

    fall[at["zh"]] = f_ref[...]
    squares = f_ref[...].astype(F32)
    squares = squares * squares
    for t in range(2):
        sown[t : t + 1] = jnp.sum(squares[CH * t : CH * t + CH], axis=0, keepdims=True)
    pl.semaphore_wait(barrier, len(greeted))

    row = at["zl"] * 2 + at["k"]
    below, above = row < 7, row > 0
    frame = send(d_ref, dnall.at[0], neighbour(at, -1, 0))
    halo = []
    for n, (dx, dh) in enumerate(HALO[1:]):
        i = count[0]
        count[0] += 1
        copy = pltpu.make_async_remote_copy(
            src_ref=d_ref.at[:, pl.ds(384 if dh == 1 else 0, 256)], dst_ref=edall.at[0, n],
            send_sem=ssem.at[i], recv_sem=rsem.at[i],
            device_id=neighbour(at, dx, dh), device_id_type=MESH,
        )
        goes, comes = (below, above) if dh == 1 else (above, below)
        pl.when(goes)(copy.start)
        halo.append((copy, goes, comes))
    fz = [
        [send(f_ref.at[rows], fall.at[at["zh"], rows], shifted(at, zh=by)) for by in (1, 3)] for rows in STEPS
    ]
    sys = [send(sown, sry.at[by - 1], shifted(at, y=by)) for by in (2, 1, 3)]
    dy = {by: [send(d_ref, dall.at[by - 1], shifted(at, y=by))] for by in (1, 3, 2)}

    loads[2].wait()
    for kt in range(3):
        tall[kt] = raw[216 * kt : 216 * kt + 216].astype(F32).T

    def slab(by):
        y = (at["y"] + by) % 4
        groups = [
            tall[kt, pl.ds(pl.multiple_of(96 * zh + y * CH, 8), CH)] for kt in range(3) for zh in range(4)
        ]
        return jnp.concatenate(groups, axis=0).astype(BF16)

    wall[0] = slab(0)
    for by in (1, 2, 3):
        slabs[by - 1] = slab(by)
    half = pl.multiple_of(at["k"] * 144, 16)
    ws = [
        send(slabs.at[by - 1, pl.ds(half, 144)], wall.at[by, pl.ds(half, 144)], shifted(at, y=by))
        for by in (2, 1, 3)
    ]

    arrived([frame])
    for by in (1, 3, 2):
        dy[by].append(send(dnall.at[0], dnall.at[by], shifted(at, y=by)))
    for copy, _, comes in halo:
        pl.when(comes)(copy.wait_recv)
    for by in (1, 3, 2):
        dy[by].append(send(edall.at[0], edall.at[by], shifted(at, y=by)))
    column = lax.broadcasted_iota(jnp.int32, (CH, LANES), 1) % 160
    left_end, right_end = column == 0, column == 159
    next_on = jnp.where(at["x"] < 3, 1.0, 0.0).astype(F32)

    def build(slot):
        for tp in range(4):
            rows = slice(CH * (tp % 2), CH * (tp % 2) + CH)
            late = tp >= 2
            if late:
                own = dnall[slot].astype(F32)[rows]
            else:
                own = (d_ref[...] if slot == 0 else dall[slot - 1]).astype(F32)[rows]
            top = edall[slot, 2 if late else 0].astype(F32)[rows]
            bottom = edall[slot, 3 if late else 1].astype(F32)[rows]
            if late:
                own, top, bottom = own * next_on, top * next_on, bottom * next_on
            moved = (
                jnp.concatenate([own[:, 160:], bottom[:, :160]], axis=1),
                own,
                jnp.concatenate([top[:, 96:], own[:, :480]], axis=1),
            )
            pieces = []
            for one in moved:
                pieces.append(jnp.where(right_end, 0.0, pltpu.roll(one, LANES - 1, 1)))
                pieces.append(one)
                pieces.append(jnp.where(left_end, 0.0, pltpu.roll(one, 1, 1)))
            s9[slot, tp] = jnp.concatenate(pieces, axis=0).astype(BF16)

    def dgrad(slot):
        for tp, (low, high) in enumerate(((192, 288), (96, 288), (0, 192), (0, 96))):
            part = jnp.dot(wall[slot, low:high], s9[slot, tp], preferred_element_type=F32)
            for n in range((high - low) // 96):
                t = n if high - low > 96 else tp // 3
                piece = part[96 * n : 96 * n + 96]
                if slot == 0 and (tp == 0 or (tp == 1 and t == 1)):
                    p[t] = piece
                else:
                    p[t] += piece

    side = 1 + 2 * at["k"]
    source = (at["zh"] + side) % 4
    away = {"tm": at["x"], "height": row, "chan": (at["zh"] + 4 - side) % 4 * 4 + at["y"]}
    fz_far = []

    def far_step(n):
        arrived(fz[n])
        ref = fall.at[source, STEPS[n]]
        fz_far.append(send(ref, ref, away))

    arrived(sys)
    smid[0] = sown[...] + sry[0] + sry[1] + sry[2]
    szs = [send(smid.at[0], smid.at[by], shifted(at, zh=by)) for by in (1, 3)]
    far_step(0)
    build(0)
    far_step(1)
    dgrad(0)
    far_step(2)
    arrived(ws)
    ref = wall.at[pl.ds(1, 3), pl.ds(half, 144)]
    wx = send(ref, ref, shifted(at, k=1))
    arrived(szs)
    szf = send(smid.at[1], srz, shifted(at, zh=1))
    loads[0].wait()
    loads[1].wait()
    pair = [ref[...].reshape(1, TOTAL) for ref in (gain_ref, bias_ref)]
    both = jnp.concatenate(pair + [jnp.zeros((6, TOTAL), F32)], axis=0)
    gb_ref[...] = both.T

    r = lax.broadcasted_iota(jnp.int32, (96, TOTAL), 0)
    lane = lax.broadcasted_iota(jnp.int32, (96, TOTAL), 1)
    group = (r >= 24).astype(jnp.int32) + (r >= 48).astype(jnp.int32) + (r >= 72).astype(jnp.int32)
    for s in range(4):
        target = r + 72 * group + CH * ((at["y"] + s) % 4)
        perm[s] = jnp.where(lane == target, 1.0, 0.0).astype(BF16)

    arrived(dy[1])
    build(1)
    arrived([wx])
    dgrad(1)
    arrived(dy[3])
    build(3)
    dgrad(3)
    arrived([szf])
    total = smid[0] + smid[1] + smid[3] + srz[...]
    inv[...] = lax.rsqrt(total * (1.0 / TOTAL) + 1e-06)

    def activation(x, t, block):
        start = pl.multiple_of(block * CH, 8)
        gain = gb_ref[pl.ds(start, CH), 0:1]
        bias = gb_ref[pl.ds(start, CH), 1:2]
        normed = x * inv[t : t + 1] * gain + bias
        sig = 0.5 * jnp.tanh(0.5 * normed) + 0.5
        return normed * sig, sig * (1.0 + normed * (1.0 - sig)) * gain

    arrived(fz_far)

    @pl.loop(0, 2)
    def _(n):
        blocks = [fall[2 * n + j].astype(F32) for j in range(2)]
        for t in range(2):
            pair, slopes = [], []
            for j in range(2):
                x = blocks[j][CH * t : CH * t + CH]
                active, slope = activation(x, t, (2 * n + j) * 4 + at["y"])
                pair.append(active)
                slopes.append(slope * x)
            start = pl.multiple_of(n * 48, 16)
            act[t, pl.ds(start, 48)] = jnp.concatenate(pair, axis=0).astype(BF16)
            sx[t, pl.ds(start, 48)] = jnp.concatenate(slopes, axis=0)

    def weigh(slot, g, n):
        for kt in range(3):
            total = None
            for t in range(2):
                part = lax.dot_general(
                    s9[slot, t + 2 - kt], act[t], (((1,), (1,)), ((), ())), preferred_element_type=F32
                )
                total = part if total is None else total + part
            gc[216 * kt : 216 * kt + 216] = total
        g[n, 0:328] = jnp.concatenate([gc[0:328, 0:64], gc[320:648, 0:64]], axis=1)
        g[n, 328:USED] = jnp.concatenate([gc[160 * m : 160 * m + 168, 64:96] for m in range(4)], axis=1)
        g[n, USED:ROWS] = jnp.zeros((ROWS - USED, 128), F32)

    def core_reduce(bufs):
        other = pl.multiple_of((1 - at["k"]) * 256, 256)
        return send(bufs[0].at[:, pl.ds(other, 256)], bufs[1], shifted(at, k=1))

    def x_reduce(bufs):
        g, gr, h, hb, hr = bufs[:5]
        sends = []
        for by in (2, 1, 3, 0):
            start = (at["x"] + by) % 4 * 64
            value = (
                g[:, pl.ds(pl.multiple_of(at["k"] * 256 + start, 64), 64)]
                + gr[:, pl.ds(pl.multiple_of(start, 64), 64)]
            )
            if by == 0:
                h[...] = value
            else:
                hb[by - 1] = value.astype(BF16)
                sends.append(send(hb.at[by - 1], hr.at[by - 1], shifted(at, x=by)))
        return sends

    def z_reduce(bufs):
        h, hr, zs, zr = bufs[2], bufs[4], bufs[5], bufs[6]
        h[...] = h[...] + hr[0].astype(F32) + hr[1].astype(F32) + hr[2].astype(F32)
        sends = []
        for by in (3, 1, 2):
            zs[by - 1] = h[:, pl.ds(pl.multiple_of((at["zl"] + by) % 4 * 16, 16), 16)]
            sends.append(send(zs.at[by - 1], zr.at[by - 1], shifted(at, zl=by)))
        return sends

    def yz_gather(bufs, base):
        h, zr, sb = bufs[2], bufs[6], bufs[7]
        value = h[:, pl.ds(pl.multiple_of(at["zl"] * 16, 16), 16)] + zr[0] + zr[1] + zr[2]
        sb[...] = (value * (1.0 / math.sqrt(40960))).astype(BF16)
        piece = pl.multiple_of(at["k"] * 256 + at["x"] * 64 + at["zl"] * 16, 16)
        sends = []
        for n in range(2):
            slot = SLOTS[base + n]
            for dz in (3, 2, 1, 0):
                if slot == 0 and dz == 0:
                    ag[0, pl.ds(piece, 16)] = sb[0]
                else:
                    dst = ag.at[base + n, pl.ds(piece, 16)]
                    sends.append(send(sb.at[n], dst, shifted(at, y=-slot, zl=dz)))
        return sends

    def x_gather(base):
        start = pl.multiple_of(at["k"] * 256 + at["x"] * 64, 64)
        ref = ag.at[pl.ds(base, 2), pl.ds(start, 64)]
        return [send(ref, ref, shifted(at, x=by)) for by in (2, 1, 3)]

    def core_gather(base):
        ref = ag.at[pl.ds(base, 2), pl.ds(pl.multiple_of(at["k"] * 256, 256), 256)]
        return send(ref, ref, shifted(at, k=1))

    def unpack(place):
        value = ag[place].astype(F32)
        low, high = value[:328], value[328:USED]
        left = jnp.concatenate([low[:, :64], low[8:, 64:]], axis=0)
        right = jnp.concatenate(
            [high[:, :32], high[8:, 32:64], high[8:, 64:96], high[8:, 96:]], axis=0
        )
        piece = jnp.concatenate([left, right], axis=1).astype(BF16)
        return jnp.dot(piece, perm[SLOTS[place]], preferred_element_type=F32)

    weigh(SLOTS[0], chain_a[0], 0)
    weigh(SLOTS[1], chain_a[0], 1)
    a = core_reduce(chain_a)
    arrived(dy[2])
    build(2)
    dgrad(2)
    def grad_part(by):
        start = pl.multiple_of((at["zh"] + by) % 4 * CH, 8)
        return jnp.concatenate([p[0, pl.ds(start, CH)], p[1, pl.ds(start, CH)]], axis=0)

    along = {"tm": at["x"], "height": row, "chan": (at["zh"] + side) % 4 * 4 + at["y"]}
    qb[0] = grad_part(2).astype(BF16)
    z_far = send(qb.at[0], rz.at[0], along)
    qb[1] = grad_part(4 - side).astype(BF16)
    z_near = send(qb.at[1], rz.at[1], away)
    q[...] = grad_part(0)
    arrived([a])
    a = x_reduce(chain_a)
    for t in range(2):
        dsend[t : t + 1] = jnp.sum(p[t] * sx[t], axis=0, keepdims=True)
    dys = [send(dsend, dry.at[by - 1], shifted(at, y=by)) for by in (2, 1, 3)]
    weigh(SLOTS[2], chain_b[0], 0)
    weigh(SLOTS[3], chain_b[0], 1)
    b = core_reduce(chain_b)
    arrived([z_far])
    qb[2] = (grad_part(side) + rz[0].astype(F32)).astype(BF16)
    z_sum = send(qb.at[2], rz.at[2], along)
    arrived(dys)
    dmid[...] = dsend[...] + dry[0] + dry[1] + dry[2]
    dzs = [send(dmid, drz.at[by - 1], shifted(at, zh=by)) for by in (2, 1, 3)]
    arrived([b])
    b = x_reduce(chain_b)
    arrived(a)
    a = z_reduce(chain_a)
    arrived(b)
    b = z_reduce(chain_b)
    arrived(a)
    a = yz_gather(chain_a, 0)
    arrived(b)
    b = yz_gather(chain_b, 2)
    arrived(a)
    a = x_gather(0)
    arrived(b)
    b = x_gather(2)
    arrived(a)
    a = core_gather(0)
    arrived(b)
    b = core_gather(2)

    arrived([z_near, z_sum] + dzs)
    grad = q[...] + rz[1].astype(F32) + rz[2].astype(F32)
    dots = dmid[...] + drz[0] + drz[1] + drz[2]
    mine_x = f_ref[...].astype(F32)
    ct = d_ref[...].astype(F32)
    outs = []
    for t in range(2):
        rows = slice(CH * t, CH * t + CH)
        x = mine_x[rows]
        _, slope = activation(x, t, at["zh"] * 4 + at["y"])
        up = grad[rows] * slope
        r = inv[t : t + 1]
        back = r * up - x * (r * r * r * dots[t : t + 1] * (1.0 / TOTAL))
        outs.append(ct[rows] + back)
    od_ref[...] = jnp.concatenate(outs, axis=0).astype(BF16)

    arrived([a])
    wgrad[...] = unpack(0) + unpack(1)
    arrived([b])
    og_ref[...] = (wgrad[...] + unpack(2) + unpack(3)).astype(BF16)
    for copy in started:
        copy.wait_send()
    for copy, goes, _ in halo:
        pl.when(goes)(copy.wait_send)


def chain_buffers():
    return [
        pltpu.VMEM((2, ROWS, 128), F32),
        pltpu.VMEM((2, 256, 128), F32),
        pltpu.VMEM((2, 64, 128), F32),
        pltpu.VMEM((3, 2, 64, 128), BF16),
        pltpu.VMEM((3, 2, 64, 128), BF16),
        pltpu.VMEM((3, 2, 16, 128), F32),
        pltpu.VMEM((3, 2, 16, 128), F32),
        pltpu.VMEM((2, 16, 128), BF16),
    ]


def on_device(features, cotangent, conv_weight, norm_gain, norm_bias):
    chans, frames, rows, cols = features.shape
    fd = jnp.transpose(jnp.stack([features, cotangent]), (0, 2, 1, 3, 4))
    fd = fd.reshape(2 * frames * chans, rows * cols)
    vmem = pl.BlockSpec(memory_space=pltpu.VMEM)
    hbm = pl.BlockSpec(memory_space=pl.ANY)
    w = jnp.transpose(conv_weight, (1, 0, 2)).reshape(27 * chans, TOTAL)
    sums = pltpu.VMEM((2, LANES), F32)
    sums3 = pltpu.VMEM((3, 2, LANES), F32)
    cells = pltpu.VMEM((3, 48, LANES), BF16)
    grads, out = pl.pallas_call(
        kernel,
        name="unit_backward",
        out_shape=(
            jax.ShapeDtypeStruct((648, TOTAL), BF16),
            jax.ShapeDtypeStruct((48, LANES), BF16),
        ),
        in_specs=[vmem, hbm, hbm, hbm],
        out_specs=(vmem, vmem),
        scratch_shapes=[
            pltpu.VMEM((27 * CH, TOTAL), BF16),
            pltpu.VMEM((TOTAL,), F32),
            pltpu.VMEM((TOTAL,), F32),
            pltpu.VMEM((3, TOTAL, 9 * CH), F32),
            pltpu.VMEM((3, 288, 9 * CH), BF16),
            pltpu.VMEM((4, 288, 9 * CH), BF16),
            pltpu.VMEM((TOTAL, 8), F32),
            cells,
            pltpu.VMEM((4, 48, LANES), BF16),
            pltpu.VMEM((4, 4, 48, 256), BF16),
            pltpu.VMEM((4, 48, LANES), BF16),
            pltpu.VMEM((4, 4, 216, LANES), BF16),
            pltpu.VMEM((2, 96, LANES), F32),
            pltpu.VMEM((48, LANES), F32),
            cells,
            cells,
            pltpu.VMEM((2, 96, LANES), BF16),
            pltpu.VMEM((2, 96, LANES), F32),
            sums,
            sums,
            pltpu.VMEM((4, 2, LANES), F32),
            sums3,
            sums,
            sums,
            sums,
            sums3,
            sums3,
            pltpu.VMEM((648, 96), F32),
            pltpu.VMEM((4, 96, TOTAL), BF16),
            pltpu.VMEM((648, TOTAL), F32),
            pltpu.VMEM((4, ROWS, 128), BF16),
            chain_buffers(),
            chain_buffers(),
            pltpu.SemaphoreType.DMA((3,)),
            pltpu.SemaphoreType.DMA((COPIES,)),
            pltpu.SemaphoreType.DMA((COPIES,)),
        ],
        compiler_params=pltpu.CompilerParams(
            collective_id=0, has_side_effects=True, vmem_limit_bytes=40 << 20
        ),
    )(fd, w, norm_gain, norm_bias)
    result = jnp.transpose(out.reshape(frames, chans, rows, cols), (1, 0, 2, 3))
    weight_grad = jnp.transpose(grads.reshape(27, chans, TOTAL), (1, 0, 2)).astype(F32)
    return result, weight_grad


def solution(mesh):
    return jax.shard_map(
        on_device,
        mesh=mesh,
        in_specs=(
            P("chan", "tm", "height", None),
            P("chan", "tm", "height", None),
            P("chan", None, None),
            P(),
            P(),
        ),
        out_specs=(P("chan", "tm", "height", None), P("chan", None, None)),
        check_vma=False,
    )
```

```python
import functools
import math

import jax
import jax.numpy as jnp
from jax import lax
from jax.experimental import pallas as pl
from jax.experimental.pallas import tpu as pltpu
from jax.sharding import PartitionSpec as P

MESH = pl.DeviceIdType.MESH
SIZES = {"x": 4, "zl": 4, "k": 2, "zh": 4, "y": 4}
CH = 24
TOTAL = 384
LANES = 640
F32 = jnp.float32
BF16 = jnp.bfloat16


def coords():
    t = lax.axis_index("tm")
    h = lax.axis_index("height")
    c = lax.axis_index("chan")
    return {"x": t, "zl": h // 2, "k": h % 2, "zh": c // 4, "y": c % 4}


def shifted(at, **offsets):
    at = dict(at)
    for name, by in offsets.items():
        at[name] = (at[name] + (by % SIZES[name])) % SIZES[name]
    return {"tm": at["x"], "height": at["zl"] * 2 + at["k"], "chan": at["zh"] * 4 + at["y"]}


def neighbour(at, dx, dh):
    t = (at["x"] + (dx % 4)) % 4
    h = (at["zl"] * 2 + at["k"] + (dh % 8)) % 8
    return {"tm": t, "height": h, "chan": at["zh"] * 4 + at["y"]}


HALO = ((-1, 0), (0, 1), (0, -1), (-1, 1), (-1, -1))
COPIES = 96
STEPS = tuple(slice(16 * n, 16 * n + 16) for n in range(3))
SLOTS = (0, 1, 3, 2)
ROWS = 512
USED = 496


def kernel(
    fd_ref, raw_hbm, gain_hbm, bias_hbm, og_ref, od_ref,
    raw, gain_ref, bias_ref, tall, slabs, wall, gb_ref, dall, dnall, edall, fall, s9, p, q, qb, rz, act, sx, inv,
    sown, smid, sry, srz, dsend, dmid, dry, drz, gc, perm, wgrad, ag, chain_a, chain_b, lsem, ssem, rsem,
):
    f_ref, d_ref = fd_ref.at[0:48], fd_ref.at[48:96]
    at = coords()
    count = [0]
    started = []

    def send(src, dst, target):
        i = count[0]
        count[0] += 1
        copy = pltpu.make_async_remote_copy(
            src_ref=src, dst_ref=dst, send_sem=ssem.at[i], recv_sem=rsem.at[i],
            device_id=target, device_id_type=MESH,
        )
        copy.start()
        started.append(copy)
        return copy

    def arrived(copies):
        for copy in copies:
            copy.wait_recv()

    loads = [
        pltpu.make_async_copy(src, dst, lsem.at[n])
        for n, (src, dst) in enumerate(((gain_hbm, gain_ref), (bias_hbm, bias_ref), (raw_hbm, raw)))
    ]
    for copy in loads:
        copy.start()
    edall[0] = jnp.zeros((4, 48, 256), BF16)
    barrier = pltpu.get_barrier_semaphore()
    greeted = [shifted(at, zh=1), shifted(at, zh=3)]
    greeted += [neighbour(at, -dx, -dh) for dx, dh in HALO]
    greeted += [shifted(at, x=by) for by in (1, 2, 3)]
    greeted += [shifted(at, y=dy, zl=dz) for dy in range(4) for dz in range(4) if dy or dz]
    greeted.append(shifted(at, k=1))
    for one in greeted:
        pl.semaphore_signal(barrier, inc=1, device_id=one, device_id_type=MESH)

    fall[at["zh"]] = f_ref[...]
    squares = f_ref[...].astype(F32)
    squares = squares * squares
    for t in range(2):
        sown[t : t + 1] = jnp.sum(squares[CH * t : CH * t + CH], axis=0, keepdims=True)
    pl.semaphore_wait(barrier, len(greeted))

    row = at["zl"] * 2 + at["k"]
    below, above = row < 7, row > 0
    frame = send(d_ref, dnall.at[0], neighbour(at, -1, 0))
    halo = []
    for n, (dx, dh) in enumerate(HALO[1:]):
        i = count[0]
        count[0] += 1
        copy = pltpu.make_async_remote_copy(
            src_ref=d_ref.at[:, pl.ds(384 if dh == 1 else 0, 256)], dst_ref=edall.at[0, n],
            send_sem=ssem.at[i], recv_sem=rsem.at[i],
            device_id=neighbour(at, dx, dh), device_id_type=MESH,
        )
        goes, comes = (below, above) if dh == 1 else (above, below)
        pl.when(goes)(copy.start)
        halo.append((copy, goes, comes))
    fz = [
        [send(f_ref.at[rows], fall.at[at["zh"], rows], shifted(at, zh=by)) for by in (1, 3)] for rows in STEPS
    ]
    sys = [send(sown, sry.at[by - 1], shifted(at, y=by)) for by in (2, 1, 3)]
    dy = {by: [send(d_ref, dall.at[by - 1], shifted(at, y=by))] for by in (1, 3, 2)}

    loads[2].wait()
    for kt in range(3):
        tall[kt] = raw[216 * kt : 216 * kt + 216].astype(F32).T

    def slab(by):
        y = (at["y"] + by) % 4
        groups = [
            tall[kt, pl.ds(pl.multiple_of(96 * zh + y * CH, 8), CH)] for kt in range(3) for zh in range(4)
        ]
        return jnp.concatenate(groups, axis=0).astype(BF16)

    wall[0] = slab(0)
    for by in (1, 2, 3):
        slabs[by - 1] = slab(by)
    half = pl.multiple_of(at["k"] * 144, 16)
    ws = [
        send(slabs.at[by - 1, pl.ds(half, 144)], wall.at[by, pl.ds(half, 144)], shifted(at, y=by))
        for by in (2, 1, 3)
    ]

    arrived([frame])
    for by in (1, 3, 2):
        dy[by].append(send(dnall.at[0], dnall.at[by], shifted(at, y=by)))
    for copy, _, comes in halo:
        pl.when(comes)(copy.wait_recv)
    for by in (1, 3, 2):
        dy[by].append(send(edall.at[0], edall.at[by], shifted(at, y=by)))
    column = lax.broadcasted_iota(jnp.int32, (CH, LANES), 1) % 160
    left_end, right_end = column == 0, column == 159
    next_on = jnp.where(at["x"] < 3, 1.0, 0.0).astype(F32)

    def build(slot):
        for tp in range(4):
            rows = slice(CH * (tp % 2), CH * (tp % 2) + CH)
            late = tp >= 2
            if late:
                own = dnall[slot].astype(F32)[rows]
            else:
                own = (d_ref[...] if slot == 0 else dall[slot - 1]).astype(F32)[rows]
            top = edall[slot, 2 if late else 0].astype(F32)[rows]
            bottom = edall[slot, 3 if late else 1].astype(F32)[rows]
            if late:
                own, top, bottom = own * next_on, top * next_on, bottom * next_on
            moved = (
                jnp.concatenate([own[:, 160:], bottom[:, :160]], axis=1),
                own,
                jnp.concatenate([top[:, 96:], own[:, :480]], axis=1),
            )
            pieces = []
            for one in moved:
                pieces.append(jnp.where(right_end, 0.0, pltpu.roll(one, LANES - 1, 1)))
                pieces.append(one)
                pieces.append(jnp.where(left_end, 0.0, pltpu.roll(one, 1, 1)))
            s9[slot, tp] = jnp.concatenate(pieces, axis=0).astype(BF16)

    def dgrad(slot):
        for tp, (low, high) in enumerate(((192, 288), (96, 288), (0, 192), (0, 96))):
            part = jnp.dot(wall[slot, low:high], s9[slot, tp], preferred_element_type=F32)
            for n in range((high - low) // 96):
                t = n if high - low > 96 else tp // 3
                piece = part[96 * n : 96 * n + 96]
                if slot == 0 and (tp == 0 or (tp == 1 and t == 1)):
                    p[t] = piece
                else:
                    p[t] += piece

    side = 1 + 2 * at["k"]
    source = (at["zh"] + side) % 4
    away = {"tm": at["x"], "height": row, "chan": (at["zh"] + 4 - side) % 4 * 4 + at["y"]}
    fz_far = []

    def far_step(n):
        arrived(fz[n])
        ref = fall.at[source, STEPS[n]]
        fz_far.append(send(ref, ref, away))

    arrived(sys)
    smid[0] = sown[...] + sry[0] + sry[1] + sry[2]
    szs = [send(smid.at[0], smid.at[by], shifted(at, zh=by)) for by in (1, 3)]
    far_step(0)
    build(0)
    far_step(1)
    dgrad(0)
    far_step(2)
    arrived(ws)
    ref = wall.at[pl.ds(1, 3), pl.ds(half, 144)]
    wx = send(ref, ref, shifted(at, k=1))
    arrived(szs)
    szf = send(smid.at[1], srz, shifted(at, zh=1))
    loads[0].wait()
    loads[1].wait()
    pair = [ref[...].reshape(1, TOTAL) for ref in (gain_ref, bias_ref)]
    both = jnp.concatenate(pair + [jnp.zeros((6, TOTAL), F32)], axis=0)
    gb_ref[...] = both.T

    r = lax.broadcasted_iota(jnp.int32, (96, TOTAL), 0)
    lane = lax.broadcasted_iota(jnp.int32, (96, TOTAL), 1)
    group = (r >= 24).astype(jnp.int32) + (r >= 48).astype(jnp.int32) + (r >= 72).astype(jnp.int32)
    for s in range(4):
        target = r + 72 * group + CH * ((at["y"] + s) % 4)
        perm[s] = jnp.where(lane == target, 1.0, 0.0).astype(BF16)

    arrived(dy[1])
    build(1)
    arrived([wx])
    dgrad(1)
    arrived(dy[3])
    build(3)
    dgrad(3)
    arrived([szf])
    total = smid[0] + smid[1] + smid[3] + srz[...]
    inv[...] = lax.rsqrt(total * (1.0 / TOTAL) + 1e-06)

    def activation(x, t, block):
        start = pl.multiple_of(block * CH, 8)
        gain = gb_ref[pl.ds(start, CH), 0:1]
        bias = gb_ref[pl.ds(start, CH), 1:2]
        normed = x * inv[t : t + 1] * gain + bias
        sig = 0.5 * jnp.tanh(0.5 * normed) + 0.5
        return normed * sig, sig * (1.0 + normed * (1.0 - sig)) * gain

    arrived(fz_far)

    @pl.loop(0, 2)
    def _(n):
        blocks = [fall[2 * n + j].astype(F32) for j in range(2)]
        for t in range(2):
            pair, slopes = [], []
            for j in range(2):
                x = blocks[j][CH * t : CH * t + CH]
                active, slope = activation(x, t, (2 * n + j) * 4 + at["y"])
                pair.append(active)
                slopes.append(slope * x)
            start = pl.multiple_of(n * 48, 16)
            act[t, pl.ds(start, 48)] = jnp.concatenate(pair, axis=0).astype(BF16)
            sx[t, pl.ds(start, 48)] = jnp.concatenate(slopes, axis=0)

    def weigh(slot, g, n):
        for kt in range(3):
            total = None
            for t in range(2):
                part = lax.dot_general(
                    s9[slot, t + 2 - kt], act[t], (((1,), (1,)), ((), ())), preferred_element_type=F32
                )
                total = part if total is None else total + part
            gc[216 * kt : 216 * kt + 216] = total
        g[n, 0:328] = jnp.concatenate([gc[0:328, 0:64], gc[320:648, 0:64]], axis=1)
        g[n, 328:USED] = jnp.concatenate([gc[160 * m : 160 * m + 168, 64:96] for m in range(4)], axis=1)
        g[n, USED:ROWS] = jnp.zeros((ROWS - USED, 128), F32)

    def core_reduce(bufs):
        other = pl.multiple_of((1 - at["k"]) * 256, 256)
        return send(bufs[0].at[:, pl.ds(other, 256)], bufs[1], shifted(at, k=1))

    def x_reduce(bufs):
        g, gr, h, hb, hr = bufs[:5]
        sends = []
        for by in (2, 1, 3, 0):
            start = (at["x"] + by) % 4 * 64
            value = (
                g[:, pl.ds(pl.multiple_of(at["k"] * 256 + start, 64), 64)]
                + gr[:, pl.ds(pl.multiple_of(start, 64), 64)]
            )
            if by == 0:
                h[...] = value
            else:
                hb[by - 1] = value.astype(BF16)
                sends.append(send(hb.at[by - 1], hr.at[by - 1], shifted(at, x=by)))
        return sends

    def z_reduce(bufs):
        h, hr, zs, zr = bufs[2], bufs[4], bufs[5], bufs[6]
        h[...] = h[...] + hr[0].astype(F32) + hr[1].astype(F32) + hr[2].astype(F32)
        sends = []
        for by in (3, 1, 2):
            zs[by - 1] = h[:, pl.ds(pl.multiple_of((at["zl"] + by) % 4 * 16, 16), 16)]
            sends.append(send(zs.at[by - 1], zr.at[by - 1], shifted(at, zl=by)))
        return sends

    def yz_gather(bufs, base):
        h, zr, sb = bufs[2], bufs[6], bufs[7]
        value = h[:, pl.ds(pl.multiple_of(at["zl"] * 16, 16), 16)] + zr[0] + zr[1] + zr[2]
        sb[...] = (value * (1.0 / math.sqrt(40960))).astype(BF16)
        piece = pl.multiple_of(at["k"] * 256 + at["x"] * 64 + at["zl"] * 16, 16)
        sends = []
        for n in range(2):
            slot = SLOTS[base + n]
            for dz in (3, 2, 1, 0):
                if slot == 0 and dz == 0:
                    ag[0, pl.ds(piece, 16)] = sb[0]
                else:
                    dst = ag.at[base + n, pl.ds(piece, 16)]
                    sends.append(send(sb.at[n], dst, shifted(at, y=-slot, zl=dz)))
        return sends

    def x_gather(base):
        start = pl.multiple_of(at["k"] * 256 + at["x"] * 64, 64)
        ref = ag.at[pl.ds(base, 2), pl.ds(start, 64)]
        return [send(ref, ref, shifted(at, x=by)) for by in (2, 1, 3)]

    def core_gather(base):
        ref = ag.at[pl.ds(base, 2), pl.ds(pl.multiple_of(at["k"] * 256, 256), 256)]
        return send(ref, ref, shifted(at, k=1))

    def unpack(place):
        value = ag[place].astype(F32)
        low, high = value[:328], value[328:USED]
        left = jnp.concatenate([low[:, :64], low[8:, 64:]], axis=0)
        right = jnp.concatenate(
            [high[:, :32], high[8:, 32:64], high[8:, 64:96], high[8:, 96:]], axis=0
        )
        piece = jnp.concatenate([left, right], axis=1).astype(BF16)
        return jnp.dot(piece, perm[SLOTS[place]], preferred_element_type=F32)

    weigh(SLOTS[0], chain_a[0], 0)
    weigh(SLOTS[1], chain_a[0], 1)
    a = core_reduce(chain_a)
    arrived(dy[2])
    build(2)
    dgrad(2)
    def grad_part(by):
        start = pl.multiple_of((at["zh"] + by) % 4 * CH, 8)
        return jnp.concatenate([p[0, pl.ds(start, CH)], p[1, pl.ds(start, CH)]], axis=0)

    along = {"tm": at["x"], "height": row, "chan": (at["zh"] + side) % 4 * 4 + at["y"]}
    qb[0] = grad_part(2).astype(BF16)
    z_far = send(qb.at[0], rz.at[0], along)
    qb[1] = grad_part(4 - side).astype(BF16)
    z_near = send(qb.at[1], rz.at[1], away)
    q[...] = grad_part(0)
    arrived([a])
    a = x_reduce(chain_a)
    for t in range(2):
        dsend[t : t + 1] = jnp.sum(p[t] * sx[t], axis=0, keepdims=True)
    dys = [send(dsend, dry.at[by - 1], shifted(at, y=by)) for by in (2, 1, 3)]
    weigh(SLOTS[2], chain_b[0], 0)
    weigh(SLOTS[3], chain_b[0], 1)
    b = core_reduce(chain_b)
    arrived(a)
    a = z_reduce(chain_a)
    arrived(dys)
    dmid[...] = dsend[...] + dry[0] + dry[1] + dry[2]
    dzs = [send(dmid, drz.at[by - 1], shifted(at, zh=by)) for by in (2, 1, 3)]
    arrived([b])
    b = x_reduce(chain_b)
    arrived([z_far])
    qb[2] = (grad_part(side) + rz[0].astype(F32)).astype(BF16)
    z_sum = send(qb.at[2], rz.at[2], along)
    arrived(a)
    a = yz_gather(chain_a, 0)
    arrived(b)
    b = z_reduce(chain_b)
    arrived(b)
    b = yz_gather(chain_b, 2)
    arrived(a)
    a = x_gather(0)
    arrived(b)
    b = x_gather(2)
    arrived(a)
    a = core_gather(0)

    arrived([z_near, z_sum] + dzs)
    grad = q[...] + rz[1].astype(F32) + rz[2].astype(F32)
    dots = dmid[...] + drz[0] + drz[1] + drz[2]
    mine_x = f_ref[...].astype(F32)
    ct = d_ref[...].astype(F32)
    outs = []
    for t in range(2):
        rows = slice(CH * t, CH * t + CH)
        x = mine_x[rows]
        _, slope = activation(x, t, at["zh"] * 4 + at["y"])
        up = grad[rows] * slope
        r = inv[t : t + 1]
        back = r * up - x * (r * r * r * dots[t : t + 1] * (1.0 / TOTAL))
        outs.append(ct[rows] + back)
    od_ref[...] = jnp.concatenate(outs, axis=0).astype(BF16)

    arrived(b)
    b = core_gather(2)
    arrived([a])
    wgrad[...] = unpack(0) + unpack(1)
    arrived([b])
    og_ref[...] = (wgrad[...] + unpack(2) + unpack(3)).astype(BF16)
    for copy in started:
        copy.wait_send()
    for copy, goes, _ in halo:
        pl.when(goes)(copy.wait_send)


def chain_buffers():
    return [
        pltpu.VMEM((2, ROWS, 128), F32),
        pltpu.VMEM((2, 256, 128), F32),
        pltpu.VMEM((2, 64, 128), F32),
        pltpu.VMEM((3, 2, 64, 128), BF16),
        pltpu.VMEM((3, 2, 64, 128), BF16),
        pltpu.VMEM((3, 2, 16, 128), F32),
        pltpu.VMEM((3, 2, 16, 128), F32),
        pltpu.VMEM((2, 16, 128), BF16),
    ]


def on_device(features, cotangent, conv_weight, norm_gain, norm_bias):
    chans, frames, rows, cols = features.shape
    fd = jnp.transpose(jnp.stack([features, cotangent]), (0, 2, 1, 3, 4))
    fd = fd.reshape(2 * frames * chans, rows * cols)
    vmem = pl.BlockSpec(memory_space=pltpu.VMEM)
    hbm = pl.BlockSpec(memory_space=pl.ANY)
    w = jnp.transpose(conv_weight, (1, 0, 2)).reshape(27 * chans, TOTAL)
    sums = pltpu.VMEM((2, LANES), F32)
    sums3 = pltpu.VMEM((3, 2, LANES), F32)
    cells = pltpu.VMEM((3, 48, LANES), BF16)
    grads, out = pl.pallas_call(
        kernel,
        name="unit_backward",
        out_shape=(
            jax.ShapeDtypeStruct((648, TOTAL), BF16),
            jax.ShapeDtypeStruct((48, LANES), BF16),
        ),
        in_specs=[vmem, hbm, hbm, hbm],
        out_specs=(vmem, vmem),
        scratch_shapes=[
            pltpu.VMEM((27 * CH, TOTAL), BF16),
            pltpu.VMEM((TOTAL,), F32),
            pltpu.VMEM((TOTAL,), F32),
            pltpu.VMEM((3, TOTAL, 9 * CH), F32),
            pltpu.VMEM((3, 288, 9 * CH), BF16),
            pltpu.VMEM((4, 288, 9 * CH), BF16),
            pltpu.VMEM((TOTAL, 8), F32),
            cells,
            pltpu.VMEM((4, 48, LANES), BF16),
            pltpu.VMEM((4, 4, 48, 256), BF16),
            pltpu.VMEM((4, 48, LANES), BF16),
            pltpu.VMEM((4, 4, 216, LANES), BF16),
            pltpu.VMEM((2, 96, LANES), F32),
            pltpu.VMEM((48, LANES), F32),
            cells,
            cells,
            pltpu.VMEM((2, 96, LANES), BF16),
            pltpu.VMEM((2, 96, LANES), F32),
            sums,
            sums,
            pltpu.VMEM((4, 2, LANES), F32),
            sums3,
            sums,
            sums,
            sums,
            sums3,
            sums3,
            pltpu.VMEM((648, 96), F32),
            pltpu.VMEM((4, 96, TOTAL), BF16),
            pltpu.VMEM((648, TOTAL), F32),
            pltpu.VMEM((4, ROWS, 128), BF16),
            chain_buffers(),
            chain_buffers(),
            pltpu.SemaphoreType.DMA((3,)),
            pltpu.SemaphoreType.DMA((COPIES,)),
            pltpu.SemaphoreType.DMA((COPIES,)),
        ],
        compiler_params=pltpu.CompilerParams(
            collective_id=0, has_side_effects=True, vmem_limit_bytes=40 << 20
        ),
    )(fd, w, norm_gain, norm_bias)
    result = jnp.transpose(out.reshape(frames, chans, rows, cols), (1, 0, 2, 3))
    weight_grad = jnp.transpose(grads.reshape(27, chans, TOTAL), (1, 0, 2)).astype(F32)
    return result, weight_grad


def solution(mesh):
    return jax.shard_map(
        on_device,
        mesh=mesh,
        in_specs=(
            P("chan", "tm", "height", None),
            P("chan", "tm", "height", None),
            P("chan", None, None),
            P(),
            P(),
        ),
        out_specs=(P("chan", "tm", "height", None), P("chan", None, None)),
        check_vma=False,
    )
```

```python
import functools
import math

import jax
import jax.numpy as jnp
from jax import lax
from jax.experimental import pallas as pl
from jax.experimental.pallas import tpu as pltpu
from jax.sharding import PartitionSpec as P

MESH = pl.DeviceIdType.MESH
SIZES = {"x": 4, "zl": 4, "k": 2, "zh": 4, "y": 4}
CH = 24
TOTAL = 384
LANES = 640
F32 = jnp.float32
BF16 = jnp.bfloat16


def coords():
    t = lax.axis_index("tm")
    h = lax.axis_index("height")
    c = lax.axis_index("chan")
    return {"x": t, "zl": h // 2, "k": h % 2, "zh": c // 4, "y": c % 4}


def shifted(at, **offsets):
    at = dict(at)
    for name, by in offsets.items():
        at[name] = (at[name] + (by % SIZES[name])) % SIZES[name]
    return {"tm": at["x"], "height": at["zl"] * 2 + at["k"], "chan": at["zh"] * 4 + at["y"]}


def neighbour(at, dx, dh):
    t = (at["x"] + (dx % 4)) % 4
    h = (at["zl"] * 2 + at["k"] + (dh % 8)) % 8
    return {"tm": t, "height": h, "chan": at["zh"] * 4 + at["y"]}


HALO = ((-1, 0), (0, 1), (0, -1), (-1, 1), (-1, -1))
COPIES = 96
STEPS = tuple(slice(16 * n, 16 * n + 16) for n in range(3))
SLOTS = (0, 1, 3, 2)
ROWS = 512
USED = 496


def kernel(
    fd_ref, raw_hbm, gain_hbm, bias_hbm, og_ref, od_ref,
    raw, gain_ref, bias_ref, tall, slabs, wall, gb_ref, dall, dnall, edall, joint, fall, s9, p, q, qb, rz, act, sx, inv,
    sown, smid, sry, srz, dsend, dmid, dry, drz, gc, perm, wgrad, ag, chain_a, chain_b, lsem, ssem, rsem,
):
    f_ref, d_ref = fd_ref.at[0:48], fd_ref.at[48:96]
    at = coords()
    count = [0]
    started = []

    def send(src, dst, target):
        i = count[0]
        count[0] += 1
        copy = pltpu.make_async_remote_copy(
            src_ref=src, dst_ref=dst, send_sem=ssem.at[i], recv_sem=rsem.at[i],
            device_id=target, device_id_type=MESH,
        )
        copy.start()
        started.append(copy)
        return copy

    def arrived(copies):
        for copy in copies:
            copy.wait_recv()

    loads = [
        pltpu.make_async_copy(src, dst, lsem.at[n])
        for n, (src, dst) in enumerate(((gain_hbm, gain_ref), (bias_hbm, bias_ref), (raw_hbm, raw)))
    ]
    for copy in loads:
        copy.start()
    edall[...] = jnp.zeros((4, 48, 256), BF16)
    barrier = pltpu.get_barrier_semaphore()
    greeted = [shifted(at, zh=1), shifted(at, zh=3)]
    greeted += [neighbour(at, -dx, -dh) for dx, dh in HALO]
    greeted += [shifted(at, x=by) for by in (1, 2, 3)]
    greeted += [shifted(at, y=dy, zl=dz) for dy in range(4) for dz in range(4) if dy or dz]
    greeted.append(shifted(at, k=1))
    for one in greeted:
        pl.semaphore_signal(barrier, inc=1, device_id=one, device_id_type=MESH)

    fall[at["zh"]] = f_ref[...]
    squares = f_ref[...].astype(F32)
    squares = squares * squares
    for t in range(2):
        sown[t : t + 1] = jnp.sum(squares[CH * t : CH * t + CH], axis=0, keepdims=True)
    pl.semaphore_wait(barrier, len(greeted))

    row = at["zl"] * 2 + at["k"]
    below, above = row < 7, row > 0
    frame = send(d_ref, dnall.at[0], neighbour(at, -1, 0))
    halo = []
    for n, (dx, dh) in enumerate(HALO[1:]):
        i = count[0]
        count[0] += 1
        copy = pltpu.make_async_remote_copy(
            src_ref=d_ref.at[:, pl.ds(384 if dh == 1 else 0, 256)], dst_ref=edall.at[n],
            send_sem=ssem.at[i], recv_sem=rsem.at[i],
            device_id=neighbour(at, dx, dh), device_id_type=MESH,
        )
        goes, comes = (below, above) if dh == 1 else (above, below)
        pl.when(goes)(copy.start)
        halo.append((copy, goes, comes))
    fz = [
        [send(f_ref.at[rows], fall.at[at["zh"], rows], shifted(at, zh=by)) for by in (1, 3)] for rows in STEPS
    ]
    sys = [send(sown, sry.at[by - 1], shifted(at, y=by)) for by in (2, 1, 3)]
    dy = {by: [send(d_ref, dall.at[by - 1], shifted(at, y=by))] for by in (1, 3, 2)}

    loads[2].wait()
    for kt in range(3):
        tall[kt] = raw[216 * kt : 216 * kt + 216].astype(F32).T

    def slab(by):
        y = (at["y"] + by) % 4
        groups = [
            tall[kt, pl.ds(pl.multiple_of(96 * zh + y * CH, 8), CH)] for kt in range(3) for zh in range(4)
        ]
        return jnp.concatenate(groups, axis=0).astype(BF16)

    wall[0] = slab(0)
    for by in (1, 2, 3):
        slabs[by - 1] = slab(by)
    half = pl.multiple_of(at["k"] * 144, 16)
    ws = [
        send(slabs.at[by - 1, pl.ds(half, 144)], wall.at[by, pl.ds(half, 144)], shifted(at, y=by))
        for by in (2, 1, 3)
    ]

    arrived([frame])
    for by in (1, 3, 2):
        dy[by].append(send(dnall.at[0], dnall.at[by], shifted(at, y=by)))
    for copy, _, comes in halo:
        pl.when(comes)(copy.wait_recv)
    for late in range(2):
        top, bottom = edall[2 * late].astype(F32), edall[2 * late + 1].astype(F32)
        joined = [top[:, 96:], bottom[:, :160], jnp.zeros((48, 64), F32)]
        joint[0, late] = jnp.concatenate(joined, axis=1).astype(BF16)
    for by in (1, 3, 2):
        dy[by].append(send(joint.at[0], joint.at[by], shifted(at, y=by)))
    column = lax.broadcasted_iota(jnp.int32, (CH, LANES), 1) % 160
    left_end, right_end = column == 0, column == 159
    next_on = jnp.where(at["x"] < 3, 1.0, 0.0).astype(F32)

    def build(slot):
        for tp in range(4):
            rows = slice(CH * (tp % 2), CH * (tp % 2) + CH)
            late = tp >= 2
            if late:
                own = dnall[slot].astype(F32)[rows]
            else:
                own = (d_ref[...] if slot == 0 else dall[slot - 1]).astype(F32)[rows]
            edge = joint[slot, tp // 2].astype(F32)[rows]
            top, bottom = edge[:, :160], edge[:, 160:320]
            if late:
                own, top, bottom = own * next_on, top * next_on, bottom * next_on
            moved = (
                jnp.concatenate([own[:, 160:], bottom], axis=1),
                own,
                jnp.concatenate([top, own[:, :480]], axis=1),
            )
            pieces = []
            for one in moved:
                pieces.append(jnp.where(right_end, 0.0, pltpu.roll(one, LANES - 1, 1)))
                pieces.append(one)
                pieces.append(jnp.where(left_end, 0.0, pltpu.roll(one, 1, 1)))
            s9[slot, tp] = jnp.concatenate(pieces, axis=0).astype(BF16)

    def dgrad(slot):
        for tp, (low, high) in enumerate(((192, 288), (96, 288), (0, 192), (0, 96))):
            part = jnp.dot(wall[slot, low:high], s9[slot, tp], preferred_element_type=F32)
            for n in range((high - low) // 96):
                t = n if high - low > 96 else tp // 3
                piece = part[96 * n : 96 * n + 96]
                if slot == 0 and (tp == 0 or (tp == 1 and t == 1)):
                    p[t] = piece
                else:
                    p[t] += piece

    side = 1 + 2 * at["k"]
    source = (at["zh"] + side) % 4
    away = {"tm": at["x"], "height": row, "chan": (at["zh"] + 4 - side) % 4 * 4 + at["y"]}
    fz_far = []

    def far_step(n):
        arrived(fz[n])
        ref = fall.at[source, STEPS[n]]
        fz_far.append(send(ref, ref, away))

    arrived(sys)
    smid[0] = sown[...] + sry[0] + sry[1] + sry[2]
    szs = [send(smid.at[0], smid.at[by], shifted(at, zh=by)) for by in (1, 3)]
    far_step(0)
    build(0)
    far_step(1)
    dgrad(0)
    far_step(2)
    arrived(ws)
    ref = wall.at[pl.ds(1, 3), pl.ds(half, 144)]
    wx = send(ref, ref, shifted(at, k=1))
    arrived(szs)
    szf = send(smid.at[1], srz, shifted(at, zh=1))
    loads[0].wait()
    loads[1].wait()
    pair = [ref[...].reshape(1, TOTAL) for ref in (gain_ref, bias_ref)]
    both = jnp.concatenate(pair + [jnp.zeros((6, TOTAL), F32)], axis=0)
    gb_ref[...] = both.T

    r = lax.broadcasted_iota(jnp.int32, (96, TOTAL), 0)
    lane = lax.broadcasted_iota(jnp.int32, (96, TOTAL), 1)
    group = (r >= 24).astype(jnp.int32) + (r >= 48).astype(jnp.int32) + (r >= 72).astype(jnp.int32)
    for s in range(4):
        target = r + 72 * group + CH * ((at["y"] + s) % 4)
        perm[s] = jnp.where(lane == target, 1.0, 0.0).astype(BF16)

    arrived(dy[1])
    build(1)
    arrived([wx])
    dgrad(1)
    arrived(dy[3])
    build(3)
    dgrad(3)
    arrived([szf])
    total = smid[0] + smid[1] + smid[3] + srz[...]
    inv[...] = lax.rsqrt(total * (1.0 / TOTAL) + 1e-06)

    def activation(x, t, block):
        start = pl.multiple_of(block * CH, 8)
        gain = gb_ref[pl.ds(start, CH), 0:1]
        bias = gb_ref[pl.ds(start, CH), 1:2]
        normed = x * inv[t : t + 1] * gain + bias
        sig = 0.5 * jnp.tanh(0.5 * normed) + 0.5
        return normed * sig, sig * (1.0 + normed * (1.0 - sig)) * gain

    arrived(fz_far)

    @pl.loop(0, 2)
    def _(n):
        blocks = [fall[2 * n + j].astype(F32) for j in range(2)]
        for t in range(2):
            pair, slopes = [], []
            for j in range(2):
                x = blocks[j][CH * t : CH * t + CH]
                active, slope = activation(x, t, (2 * n + j) * 4 + at["y"])
                pair.append(active)
                slopes.append(slope * x)
            start = pl.multiple_of(n * 48, 16)
            act[t, pl.ds(start, 48)] = jnp.concatenate(pair, axis=0).astype(BF16)
            sx[t, pl.ds(start, 48)] = jnp.concatenate(slopes, axis=0)

    def weigh(slot, g, n):
        for kt in range(3):
            total = None
            for t in range(2):
                part = lax.dot_general(
                    s9[slot, t + 2 - kt], act[t], (((1,), (1,)), ((), ())), preferred_element_type=F32
                )
                total = part if total is None else total + part
            gc[216 * kt : 216 * kt + 216] = total
        g[n, 0:328] = jnp.concatenate([gc[0:328, 0:64], gc[320:648, 0:64]], axis=1)
        g[n, 328:USED] = jnp.concatenate([gc[160 * m : 160 * m + 168, 64:96] for m in range(4)], axis=1)
        g[n, USED:ROWS] = jnp.zeros((ROWS - USED, 128), F32)

    def core_reduce(bufs):
        other = pl.multiple_of((1 - at["k"]) * 256, 256)
        return send(bufs[0].at[:, pl.ds(other, 256)], bufs[1], shifted(at, k=1))

    def x_reduce(bufs):
        g, gr, h, hb, hr = bufs[:5]
        sends = []
        for by in (2, 1, 3, 0):
            start = (at["x"] + by) % 4 * 64
            value = (
                g[:, pl.ds(pl.multiple_of(at["k"] * 256 + start, 64), 64)]
                + gr[:, pl.ds(pl.multiple_of(start, 64), 64)]
            )
            if by == 0:
                h[...] = value
            else:
                hb[by - 1] = value.astype(BF16)
                sends.append(send(hb.at[by - 1], hr.at[by - 1], shifted(at, x=by)))
        return sends

    def z_reduce(bufs):
        h, hr, zs, zr = bufs[2], bufs[4], bufs[5], bufs[6]
        h[...] = h[...] + hr[0].astype(F32) + hr[1].astype(F32) + hr[2].astype(F32)
        sends = []
        for by in (3, 1, 2):
            zs[by - 1] = h[:, pl.ds(pl.multiple_of((at["zl"] + by) % 4 * 16, 16), 16)]
            sends.append(send(zs.at[by - 1], zr.at[by - 1], shifted(at, zl=by)))
        return sends

    def yz_gather(bufs, base):
        h, zr, sb = bufs[2], bufs[6], bufs[7]
        value = h[:, pl.ds(pl.multiple_of(at["zl"] * 16, 16), 16)] + zr[0] + zr[1] + zr[2]
        sb[...] = (value * (1.0 / math.sqrt(40960))).astype(BF16)
        piece = pl.multiple_of(at["k"] * 256 + at["x"] * 64 + at["zl"] * 16, 16)
        sends = []
        for n in range(2):
            slot = SLOTS[base + n]
            for dz in (3, 2, 1, 0):
                if slot == 0 and dz == 0:
                    ag[0, pl.ds(piece, 16)] = sb[0]
                else:
                    dst = ag.at[base + n, pl.ds(piece, 16)]
                    sends.append(send(sb.at[n], dst, shifted(at, y=-slot, zl=dz)))
        return sends

    def x_gather(base):
        start = pl.multiple_of(at["k"] * 256 + at["x"] * 64, 64)
        ref = ag.at[pl.ds(base, 2), pl.ds(start, 64)]
        return [send(ref, ref, shifted(at, x=by)) for by in (2, 1, 3)]

    def core_gather(base):
        ref = ag.at[pl.ds(base, 2), pl.ds(pl.multiple_of(at["k"] * 256, 256), 256)]
        return send(ref, ref, shifted(at, k=1))

    def unpack(place):
        value = ag[place].astype(F32)
        low, high = value[:328], value[328:USED]
        left = jnp.concatenate([low[:, :64], low[8:, 64:]], axis=0)
        right = jnp.concatenate(
            [high[:, :32], high[8:, 32:64], high[8:, 64:96], high[8:, 96:]], axis=0
        )
        piece = jnp.concatenate([left, right], axis=1).astype(BF16)
        return jnp.dot(piece, perm[SLOTS[place]], preferred_element_type=F32)

    weigh(SLOTS[0], chain_a[0], 0)
    weigh(SLOTS[1], chain_a[0], 1)
    a = core_reduce(chain_a)
    arrived(dy[2])
    build(2)
    dgrad(2)
    def grad_part(by):
        start = pl.multiple_of((at["zh"] + by) % 4 * CH, 8)
        return jnp.concatenate([p[0, pl.ds(start, CH)], p[1, pl.ds(start, CH)]], axis=0)

    along = {"tm": at["x"], "height": row, "chan": (at["zh"] + side) % 4 * 4 + at["y"]}
    qb[0] = grad_part(2).astype(BF16)
    z_far = send(qb.at[0], rz.at[0], along)
    qb[1] = grad_part(4 - side).astype(BF16)
    z_near = send(qb.at[1], rz.at[1], away)
    q[...] = grad_part(0)
    arrived([a])
    a = x_reduce(chain_a)
    for t in range(2):
        dsend[t : t + 1] = jnp.sum(p[t] * sx[t], axis=0, keepdims=True)
    dys = [send(dsend, dry.at[by - 1], shifted(at, y=by)) for by in (2, 1, 3)]
    weigh(SLOTS[2], chain_b[0], 0)
    weigh(SLOTS[3], chain_b[0], 1)
    b = core_reduce(chain_b)
    arrived(a)
    a = z_reduce(chain_a)
    arrived(dys)
    dmid[...] = dsend[...] + dry[0] + dry[1] + dry[2]
    dzs = [send(dmid, drz.at[by - 1], shifted(at, zh=by)) for by in (2, 1, 3)]
    arrived([b])
    b = x_reduce(chain_b)
    arrived([z_far])
    qb[2] = (grad_part(side) + rz[0].astype(F32)).astype(BF16)
    z_sum = send(qb.at[2], rz.at[2], along)
    arrived(a)
    a = yz_gather(chain_a, 0)
    arrived(b)
    b = z_reduce(chain_b)
    arrived(b)
    b = yz_gather(chain_b, 2)
    arrived(a)
    a = x_gather(0)
    arrived(b)
    b = x_gather(2)
    arrived(a)
    a = core_gather(0)

    arrived([z_near, z_sum] + dzs)
    grad = q[...] + rz[1].astype(F32) + rz[2].astype(F32)
    dots = dmid[...] + drz[0] + drz[1] + drz[2]
    mine_x = f_ref[...].astype(F32)
    ct = d_ref[...].astype(F32)
    outs = []
    for t in range(2):
        rows = slice(CH * t, CH * t + CH)
        x = mine_x[rows]
        _, slope = activation(x, t, at["zh"] * 4 + at["y"])
        up = grad[rows] * slope
        r = inv[t : t + 1]
        back = r * up - x * (r * r * r * dots[t : t + 1] * (1.0 / TOTAL))
        outs.append(ct[rows] + back)
    od_ref[...] = jnp.concatenate(outs, axis=0).astype(BF16)

    arrived(b)
    b = core_gather(2)
    arrived([a])
    wgrad[...] = unpack(0) + unpack(1)
    arrived([b])
    og_ref[...] = (wgrad[...] + unpack(2) + unpack(3)).astype(BF16)
    for copy in started:
        copy.wait_send()
    for copy, goes, _ in halo:
        pl.when(goes)(copy.wait_send)


def chain_buffers():
    return [
        pltpu.VMEM((2, ROWS, 128), F32),
        pltpu.VMEM((2, 256, 128), F32),
        pltpu.VMEM((2, 64, 128), F32),
        pltpu.VMEM((3, 2, 64, 128), BF16),
        pltpu.VMEM((3, 2, 64, 128), BF16),
        pltpu.VMEM((3, 2, 16, 128), F32),
        pltpu.VMEM((3, 2, 16, 128), F32),
        pltpu.VMEM((2, 16, 128), BF16),
    ]


def on_device(features, cotangent, conv_weight, norm_gain, norm_bias):
    chans, frames, rows, cols = features.shape
    fd = jnp.transpose(jnp.stack([features, cotangent]), (0, 2, 1, 3, 4))
    fd = fd.reshape(2 * frames * chans, rows * cols)
    vmem = pl.BlockSpec(memory_space=pltpu.VMEM)
    hbm = pl.BlockSpec(memory_space=pl.ANY)
    w = jnp.transpose(conv_weight, (1, 0, 2)).reshape(27 * chans, TOTAL)
    sums = pltpu.VMEM((2, LANES), F32)
    sums3 = pltpu.VMEM((3, 2, LANES), F32)
    cells = pltpu.VMEM((3, 48, LANES), BF16)
    grads, out = pl.pallas_call(
        kernel,
        name="unit_backward",
        out_shape=(
            jax.ShapeDtypeStruct((648, TOTAL), BF16),
            jax.ShapeDtypeStruct((48, LANES), BF16),
        ),
        in_specs=[vmem, hbm, hbm, hbm],
        out_specs=(vmem, vmem),
        scratch_shapes=[
            pltpu.VMEM((27 * CH, TOTAL), BF16),
            pltpu.VMEM((TOTAL,), F32),
            pltpu.VMEM((TOTAL,), F32),
            pltpu.VMEM((3, TOTAL, 9 * CH), F32),
            pltpu.VMEM((3, 288, 9 * CH), BF16),
            pltpu.VMEM((4, 288, 9 * CH), BF16),
            pltpu.VMEM((TOTAL, 8), F32),
            cells,
            pltpu.VMEM((4, 48, LANES), BF16),
            pltpu.VMEM((4, 48, 256), BF16),
            pltpu.VMEM((4, 2, 48, 384), BF16),
            pltpu.VMEM((4, 48, LANES), BF16),
            pltpu.VMEM((4, 4, 216, LANES), BF16),
            pltpu.VMEM((2, 96, LANES), F32),
            pltpu.VMEM((48, LANES), F32),
            cells,
            cells,
            pltpu.VMEM((2, 96, LANES), BF16),
            pltpu.VMEM((2, 96, LANES), F32),
            sums,
            sums,
            pltpu.VMEM((4, 2, LANES), F32),
            sums3,
            sums,
            sums,
            sums,
            sums3,
            sums3,
            pltpu.VMEM((648, 96), F32),
            pltpu.VMEM((4, 96, TOTAL), BF16),
            pltpu.VMEM((648, TOTAL), F32),
            pltpu.VMEM((4, ROWS, 128), BF16),
            chain_buffers(),
            chain_buffers(),
            pltpu.SemaphoreType.DMA((3,)),
            pltpu.SemaphoreType.DMA((COPIES,)),
            pltpu.SemaphoreType.DMA((COPIES,)),
        ],
        compiler_params=pltpu.CompilerParams(
            collective_id=0, has_side_effects=True, vmem_limit_bytes=40 << 20
        ),
    )(fd, w, norm_gain, norm_bias)
    result = jnp.transpose(out.reshape(frames, chans, rows, cols), (1, 0, 2, 3))
    weight_grad = jnp.transpose(grads.reshape(27, chans, TOTAL), (1, 0, 2)).astype(F32)
    return result, weight_grad


def solution(mesh):
    return jax.shard_map(
        on_device,
        mesh=mesh,
        in_specs=(
            P("chan", "tm", "height", None),
            P("chan", "tm", "height", None),
            P("chan", None, None),
            P(),
            P(),
        ),
        out_specs=(P("chan", "tm", "height", None), P("chan", None, None)),
        check_vma=False,
    )
```

```python
import functools
import math

import jax
import jax.numpy as jnp
from jax import lax
from jax.experimental import pallas as pl
from jax.experimental.pallas import tpu as pltpu
from jax.sharding import PartitionSpec as P

MESH = pl.DeviceIdType.MESH
SIZES = {"x": 4, "zl": 4, "k": 2, "zh": 4, "y": 4}
CH = 24
TOTAL = 384
LANES = 640
F32 = jnp.float32
BF16 = jnp.bfloat16


def coords():
    t = lax.axis_index("tm")
    h = lax.axis_index("height")
    c = lax.axis_index("chan")
    return {"x": t, "zl": h // 2, "k": h % 2, "zh": c // 4, "y": c % 4}


def shifted(at, **offsets):
    at = dict(at)
    for name, by in offsets.items():
        at[name] = (at[name] + (by % SIZES[name])) % SIZES[name]
    return {"tm": at["x"], "height": at["zl"] * 2 + at["k"], "chan": at["zh"] * 4 + at["y"]}


def neighbour(at, dx, dh):
    t = (at["x"] + (dx % 4)) % 4
    h = (at["zl"] * 2 + at["k"] + (dh % 8)) % 8
    return {"tm": t, "height": h, "chan": at["zh"] * 4 + at["y"]}


HALO = ((-1, 0), (0, 1), (0, -1), (-1, 1), (-1, -1))
COPIES = 96
STEPS = tuple(slice(16 * n, 16 * n + 16) for n in range(3))
SLOTS = (0, 1, 3, 2)
ROWS = 512
USED = 496


def kernel(
    fd_ref, raw_hbm, gain_hbm, bias_hbm, og_ref, od_ref,
    raw, gain_ref, bias_ref, tall, slabs, wall, gb_ref, dall, dnall, edall, fall, s9, p, q, qb, rz, act, sx, inv,
    sown, smid, sry, srz, dsend, dmid, dry, drz, gc, perm, wgrad, ag, chain_a, chain_b, lsem, ssem, rsem,
):
    f_ref, d_ref = fd_ref.at[0:48], fd_ref.at[48:96]
    at = coords()
    count = [0]
    started = []

    def send(src, dst, target):
        i = count[0]
        count[0] += 1
        copy = pltpu.make_async_remote_copy(
            src_ref=src, dst_ref=dst, send_sem=ssem.at[i], recv_sem=rsem.at[i],
            device_id=target, device_id_type=MESH,
        )
        copy.start()
        started.append(copy)
        return copy

    def arrived(copies):
        for copy in copies:
            copy.wait_recv()

    loads = [
        pltpu.make_async_copy(src, dst, lsem.at[n])
        for n, (src, dst) in enumerate(((gain_hbm, gain_ref), (bias_hbm, bias_ref), (raw_hbm, raw)))
    ]
    for copy in loads:
        copy.start()
    edall[0] = jnp.zeros((4, 48, 256), BF16)
    barrier = pltpu.get_barrier_semaphore()
    greeted = [shifted(at, zh=1), shifted(at, zh=3)]
    greeted += [neighbour(at, -dx, -dh) for dx, dh in HALO]
    greeted += [shifted(at, x=by) for by in (1, 2, 3)]
    greeted += [shifted(at, y=dy, zl=dz) for dy in range(4) for dz in range(4) if dy or dz]
    greeted.append(shifted(at, k=1))
    for one in greeted:
        pl.semaphore_signal(barrier, inc=1, device_id=one, device_id_type=MESH)

    fall[at["zh"]] = f_ref[...]
    squares = f_ref[...].astype(F32)
    squares = squares * squares
    for t in range(2):
        sown[t : t + 1] = jnp.sum(squares[CH * t : CH * t + CH], axis=0, keepdims=True)
    pl.semaphore_wait(barrier, len(greeted))

    row = at["zl"] * 2 + at["k"]
    below, above = row < 7, row > 0
    frame = send(d_ref, dnall.at[0], neighbour(at, -1, 0))
    halo = []
    for n, (dx, dh) in enumerate(HALO[1:]):
        i = count[0]
        count[0] += 1
        copy = pltpu.make_async_remote_copy(
            src_ref=d_ref.at[:, pl.ds(384 if dh == 1 else 0, 256)], dst_ref=edall.at[0, n],
            send_sem=ssem.at[i], recv_sem=rsem.at[i],
            device_id=neighbour(at, dx, dh), device_id_type=MESH,
        )
        goes, comes = (below, above) if dh == 1 else (above, below)
        pl.when(goes)(copy.start)
        halo.append((copy, goes, comes))
    fz = [
        [send(f_ref.at[rows], fall.at[at["zh"], rows], shifted(at, zh=by)) for by in (1, 3)] for rows in STEPS
    ]
    sys = [send(sown, sry.at[by - 1], shifted(at, y=by)) for by in (2, 1, 3)]
    dy = {by: [send(d_ref, dall.at[by - 1], shifted(at, y=by))] for by in (1, 3, 2)}

    loads[2].wait()
    for kt in range(3):
        tall[kt] = raw[216 * kt : 216 * kt + 216].astype(F32).T

    def slab(by):
        y = (at["y"] + by) % 4
        groups = [
            tall[kt, pl.ds(pl.multiple_of(96 * zh + y * CH, 8), CH)] for kt in range(3) for zh in range(4)
        ]
        return jnp.concatenate(groups, axis=0).astype(BF16)

    wall[0] = slab(0)
    for by in (1, 2, 3):
        slabs[by - 1] = slab(by)
    half = pl.multiple_of(at["k"] * 144, 16)
    ws = [
        send(slabs.at[by - 1, pl.ds(half, 144)], wall.at[by, pl.ds(half, 144)], shifted(at, y=by))
        for by in (2, 1, 3)
    ]

    arrived([frame])
    for by in (1, 3, 2):
        dy[by].append(send(dnall.at[0], dnall.at[by], shifted(at, y=by)))
    for copy, _, comes in halo:
        pl.when(comes)(copy.wait_recv)
    for by in (1, 3, 2):
        dy[by].append(send(edall.at[0], edall.at[by], shifted(at, y=by)))
    column = lax.broadcasted_iota(jnp.int32, (CH, LANES), 1) % 160
    left_end, right_end = column == 0, column == 159
    next_on = jnp.where(at["x"] < 3, 1.0, 0.0).astype(F32)

    def build(slot):
        for tp in range(4):
            rows = slice(CH * (tp % 2), CH * (tp % 2) + CH)
            late = tp >= 2
            if late:
                own = dnall[slot].astype(F32)[rows]
            else:
                own = (d_ref[...] if slot == 0 else dall[slot - 1]).astype(F32)[rows]
            top = edall[slot, 2 if late else 0].astype(F32)[rows]
            bottom = edall[slot, 3 if late else 1].astype(F32)[rows]
            if late:
                own, top, bottom = own * next_on, top * next_on, bottom * next_on
            moved = (
                jnp.concatenate([own[:, 160:], bottom[:, :160]], axis=1),
                own,
                jnp.concatenate([top[:, 96:], own[:, :480]], axis=1),
            )
            pieces = []
            for one in moved:
                pieces.append(jnp.where(right_end, 0.0, pltpu.roll(one, LANES - 1, 1)))
                pieces.append(one)
                pieces.append(jnp.where(left_end, 0.0, pltpu.roll(one, 1, 1)))
            s9[slot, tp] = jnp.concatenate(pieces, axis=0).astype(BF16)

    def dgrad(slot):
        for tp, (low, high) in enumerate(((192, 288), (96, 288), (0, 192), (0, 96))):
            part = jnp.dot(wall[slot, low:high], s9[slot, tp], preferred_element_type=F32)
            for n in range((high - low) // 96):
                t = n if high - low > 96 else tp // 3
                piece = part[96 * n : 96 * n + 96]
                if slot == 0 and (tp == 0 or (tp == 1 and t == 1)):
                    p[t] = piece
                else:
                    p[t] += piece

    side = 1 + 2 * at["k"]
    source = (at["zh"] + side) % 4
    away = {"tm": at["x"], "height": row, "chan": (at["zh"] + 4 - side) % 4 * 4 + at["y"]}
    fz_far = []

    def far_step(n):
        arrived(fz[n])
        ref = fall.at[source, STEPS[n]]
        fz_far.append(send(ref, ref, away))

    arrived(sys)
    smid[0] = sown[...] + sry[0] + sry[1] + sry[2]
    szs = [send(smid.at[0], smid.at[by], shifted(at, zh=by)) for by in (1, 3)]
    far_step(0)
    build(0)
    far_step(1)
    dgrad(0)
    far_step(2)
    arrived(ws)
    ref = wall.at[pl.ds(1, 3), pl.ds(half, 144)]
    wx = send(ref, ref, shifted(at, k=1))
    arrived(szs)
    szf = send(smid.at[1], srz, shifted(at, zh=1))
    loads[0].wait()
    loads[1].wait()
    pair = [ref[...].reshape(1, TOTAL) for ref in (gain_ref, bias_ref)]
    both = jnp.concatenate(pair + [jnp.zeros((6, TOTAL), F32)], axis=0)
    gb_ref[...] = both.T

    r = lax.broadcasted_iota(jnp.int32, (96, TOTAL), 0)
    lane = lax.broadcasted_iota(jnp.int32, (96, TOTAL), 1)
    group = (r >= 24).astype(jnp.int32) + (r >= 48).astype(jnp.int32) + (r >= 72).astype(jnp.int32)
    for s in range(4):
        target = r + 72 * group + CH * ((at["y"] + s) % 4)
        perm[s] = jnp.where(lane == target, 1.0, 0.0).astype(BF16)

    arrived(dy[1])
    build(1)
    arrived([wx])
    dgrad(1)
    arrived(dy[3])
    build(3)
    dgrad(3)
    arrived([szf])
    total = smid[0] + smid[1] + smid[3] + srz[...]
    inv[...] = lax.rsqrt(total * (1.0 / TOTAL) + 1e-06)

    def activation(x, t, block):
        start = pl.multiple_of(block * CH, 8)
        gain = gb_ref[pl.ds(start, CH), 0:1]
        bias = gb_ref[pl.ds(start, CH), 1:2]
        normed = x * inv[t : t + 1] * gain + bias
        sig = 0.5 * jnp.tanh(0.5 * normed) + 0.5
        return normed * sig, sig * (1.0 + normed * (1.0 - sig)) * gain

    arrived(fz_far)

    @pl.loop(0, 2)
    def _(n):
        blocks = [fall[2 * n + j].astype(F32) for j in range(2)]
        for t in range(2):
            pair, slopes = [], []
            for j in range(2):
                x = blocks[j][CH * t : CH * t + CH]
                active, slope = activation(x, t, (2 * n + j) * 4 + at["y"])
                pair.append(active)
                slopes.append(slope * x)
            start = pl.multiple_of(n * 48, 16)
            act[t, pl.ds(start, 48)] = jnp.concatenate(pair, axis=0).astype(BF16)
            sx[t, pl.ds(start, 48)] = jnp.concatenate(slopes, axis=0)

    def weigh(slot, g, n):
        for kt in range(3):
            total = None
            for t in range(2):
                part = lax.dot_general(
                    s9[slot, t + 2 - kt], act[t], (((1,), (1,)), ((), ())), preferred_element_type=F32
                )
                total = part if total is None else total + part
            gc[216 * kt : 216 * kt + 216] = total
        g[n, 0:328] = jnp.concatenate([gc[0:328, 0:64], gc[320:648, 0:64]], axis=1)
        g[n, 328:USED] = jnp.concatenate([gc[160 * m : 160 * m + 168, 64:96] for m in range(4)], axis=1)
        g[n, USED:ROWS] = jnp.zeros((ROWS - USED, 128), F32)

    def core_reduce(bufs):
        other = pl.multiple_of((1 - at["k"]) * 256, 256)
        return send(bufs[0].at[:, pl.ds(other, 256)], bufs[1], shifted(at, k=1))

    def x_reduce(bufs):
        g, gr, h, hb, hr = bufs[:5]
        sends = []
        for by in (2, 1, 3, 0):
            start = (at["x"] + by) % 4 * 64
            value = (
                g[:, pl.ds(pl.multiple_of(at["k"] * 256 + start, 64), 64)]
                + gr[:, pl.ds(pl.multiple_of(start, 64), 64)]
            )
            if by == 0:
                h[...] = value
            else:
                hb[by - 1] = value.astype(BF16)
                sends.append(send(hb.at[by - 1], hr.at[by - 1], shifted(at, x=by)))
        return sends

    def z_reduce(bufs):
        h, hr, zs, zr = bufs[2], bufs[4], bufs[5], bufs[6]
        h[...] = h[...] + hr[0].astype(F32) + hr[1].astype(F32) + hr[2].astype(F32)
        sends = []
        for by in (3, 1, 2):
            zs[by - 1] = h[:, pl.ds(pl.multiple_of((at["zl"] + by) % 4 * 16, 16), 16)]
            sends.append(send(zs.at[by - 1], zr.at[by - 1], shifted(at, zl=by)))
        return sends

    def yz_gather(bufs, base):
        h, zr, sb = bufs[2], bufs[6], bufs[7]
        value = h[:, pl.ds(pl.multiple_of(at["zl"] * 16, 16), 16)] + zr[0] + zr[1] + zr[2]
        sb[...] = (value * (1.0 / math.sqrt(40960))).astype(BF16)
        piece = pl.multiple_of(at["k"] * 256 + at["x"] * 64 + at["zl"] * 16, 16)
        sends = []
        for n in range(2):
            slot = SLOTS[base + n]
            for dz in (3, 2, 1, 0):
                if slot == 0 and dz == 0:
                    ag[0, pl.ds(piece, 16)] = sb[0]
                else:
                    dst = ag.at[base + n, pl.ds(piece, 16)]
                    sends.append(send(sb.at[n], dst, shifted(at, y=-slot, zl=dz)))
        return sends

    def x_gather(base):
        start = pl.multiple_of(at["k"] * 256 + at["x"] * 64, 64)
        ref = ag.at[pl.ds(base, 2), pl.ds(start, 64)]
        return [send(ref, ref, shifted(at, x=by)) for by in (2, 1, 3)]

    def core_gather(base):
        ref = ag.at[pl.ds(base, 2), pl.ds(pl.multiple_of(at["k"] * 256, 256), 256)]
        return send(ref, ref, shifted(at, k=1))

    def unpack(place):
        value = ag[place].astype(F32)
        low, high = value[:328], value[328:USED]
        left = jnp.concatenate([low[:, :64], low[8:, 64:]], axis=0)
        right = jnp.concatenate(
            [high[:, :32], high[8:, 32:64], high[8:, 64:96], high[8:, 96:]], axis=0
        )
        piece = jnp.concatenate([left, right], axis=1).astype(BF16)
        return jnp.dot(piece, perm[SLOTS[place]], preferred_element_type=F32)

    weigh(SLOTS[0], chain_a[0], 0)
    weigh(SLOTS[1], chain_a[0], 1)
    a = core_reduce(chain_a)
    arrived(dy[2])
    build(2)
    dgrad(2)
    def grad_part(by):
        start = pl.multiple_of((at["zh"] + by) % 4 * CH, 8)
        return jnp.concatenate([p[0, pl.ds(start, CH)], p[1, pl.ds(start, CH)]], axis=0)

    along = {"tm": at["x"], "height": row, "chan": (at["zh"] + side) % 4 * 4 + at["y"]}
    qb[0] = grad_part(2).astype(BF16)
    z_far = send(qb.at[0], rz.at[0], along)
    qb[1] = grad_part(4 - side).astype(BF16)
    z_near = send(qb.at[1], rz.at[1], away)
    q[...] = grad_part(0)
    arrived([a])
    a = x_reduce(chain_a)
    for t in range(2):
        dsend[t : t + 1] = jnp.sum(p[t] * sx[t], axis=0, keepdims=True)
    dys = [send(dsend, dry.at[by - 1], shifted(at, y=by)) for by in (2, 1, 3)]
    weigh(SLOTS[2], chain_b[0], 0)
    weigh(SLOTS[3], chain_b[0], 1)
    b = core_reduce(chain_b)
    arrived(a)
    a = z_reduce(chain_a)
    arrived(dys)
    dmid[...] = dsend[...] + dry[0] + dry[1] + dry[2]
    dzs = [send(dmid, drz.at[by - 1], shifted(at, zh=by)) for by in (2, 1, 3)]
    arrived([b])
    b = x_reduce(chain_b)
    arrived([z_far])
    qb[2] = (grad_part(side) + rz[0].astype(F32)).astype(BF16)
    z_sum = send(qb.at[2], rz.at[2], along)
    arrived(a)
    a = yz_gather(chain_a, 0)
    arrived(b)
    b = z_reduce(chain_b)
    arrived(b)
    b = yz_gather(chain_b, 2)
    arrived(a)
    a = x_gather(0)
    arrived(b)
    b = x_gather(2)
    arrived(a)
    a = core_gather(0)

    arrived(b)
    b = core_gather(2)
    arrived([z_near, z_sum] + dzs)
    grad = q[...] + rz[1].astype(F32) + rz[2].astype(F32)
    dots = dmid[...] + drz[0] + drz[1] + drz[2]
    mine_x = f_ref[...].astype(F32)
    ct = d_ref[...].astype(F32)
    outs = []
    for t in range(2):
        rows = slice(CH * t, CH * t + CH)
        x = mine_x[rows]
        _, slope = activation(x, t, at["zh"] * 4 + at["y"])
        up = grad[rows] * slope
        r = inv[t : t + 1]
        back = r * up - x * (r * r * r * dots[t : t + 1] * (1.0 / TOTAL))
        outs.append(ct[rows] + back)
    od_ref[...] = jnp.concatenate(outs, axis=0).astype(BF16)

    arrived([a])
    wgrad[...] = unpack(0) + unpack(1)
    arrived([b])
    og_ref[...] = (wgrad[...] + unpack(2) + unpack(3)).astype(BF16)
    for copy in started:
        copy.wait_send()
    for copy, goes, _ in halo:
        pl.when(goes)(copy.wait_send)


def chain_buffers():
    return [
        pltpu.VMEM((2, ROWS, 128), F32),
        pltpu.VMEM((2, 256, 128), F32),
        pltpu.VMEM((2, 64, 128), F32),
        pltpu.VMEM((3, 2, 64, 128), BF16),
        pltpu.VMEM((3, 2, 64, 128), BF16),
        pltpu.VMEM((3, 2, 16, 128), F32),
        pltpu.VMEM((3, 2, 16, 128), F32),
        pltpu.VMEM((2, 16, 128), BF16),
    ]


def on_device(features, cotangent, conv_weight, norm_gain, norm_bias):
    chans, frames, rows, cols = features.shape
    fd = jnp.transpose(jnp.stack([features, cotangent]), (0, 2, 1, 3, 4))
    fd = fd.reshape(2 * frames * chans, rows * cols)
    vmem = pl.BlockSpec(memory_space=pltpu.VMEM)
    hbm = pl.BlockSpec(memory_space=pl.ANY)
    w = jnp.transpose(conv_weight, (1, 0, 2)).reshape(27 * chans, TOTAL)
    sums = pltpu.VMEM((2, LANES), F32)
    sums3 = pltpu.VMEM((3, 2, LANES), F32)
    cells = pltpu.VMEM((3, 48, LANES), BF16)
    grads, out = pl.pallas_call(
        kernel,
        name="unit_backward",
        out_shape=(
            jax.ShapeDtypeStruct((648, TOTAL), BF16),
            jax.ShapeDtypeStruct((48, LANES), BF16),
        ),
        in_specs=[vmem, hbm, hbm, hbm],
        out_specs=(vmem, vmem),
        scratch_shapes=[
            pltpu.VMEM((27 * CH, TOTAL), BF16),
            pltpu.VMEM((TOTAL,), F32),
            pltpu.VMEM((TOTAL,), F32),
            pltpu.VMEM((3, TOTAL, 9 * CH), F32),
            pltpu.VMEM((3, 288, 9 * CH), BF16),
            pltpu.VMEM((4, 288, 9 * CH), BF16),
            pltpu.VMEM((TOTAL, 8), F32),
            cells,
            pltpu.VMEM((4, 48, LANES), BF16),
            pltpu.VMEM((4, 4, 48, 256), BF16),
            pltpu.VMEM((4, 48, LANES), BF16),
            pltpu.VMEM((4, 4, 216, LANES), BF16),
            pltpu.VMEM((2, 96, LANES), F32),
            pltpu.VMEM((48, LANES), F32),
            cells,
            cells,
            pltpu.VMEM((2, 96, LANES), BF16),
            pltpu.VMEM((2, 96, LANES), F32),
            sums,
            sums,
            pltpu.VMEM((4, 2, LANES), F32),
            sums3,
            sums,
            sums,
            sums,
            sums3,
            sums3,
            pltpu.VMEM((648, 96), F32),
            pltpu.VMEM((4, 96, TOTAL), BF16),
            pltpu.VMEM((648, TOTAL), F32),
            pltpu.VMEM((4, ROWS, 128), BF16),
            chain_buffers(),
            chain_buffers(),
            pltpu.SemaphoreType.DMA((3,)),
            pltpu.SemaphoreType.DMA((COPIES,)),
            pltpu.SemaphoreType.DMA((COPIES,)),
        ],
        compiler_params=pltpu.CompilerParams(
            collective_id=0, has_side_effects=True, vmem_limit_bytes=40 << 20
        ),
    )(fd, w, norm_gain, norm_bias)
    result = jnp.transpose(out.reshape(frames, chans, rows, cols), (1, 0, 2, 3))
    weight_grad = jnp.transpose(grads.reshape(27, chans, TOTAL), (1, 0, 2)).astype(F32)
    return result, weight_grad


def solution(mesh):
    return jax.shard_map(
        on_device,
        mesh=mesh,
        in_specs=(
            P("chan", "tm", "height", None),
            P("chan", "tm", "height", None),
            P("chan", None, None),
            P(),
            P(),
        ),
        out_specs=(P("chan", "tm", "height", None), P("chan", None, None)),
        check_vma=False,
    )
```
